32 devices in a mesh: dp: 16 (over z, x, core), fsdp: 2 (over y).
Axes of the slice: x: 2, y: 2, z: 4, core: 2. Of those that a mesh axis runs over, the one named last changes fastest.
Arguments:
- tokens: bfloat16 [32, 768, 768], P(('dp', 'fsdp')), may hold values from -6 to 6
- cond: bfloat16 [32, 768, 384], P(('dp', 'fsdp')), may hold values from -6 to 6
- pair: bfloat16 [2, 768, 768, 128], P(None, ('dp', 'fsdp')), may hold values from -6 to 6
- counts: int32 [2], replicated, may hold values from 385 to 768, as said below
- owner: int32 [32], replicated, may hold values from 0 to 1
- out_grad: bfloat16 [32, 768, 768], P(('dp', 'fsdp')), may hold values from -6 to 6
- cond_gain: float32 [384], replicated, may hold values from 0.1 to 1.9
- cond_weight: bfloat16 [384, 4608], P('fsdp'), may hold values from -0.3125 to 0.3125
- cond_bias: float32 [4608], replicated, may hold values from -3 to 3
- qkvg_weight: bfloat16 [768, 3072], P('fsdp'), may hold values from -0.21875 to 0.21875
- query_bias: float32 [768], replicated, may hold values from -3 to 3
- out_weight: bfloat16 [768, 768], P('fsdp'), may hold values from -4 to 4
- pair_gain: float32 [128], replicated, may hold values from 0.1 to 1.9
- pair_weight: bfloat16 [128, 16], replicated, may hold values from -0.5 to 0.5
- up_weight: bfloat16 [768, 3072], P('fsdp'), may hold values from -0.21875 to 0.21875
- down_weight: bfloat16 [1536, 768], P('fsdp'), may hold values from -0.15625 to 0.15625
Outputs:
- block_out: float32 [32, 768, 768], P(('dp', 'fsdp'))
- tokens_grad: float32 [32, 768, 768], P(('dp', 'fsdp'))
- cond_grad: float32 [32, 768, 384], P(('dp', 'fsdp'))
- pair_grad: float32 [2, 768, 768, 128], P(None, ('dp', 'fsdp'))
- cond_gain_grad: float32 [384], replicated
- cond_weight_grad: float32 [384, 4608], P('fsdp')
- cond_bias_grad: float32 [4608], replicated
- qkvg_weight_grad: float32 [768, 3072], P('fsdp')
- query_bias_grad: float32 [768], replicated
- out_weight_grad: float32 [768, 768], P('fsdp')
- pair_gain_grad: float32 [128], replicated
- pair_weight_grad: float32 [128, 16], replicated
- up_weight_grad: float32 [768, 3072], P('fsdp')
- down_weight_grad: float32 [1536, 768], P('fsdp')
The draws below stay inside these ranges and needn't reach their ends.
Inputs may be any that keep to these rules, and one draw needn't show every extreme that they name: One of the two counts is exactly 768 in every draw, which one drawn from the seed; the other lies above 384.
All inputs are finite; a program needn't handle non-finite values.
Results may differ from the reference program's by a relative error of at most 0.017.
Values may be sent and summed in bfloat16 or wider, within the bound.
A program may use at most 320 MiB of HBM per device.

```python
import math
import jax
import jax.numpy as jnp
from jax import lax

D = 768
H = 16
HD = 48
FF = 1536
CS = 384
CZ = 128
L = 768
SAMPLES = 32


def draw_counts(key, part):
    key = jax.random.fold_in(key, 11)
    length_key, pick_key = jax.random.split(key)
    lengths = jax.random.randint(length_key, (2,), L // 2 + 1, L + 1)
    picked = jax.random.randint(pick_key, (), 0, 2)
    return jnp.where(jnp.arange(2) == picked, L, lengths).astype(jnp.int32)


def set_ends(values, own_key, low, top_value):
    longest = values.shape.index(max(values.shape))
    spots = []
    for shift in (0, 1):
        where = [jax.random.randint(jax.random.fold_in(own_key, axis), (), 0, length) for axis, length in enumerate(values.shape)]
        where[longest] = (where[longest] + shift) % values.shape[longest]
        spots.append(tuple(where))
    return values.at[spots[0]].set(low).at[spots[1]].set(top_value)


def level_of(stream_key, shape, cuts, low, top_value):
    def one(axis_at, blocks):
        draws = jax.random.uniform(jax.random.fold_in(jax.random.fold_in(stream_key, 6), axis_at), (blocks,), jnp.float32, low / len(cuts), top_value / len(cuts))
        return jnp.repeat(jnp.exp(draws), shape[axis_at] // blocks).reshape((-1,) + (1,) * (len(shape) - axis_at - 1))

    gain = one(*cuts[0])
    for cut in cuts[1:]:
        gain = gain * one(*cut)
    return gain


def gaussian(stream_key, dims, scale, limit, shards=(), kind=jnp.bfloat16):
    result = scale * jax.random.normal(stream_key, dims, jnp.float32)
    if shards:
        result = result * level_of(stream_key, dims, shards, -0.22, 0.18)
    return jnp.clip(result, -limit, limit).astype(kind)


def setup_inputs(seed: int = 0) -> dict:
    seeds = jax.random.split(jax.random.key(seed), 17)
    return {
        "tokens": gaussian(seeds[0], (SAMPLES, L, D), 1.0, 6.0, ((0, 32),)),
        "cond": gaussian(seeds[1], (SAMPLES, L, CS), 1.0, 6.0, ((0, 32),)),
        "pair": gaussian(seeds[2], (2, L, L, CZ), 1.0, 6.0, ((1, 32),)),
        "counts": draw_counts(jax.random.fold_in(seeds[16], 71), 0),
        "owner": set_ends(jax.random.randint(seeds[4], (SAMPLES,), 0, 2), jax.random.fold_in(seeds[4], 1), 0, 1).astype(jnp.int32),
        "out_grad": gaussian(seeds[5], (SAMPLES, L, D), 1.0, 6.0, ((0, 32),)),
        "cond_gain": jnp.clip(1.0 + 0.18 * jax.random.normal(seeds[6], (CS,), jnp.float32), 0.1, 1.9),
        "cond_weight": gaussian(seeds[7], (CS, 6 * D), CS ** -0.5, 0.3125, ((0, 2),)),
        "cond_bias": gaussian(seeds[8], (6 * D,), 0.5, 3.0, (), jnp.float32),
        "qkvg_weight": gaussian(seeds[9], (D, 4 * D), D ** -0.5, 0.21875, ((0, 2),)),
        "query_bias": gaussian(seeds[10], (D,), 0.5, 3.0, (), jnp.float32),
        "out_weight": gaussian(seeds[11], (D, D), 2 ** -0.5, 4.0, ((0, 2),)),
        "pair_gain": jnp.clip(1.0 + 0.18 * jax.random.normal(seeds[12], (CZ,), jnp.float32), 0.1, 1.9),
        "pair_weight": gaussian(seeds[13], (CZ, H), CZ ** -0.5, 0.5),
        "up_weight": gaussian(seeds[14], (D, 2 * FF), D ** -0.5, 0.21875, ((0, 2),)),
        "down_weight": gaussian(seeds[15], (FF, D), FF ** -0.5, 0.15625, ((0, 2),)),
    }


@jax.custom_vjp
def low(v):
    return lax.optimization_barrier(v.astype(jnp.bfloat16)).astype(jnp.float32)

@jax.custom_vjp
def low_back(v):
    return v

def low_keep(v):
    return (low(v), None)

def low_pass(kept, grad):
    return (grad,)

def back_keep(v):
    return (v, None)

def back_low(kept, grad):
    return (low(grad),)
low.defvjp(low_keep, low_pass)
low_back.defvjp(back_keep, back_low)
norm_eps = 1e-05
precise = lax.Precision.HIGHEST

def normalize(values):
    mean_value = lax.optimization_barrier(jnp.mean(values, axis=-1, keepdims=True))
    centered = values - mean_value
    variance = lax.optimization_barrier(jnp.mean(centered * centered, axis=-1, keepdims=True))
    return centered * lax.rsqrt(variance + norm_eps)

def sample_block(token_rows, cond_rows, mask_rows, bias_rows, weights):
    cond_gain, cond_weight, cond_bias, qkvg_weight, query_bias, out_weight, up_weight, down_weight = weights
    cond_norm = low(normalize(cond_rows) * cond_gain)
    modul = low_back(jnp.einsum('nlc,cm->nlm', cond_norm, cond_weight, precision=precise)) + cond_bias
    scale_one, shift_one, gate_one, scale_two, shift_two, gate_two = jnp.split(modul, 6, axis=-1)
    token_norm = normalize(token_rows)
    first = low(jax.nn.sigmoid(scale_one) * token_norm + shift_one)
    second = low(jax.nn.sigmoid(scale_two) * token_norm + shift_two)
    projected = low_back(jnp.einsum('nld,de->nle', first, qkvg_weight, precision=precise))
    part_q, part_k, part_v, part_g = jnp.split(projected, 4, axis=-1)
    head_shape = token_rows.shape[:2] + (H, HD)
    inverse_root = 1.0 / math.sqrt(HD)
    queries = low((part_q + query_bias) * inverse_root).reshape(head_shape)
    key_heads = low(part_k).reshape(head_shape)
    value_heads = low(part_v).reshape(head_shape)
    scores = jnp.einsum('nqhd,nkhd->nqhk', queries, key_heads, precision=precise)
    scores = low_back(scores + bias_rows + mask_rows[:, None, None, :])
    probs = low(jax.nn.softmax(scores, axis=-1))
    mixed = low_back(jnp.einsum('nqhk,nkhd->nqhd', probs, value_heads, precision=precise).reshape(token_rows.shape))
    gated = low(jax.nn.sigmoid(part_g) * mixed)
    attn_out = low_back(jnp.einsum('nld,de->nle', gated, out_weight, precision=precise))
    hidden = low_back(jnp.einsum('nld,df->nlf', second, up_weight, precision=precise))
    h_gate, h_up = jnp.split(hidden, 2, axis=-1)
    activated = low(jax.nn.silu(h_gate) * h_up)
    trans_out = low_back(jnp.einsum('nlf,fd->nld', activated, down_weight, precision=precise))
    return token_rows + jax.nn.sigmoid(gate_one) * attn_out + jax.nn.sigmoid(gate_two) * trans_out

def forward(tokens, cond, pair, cond_gain, cond_weight, cond_bias, qkvg_weight, query_bias, out_weight, pair_gain, pair_weight, up_weight, down_weight, mask_add, owner):
    pair_norm = low(normalize(pair) * pair_gain)
    bias_all = low(low_back(jnp.einsum('cikz,zh->cihk', pair_norm, pair_weight, precision=precise)))
    weights = (cond_gain, cond_weight, cond_bias, qkvg_weight, query_bias, out_weight, up_weight, down_weight)
    group_size = 4
    group_count = tokens.shape[0] // group_size

    def group_block(group_item):
        token_rows, cond_rows, mask_rows, owner_rows = group_item
        bias_rows = jnp.take(bias_all, owner_rows, axis=0)
        return sample_block(token_rows, cond_rows, mask_rows, bias_rows, weights)
    group_items = (tokens.reshape((group_count, group_size) + tokens.shape[1:]), cond.reshape((group_count, group_size) + cond.shape[1:]), mask_add.reshape((group_count, group_size) + mask_add.shape[1:]), owner.reshape(group_count, group_size))
    outputs = lax.map(jax.checkpoint(group_block), group_items)
    return outputs.reshape(tokens.shape)

def reference(tokens, cond, pair, counts, owner, out_grad, cond_gain, cond_weight, cond_bias, qkvg_weight, query_bias, out_weight, pair_gain, pair_weight, up_weight, down_weight):
    positions = jnp.arange(L, dtype=jnp.int32)
    limits = jnp.take(counts, owner, axis=0)
    mask_add = jnp.where(positions[None, :] < limits[:, None], 0.0, -1000000000.0).astype(jnp.float32)
    primals = (tokens.astype(jnp.float32), cond.astype(jnp.float32), pair.astype(jnp.float32), cond_gain.astype(jnp.float32), cond_weight.astype(jnp.float32), cond_bias.astype(jnp.float32), qkvg_weight.astype(jnp.float32), query_bias.astype(jnp.float32), out_weight.astype(jnp.float32), pair_gain.astype(jnp.float32), pair_weight.astype(jnp.float32), up_weight.astype(jnp.float32), down_weight.astype(jnp.float32))

    def wrapped(*inputs):
        return forward(*inputs, mask_add, owner)
    block_out, pullback = jax.vjp(wrapped, *primals)
    grads = pullback(out_grad.astype(jnp.float32))
    return (block_out, grads[0], grads[1], grads[2], grads[3], grads[4], grads[5], grads[6], grads[7], grads[8], grads[9], grads[10], grads[11], grads[12])
```

```python
import functools

import jax
import jax.numpy as jnp
from jax import lax
from jax.experimental import pallas as pl
from jax.experimental.pallas import tpu as pltpu
from jax.sharding import Mesh, PartitionSpec as P

f32, bf16 = jnp.float32, jnp.bfloat16
norm_eps = 1e-05
mask_fill = -1000000000.0
log2e = 1.4426950408889634
ln2 = 0.6931471805599453
head_count = 16
group_size = 8
vmem_bytes = 58 << 20
nt_dims = (((1,), (1,)), ((), ()))


def dot(a, b):
    return jnp.dot(a, b, preferred_element_type=f32)


def dot_nt(a, b):
    return lax.dot_general(a, b, nt_dims, preferred_element_type=f32)


def dot_tn(a, b):
    return lax.dot_general(a, b, (((0,), (0,)), ((), ())), preferred_element_type=f32)


def norm_parts(values):
    centered = values - jnp.mean(values, axis=-1, keepdims=True)
    variance = jnp.mean(centered * centered, axis=-1, keepdims=True)
    scale = lax.rsqrt(variance + norm_eps)
    return centered * scale, scale


def norm_back(x, u, scale):
    mean_u = jnp.mean(u, axis=-1, keepdims=True)
    mean_ux = jnp.mean(u * x, axis=-1, keepdims=True)
    return (u - mean_u - x * mean_ux) * scale


def params(**kw):
    return pltpu.CompilerParams(vmem_limit_bytes=vmem_bytes, **kw)


def whole(a):
    zero = (0,) * a.ndim
    return pl.BlockSpec(a.shape, lambda *_: zero)


def lane_means(values):
    width = values.shape[-1]
    return dot(values, jnp.full((width, width), 1.0 / width, bf16))


def pair_norm(x):
    values = x.astype(f32)
    centered = values - lane_means(x)
    variance = lane_means((centered * centered).astype(bf16))
    scale = lax.rsqrt(variance + norm_eps)
    return centered * scale, scale


def pair_fwd_kernel(rows, counts_ref, x_ref, pw_ref, gain_ref, out_ref, scr_ref):
    step = pl.program_id(0)
    steps_each = pl.num_programs(0) // 2
    limit = counts_ref[step // steps_each]
    heads, length = scr_ref.shape[0], scr_ref.shape[2]
    valid = lax.broadcasted_iota(jnp.int32, (heads, length), 1) < limit
    pw = pw_ref[...]
    gain = gain_ref[...]
    for r in range(rows):
        x_hat, _ = pair_norm(x_ref[0, r])
        low = (x_hat * gain).astype(bf16)
        bias = dot_nt(pw, low)
        scr_ref[:, r, :] = jnp.where(valid, bias * log2e, mask_fill)
    out_ref[:, 0] = scr_ref[...].astype(bf16)


def pair_fwd(counts, pair, pw_t, gain):
    _, total, length, width = pair.shape
    rows = 8 if total % 8 == 0 else total
    steps = total // rows
    heads = pw_t.shape[0]
    return pl.pallas_call(
        functools.partial(pair_fwd_kernel, rows),
        grid_spec=pltpu.PrefetchScalarGridSpec(
            num_scalar_prefetch=1,
            grid=(2 * steps,),
            in_specs=[
                pl.BlockSpec((1, rows, length, width), lambda i, _: (i // steps, i % steps, 0, 0)),
                whole(pw_t),
                whole(gain),
            ],
            out_specs=pl.BlockSpec((heads, 1, rows, length), lambda i, _: (0, i // steps, i % steps, 0)),
            scratch_shapes=[pltpu.VMEM((heads, rows, length), f32)],
        ),
        out_shape=jax.ShapeDtypeStruct((heads, 2, total, length), bf16),
        compiler_params=params(),
        cost_estimate=pl.CostEstimate(flops=2 * pair.size * 300, bytes_accessed=pair.size * 2, transcendentals=pair.size),
        name="pair_fwd",
    )(counts, pair, pw_t, gain)


def pair_bwd_kernel(rows, x_ref, bg_ref, a_ref, out_ref, q_ref, scr_ref):
    @pl.when(pl.program_id(0) == 0)
    def _():
        q_ref[...] = jnp.zeros_like(q_ref)

    scr_ref[...] = bg_ref[:, 0].astype(f32)
    weights = a_ref[...]
    total = q_ref[...]
    width = out_ref.shape[-1]
    for r in range(rows):
        x_hat, scale = pair_norm(x_ref[0, r])
        grads = scr_ref[:, r, :].astype(bf16)
        total += dot(grads, x_hat.astype(bf16))
        u = dot_tn(jnp.concatenate([grads, grads], axis=0), weights)
        mean_ux = lane_means((u * x_hat).astype(bf16))
        out_ref[0, r] = (u - x_hat * mean_ux) * scale
    q_ref[...] = total


def pair_bwd(pair, bias_grad, centered_weights):
    _, total, length, width = pair.shape
    rows = 8 if total % 8 == 0 else total
    steps = total // rows
    heads = bias_grad.shape[0]
    return pl.pallas_call(
        functools.partial(pair_bwd_kernel, rows),
        grid=(2 * steps,),
        in_specs=[
            pl.BlockSpec((1, rows, length, width), lambda i: (i // steps, i % steps, 0, 0)),
            pl.BlockSpec((heads, 1, rows, length), lambda i: (0, i // steps, i % steps, 0)),
            whole(centered_weights),
        ],
        out_specs=[
            pl.BlockSpec((1, rows, length, width), lambda i: (i // steps, i % steps, 0, 0)),
            pl.BlockSpec((heads, width), lambda i: (0, 0)),
        ],
        out_shape=[
            jax.ShapeDtypeStruct(pair.shape, f32),
            jax.ShapeDtypeStruct((heads, width), f32),
        ],
        scratch_shapes=[pltpu.VMEM((heads, rows, length), f32)],
        compiler_params=params(),
        cost_estimate=pl.CostEstimate(flops=2 * pair.size * 500, bytes_accessed=pair.size * 6, transcendentals=pair.size),
        name="pair_bwd",
    )(pair, bias_grad, centered_weights)


def attn_kernel(rb, owner_ref, x_ref, bias_ref, y_ref, bg_ref, acc_ref):
    n = pl.program_id(0)
    c = owner_ref[n]
    length, hd = x_ref.shape[-1], x_ref.shape[-2]
    up, bz = bias_ref.shape[0], bias_ref.shape[2]

    @pl.when(n == 0)
    def _():
        acc_ref[...] = jnp.zeros_like(acc_ref)

    k_t, v_t = x_ref[0, 1], x_ref[0, 2]
    v_ext = jnp.concatenate([v_t, jnp.ones((16, length), bf16)], axis=0)
    dv = dk = 0.0
    for r in range(length // rb):
        sl = slice(r * rb, (r + 1) * rb)
        q_t = x_ref[0, 0, :, sl]
        q = q_t.T
        dm = x_ref[0, 3, :, sl].astype(f32).T
        z0 = r * rb // bz
        bias = jnp.concatenate([bias_ref[z0 + t, c].astype(f32) for t in range(rb // bz)], axis=0)
        s = dot(q, k_t) + bias
        e = jnp.exp2(s - jnp.max(s, axis=-1, keepdims=True))
        eb = e.astype(bf16)
        mx = dot_nt(eb, v_ext)
        inv = 1.0 / mx[:, hd : hd + 1]
        mixed = mx[:, :hd] * inv
        d = jnp.sum(mixed * dm, axis=-1, keepdims=True) * inv
        dms = (dm * inv).astype(bf16)
        ds = e * (dot(dms, v_t) - d)
        dsb = ds.astype(bf16)
        acc_ref[c, sl, :] += ds
        dq = dot_nt(dsb, k_t)
        dv = dv + dot(dms.T, eb)
        dk = dk + dot(q_t, dsb)
        y_ref[0, 0, :, sl] = mixed.T.astype(bf16)
        y_ref[0, 1, :, sl] = (dq * hd**-0.5).T.astype(bf16)
    y_ref[0, 2] = (dk * ln2).astype(bf16)
    y_ref[0, 3] = dv.astype(bf16)

    @pl.when(n == pl.num_programs(0) - 1)
    def _():
        for z in range(up):
            for cc in range(2):
                bg_ref[z, cc] = acc_ref[cc, z * bz : (z + 1) * bz, :].astype(bf16)


def attention(owner, x, bias):
    n, four, hd, length = x.shape
    return pl.pallas_call(
        functools.partial(attn_kernel, length // 2),
        grid_spec=pltpu.PrefetchScalarGridSpec(
            num_scalar_prefetch=1,
            grid=(n,),
            in_specs=[
                pl.BlockSpec((1, four, hd, length), lambda i, _: (i, 0, 0, 0)),
                pl.BlockSpec(bias.shape, lambda i, _: (0, 0, 0, 0)),
            ],
            out_specs=[
                pl.BlockSpec((1, four, hd, length), lambda i, _: (i, 0, 0, 0)),
                pl.BlockSpec(bias.shape, lambda i, _: (0, 0, 0, 0)),
            ],
            scratch_shapes=[pltpu.VMEM((2, length, length), f32)],
        ),
        out_shape=[jax.ShapeDtypeStruct(x.shape, bf16), jax.ShapeDtypeStruct(bias.shape, bf16)],
        compiler_params=params(),
        cost_estimate=pl.CostEstimate(
            flops=12 * n * length * length * 256, bytes_accessed=x.size * 4 + bias.size * 4, transcendentals=n * length * length
        ),
        name="attention",
    )(owner, x, bias)


def pick(flag, a, b):
    return jnp.where(flag == 0, a, b)


def split_dot(flag, x, own, other):
    half = own.shape[0]
    first, second = x[:, :half], x[:, half:]
    return dot(pick(flag, first, second), own[...]) + dot(pick(flag, second, first), other[...])


def split_dot_nt(flag, x, own, other):
    a, b = dot_nt(x, own[...]), dot_nt(x, other[...])
    return jnp.concatenate([pick(flag, a, b), pick(flag, b, a)], axis=-1)


def front_kernel(
    flag_ref, tok, cond, og, cgain, wc0, wc1, cb, wq0, wq1, qb, wo0, wo1,
    *outs,
):
    *xs, sg_o, gg_o, s1_o, g1_o, first_o = outs
    flag = flag_ref[0]
    width = tok.shape[-1]
    hd = width // head_count
    slots = len(xs)
    peers = head_count // slots
    cond_low = (norm_parts(cond[...].astype(f32))[0] * cgain[...]).astype(bf16)
    modul = split_dot(flag, cond_low, wc0, wc1) + cb[...]
    s1 = jax.nn.sigmoid(modul[:, :width])
    g1 = jax.nn.sigmoid(modul[:, 2 * width :])
    tn, _ = norm_parts(tok[...].astype(f32))
    first = (s1 * tn + modul[:, width : 2 * width]).astype(bf16)
    proj = split_dot(flag, first, wq0, wq1)
    q = (proj[:, :width] + qb[...]) * (hd**-0.5 * log2e)
    sg = jax.nn.sigmoid(proj[:, 3 * width :])
    ga = (og[...].astype(f32) * g1).astype(bf16)
    gg = split_dot_nt(flag, ga, wo0, wo1)
    dm = sg * gg
    sg_o[...] = sg.astype(bf16)
    gg_o[...] = gg.astype(bf16)
    s1_o[...] = s1.astype(bf16)
    g1_o[...] = g1.astype(bf16)
    first_o[...] = first
    for i, part in enumerate((q, proj[:, width : 2 * width], proj[:, 2 * width : 3 * width], dm)):
        turned = part.T.astype(bf16).reshape(peers, slots, hd, part.shape[0])
        for t in range(slots):
            xs[t][:, i] = turned[:, t]


def row_spec(a, rb):
    return pl.BlockSpec((rb, a.shape[1]), lambda i, *_: (i, 0))


def front(flag, tok, cond, og, cgain, wc, cb, wq, qb, wo, slots):
    length, width = tok.shape
    rb = 256
    peers, hd = head_count // slots, width // head_count
    small = jax.ShapeDtypeStruct((length, width), bf16)
    payload = jax.ShapeDtypeStruct((peers, 4, hd, length), bf16)
    return pl.pallas_call(
        front_kernel,
        grid_spec=pltpu.PrefetchScalarGridSpec(
            num_scalar_prefetch=1,
            grid=(length // rb,),
            in_specs=[row_spec(tok, rb), row_spec(cond, rb), row_spec(og, rb)]
            + [whole(a) for a in (cgain, *wc, cb, *wq, qb, *wo)],
            out_specs=[pl.BlockSpec((peers, 4, hd, rb), lambda i, _: (0, 0, 0, i))] * slots + [row_spec(tok, rb)] * 5,
        ),
        out_shape=[payload] * slots + [small] * 5,
        compiler_params=params(),
        cost_estimate=pl.CostEstimate(flops=2 * length * width * width * 7, bytes_accessed=20 << 20, transcendentals=length * width * 4),
        name="front",
    )(flag, tok, cond, og, cgain, *wc, cb, *wq, qb, *wo)


def trans_kernel(
    flag_ref, tok, cond, og, cgain, wc0, wc1, cb, wu0, wu1, wd0, wd1,
    part_o, u2_o, dcond_o, ml_o, cn_o, second_o, hid_o, act_o, gt_o, cbg_o,
):
    flag = flag_ref[0]
    width = tok.shape[-1]
    cond_low = (norm_parts(cond[...].astype(f32))[0] * cgain[...]).astype(bf16)
    cn_o[...] = cond_low
    modul = split_dot(flag, cond_low, wc0, wc1) + cb[...]
    s2 = jax.nn.sigmoid(modul[:, :width])
    g2 = jax.nn.sigmoid(modul[:, 2 * width :])
    tokens = tok[...].astype(f32)
    tn, _ = norm_parts(tokens)
    second = (s2 * tn + modul[:, width : 2 * width]).astype(bf16)
    second_o[...] = second
    hidden = split_dot(flag, second, wu0, wu1)
    ff = hidden.shape[1] // 2
    h_gate, h_up = hidden[:, :ff], hidden[:, ff:]
    sig = jax.nn.sigmoid(h_gate)
    silu = h_gate * sig
    act = (silu * h_up).astype(bf16)
    act_o[...] = act
    trans_out = split_dot(flag, act, wd0, wd1)
    part_o[...] = tokens + g2 * trans_out
    g = og[...].astype(f32)
    gt = (g * g2).astype(bf16)
    gt_o[...] = gt
    grad_act = split_dot_nt(flag, gt, wd0, wd1)
    hid = jnp.concatenate(
        [(grad_act * h_up * (sig * (1.0 + h_gate * (1.0 - sig)))).astype(bf16), (grad_act * silu).astype(bf16)], axis=-1
    )
    hid_o[...] = hid
    grad_second = split_dot_nt(flag, hid, wu0, wu1)
    u2_o[...] = (grad_second * s2).astype(bf16)
    grads = jnp.concatenate(
        [grad_second * tn * (s2 * (1.0 - s2)), grad_second, g * trans_out * (g2 * (1.0 - g2))], axis=-1
    )
    low = grads.astype(bf16)
    ml_o[...] = low

    @pl.when(pl.program_id(0) == 0)
    def _():
        cbg_o[...] = jnp.zeros_like(cbg_o)

    cbg_o[...] += jnp.sum(grads, axis=0, keepdims=True)
    dcond_o[...] = split_dot_nt(flag, low, wc0, wc1)


def transition(flag, tok, cond, og, cgain, wc, cb, wu, wd):
    length, width = tok.shape
    rb = 256
    cs, mw = cond.shape[1], cb.shape[1]
    ff2 = wu[0].shape[1]

    def out(w, dtype):
        return jax.ShapeDtypeStruct((length, w), dtype)

    shapes = [
        out(width, f32), out(width, bf16), out(cs, f32), out(mw, bf16), out(cs, bf16), out(width, bf16),
        out(ff2, bf16), out(ff2 // 2, bf16), out(width, bf16),
    ]
    return pl.pallas_call(
        trans_kernel,
        grid_spec=pltpu.PrefetchScalarGridSpec(
            num_scalar_prefetch=1,
            grid=(length // rb,),
            in_specs=[row_spec(tok, rb), row_spec(cond, rb), row_spec(og, rb)]
            + [whole(a) for a in (cgain, *wc, cb, *wu, *wd)],
            out_specs=[row_spec(s, rb) for s in shapes] + [pl.BlockSpec((1, mw), lambda i, _: (0, 0))],
        ),
        out_shape=shapes + [jax.ShapeDtypeStruct((1, mw), f32)],
        compiler_params=params(),
        cost_estimate=pl.CostEstimate(flops=2 * length * width * width * 15, bytes_accessed=40 << 20, transcendentals=length * width * 6),
        name="transition",
    )(flag, tok, cond, og, cgain, *wc, cb, *wu, *wd)


def back_kernel(slots, flag_ref, *refs):
    ys = refs[:slots]
    (
        sg, gg, s1, g1, part, u2, dcond2, tok, cond, og, cgain, wc0, wc1, wq0, wq1, wo0, wo1,
        out_o, tg_o, cg_o, gated_o, ga_o, gp_o, ml_o, qbg_o, cbg_o, cgg_o,
    ) = refs[slots:]
    flag = flag_ref[0]
    rb, width = tok.shape
    hd = width // head_count
    peers = head_count // slots

    def heads(i):
        stacked = jnp.stack([y[:, i] for y in ys], axis=1)
        return stacked.reshape(width, rb).astype(f32).T

    mixed = heads(0)
    sgv = sg[...].astype(f32)
    g1v = g1[...].astype(f32)
    gated = (sgv * mixed).astype(bf16)
    gated_o[...] = gated
    attn_out = split_dot(flag, gated, wo0, wo1)
    out_o[...] = part[...] + g1v * attn_out
    g = og[...].astype(f32)
    ga_o[...] = (g * g1v).astype(bf16)
    dg = gg[...].astype(f32) * mixed * (sgv * (1.0 - sgv))
    dq = heads(1)
    grad_proj = jnp.concatenate([dq.astype(bf16), heads(2).astype(bf16), heads(3).astype(bf16), dg.astype(bf16)], axis=-1)
    gp_o[...] = grad_proj
    grad_first = split_dot_nt(flag, grad_proj, wq0, wq1)
    s1v = s1[...].astype(f32)
    tn, tscale = norm_parts(tok[...].astype(f32))
    grads = jnp.concatenate(
        [grad_first * tn * (s1v * (1.0 - s1v)), grad_first, g * attn_out * (g1v * (1.0 - g1v))], axis=-1
    )
    low = grads.astype(bf16)
    ml_o[...] = low
    tg_o[...] = g + norm_back(tn, grad_first * s1v + u2[...].astype(f32), tscale)
    dcond = split_dot_nt(flag, low, wc0, wc1) + dcond2[...]
    cx, cscale = norm_parts(cond[...].astype(f32))
    cg_o[...] = norm_back(cx, dcond * cgain[...], cscale)

    @pl.when(pl.program_id(0) == 0)
    def _():
        qbg_o[...] = jnp.zeros_like(qbg_o)
        cbg_o[...] = jnp.zeros_like(cbg_o)
        cgg_o[...] = jnp.zeros_like(cgg_o)

    qbg_o[...] += jnp.sum(dq, axis=0, keepdims=True)
    cbg_o[...] += jnp.sum(grads, axis=0, keepdims=True)
    cgg_o[...] += jnp.sum(dcond * cx, axis=0, keepdims=True)


def back(flag, ys, sg, gg, s1, g1, part, u2, dcond2, tok, cond, og, cgain, wc, wq, wo):
    length, width = tok.shape
    rb = 256
    cs, mw = cond.shape[1], wc[0].shape[1]
    rows = (sg, gg, s1, g1, part, u2, dcond2, tok, cond, og)
    consts = (cgain, *wc, *wq, *wo)

    def out(w, dtype):
        return jax.ShapeDtypeStruct((length, w), dtype)

    shapes = [
        out(width, f32), out(width, f32), out(cs, f32), out(width, bf16), out(width, bf16), out(wq[0].shape[1], bf16), out(mw, bf16),
    ]
    small = [jax.ShapeDtypeStruct((1, w), f32) for w in (width, mw, cs)]
    return pl.pallas_call(
        functools.partial(back_kernel, len(ys)),
        grid_spec=pltpu.PrefetchScalarGridSpec(
            num_scalar_prefetch=1,
            grid=(length // rb,),
            in_specs=[pl.BlockSpec(y.shape[:3] + (rb,), lambda i, _: (0, 0, 0, i)) for y in ys]
            + [row_spec(a, rb) for a in rows]
            + [whole(a) for a in consts],
            out_specs=[row_spec(s, rb) for s in shapes] + [pl.BlockSpec(s.shape, lambda i, _: (0, 0)) for s in small],
        ),
        out_shape=shapes + small,
        compiler_params=params(),
        cost_estimate=pl.CostEstimate(flops=2 * length * width * width * 7, bytes_accessed=40 << 20, transcendentals=length * width),
        name="back",
    )(flag, *ys, *rows, *consts)


def on_device(
    tokens, cond, pair, counts, owner, out_grad, cond_gain, cond_weight, cond_bias, qkvg_weight, query_bias,
    out_weight, pair_gain, pair_weight, up_weight, down_weight,
):
    ups, los, ffs = lax.axis_size("up"), lax.axis_size("lo"), lax.axis_size("fsdp")
    plane = ("lo", "fsdp")
    members = los * ffs
    slots = head_count // members
    length, width = tokens.shape[1:]
    rows = pair.shape[1]
    fs = lax.axis_index("fsdp")

    def halves(w):
        if ffs == 2:
            quarter = w.shape[0] // los
            piece = lax.dynamic_slice_in_dim(w, lax.axis_index("lo") * quarter, quarter)
            got = lax.ppermute(piece, "fsdp", [(0, 1), (1, 0)])
            return w, lax.all_gather(got, "lo", tiled=True)
        full = lax.all_gather(w, "fsdp", axis=0, tiled=True)
        half = full.shape[0] // 2
        return full[:half], full[half:]

    flag = (fs if ffs == 2 else jnp.zeros((), jnp.int32)).astype(jnp.int32).reshape(1)
    wide = 3 * width

    bias = pair_fwd(counts, pair, pair_weight.T, pair_gain[None])
    bias = bias.reshape(members, slots, 2, rows, length)

    def spread(part):
        got = lax.all_to_all(part, plane, 0, 0, tiled=True)
        mine = got.transpose(1, 0, 2, 3).reshape(2, members * rows, length)
        return lax.all_gather(mine, "up", axis=0, tiled=False)

    def summed_up(blocks):
        size, bit = ups, 1
        me = lax.axis_index("up")
        while bit < size:
            pairs = blocks.reshape((blocks.shape[0] // 2, 2) + blocks.shape[1:])
            mine = lax.rem(me // bit, 2)
            sent = lax.dynamic_index_in_dim(pairs, 1 - mine, 1, keepdims=False)
            kept = lax.dynamic_index_in_dim(pairs, mine, 1, keepdims=False)
            got = lax.ppermute(sent, "up", [(i, i ^ bit) for i in range(size)])
            blocks = (kept.astype(f32) + got.astype(f32)).astype(bf16)
            bit *= 2
        return blocks[0]

    wc1 = halves(cond_weight[:, :wide])
    wq = halves(qkvg_weight)
    wo = halves(out_weight)
    biases = [spread(bias[:, t]) for t in range(slots)]
    wc2 = halves(cond_weight[:, wide:])
    wu = halves(up_weight)
    wd = halves(down_weight)

    tok, cnd, og = tokens[0], cond[0], out_grad[0]
    cgain = cond_gain[None]
    *xs, sg, gg, s1, g1, first = front(
        flag, tok, cnd, og, cgain, wc1, cond_bias[None, :wide], wq, query_bias[None], wo, slots
    )
    xs = [lax.all_to_all(x, plane, 0, 0, tiled=True) for x in xs]
    part, u2, dcond2, ml2, cn, second, hid, act, gt, cbg2 = transition(
        flag, tok, cnd, og, cgain, wc2, cond_bias[None, wide:], wu, wd
    )

    def fold(g):
        k, n = g.shape
        if k == width:
            return g
        if k > width:
            times = k // width
            parts = g.reshape(ffs, times, width // ffs, n)
            return jnp.concatenate([parts[:, t] for t in range(times)], axis=-1).reshape(width, n * times)
        times = width // k
        parts = g.reshape(ffs, k // ffs, times, n // times)
        return jnp.concatenate([parts[:, :, t] for t in range(times)], axis=1).reshape(width, n // times)

    def unfold(h, k, n):
        rows_each = width // ffs
        if k == width:
            return h
        if k > width:
            times = k // width
            return jnp.concatenate([h[:, t * n : (t + 1) * n] for t in range(times)], axis=0)
        times = width // k
        step = rows_each // times
        return jnp.concatenate([h[t * step : (t + 1) * step] for t in range(times)], axis=1)

    def reduced(grads):
        folded = [fold(g) for g in grads]
        mine = lax.psum_scatter(
            jnp.concatenate(folded, axis=1), ("fsdp", "up", "lo"), scatter_dimension=0, tiled=True
        )
        full = lax.all_gather(mine, ("up", "lo"), axis=0, tiled=True)
        outs, at = [], 0
        for g, h in zip(grads, folded):
            outs.append(unfold(full[:, at : at + h.shape[1]], *g.shape).astype(f32))
            at += h.shape[1]
        return outs

    up_total, down_total, cond_total2 = reduced(
        [dot_tn(second, hid).astype(bf16), dot_tn(act, gt).astype(bf16), dot_tn(cn, ml2).astype(bf16)]
    )

    owners = lax.dynamic_slice_in_dim(owner, lax.axis_index("up") * members, members)
    ys, bias_grads = [], []
    for t in range(slots):
        y, bg = attention(owners, xs[t], biases[t])
        ys.append(lax.all_to_all(y, plane, 0, 0, tiled=True))
        mine = summed_up(bg)
        mine = mine.reshape(2, members, rows, length).transpose(1, 0, 2, 3)
        bias_grads.append(lax.all_to_all(mine, plane, 0, 0, tiled=True))

    block_out, tokens_grad, cond_grad, gated, ga, gp, ml1, qbg, cbg1, cgg = back(
        flag, ys, sg, gg, s1, g1, part, u2, dcond2, tok, cnd, og, cgain, wc1, wq, wo
    )
    qkvg_total, out_total, cond_total1 = reduced(
        [dot_tn(first, gp).astype(bf16), dot_tn(gated, ga).astype(bf16), dot_tn(cn, ml1).astype(bf16)]
    )

    bias_grad = jnp.stack(bias_grads, axis=1).reshape(head_count, 2, rows, length)
    pw = pair_weight.astype(f32).T
    scaled = pw * pair_gain
    centered = scaled - jnp.mean(scaled, axis=-1, keepdims=True)
    high = centered.astype(bf16)
    low = (centered - high.astype(f32)).astype(bf16)
    pair_grad, moments = pair_bwd(pair, bias_grad, jnp.concatenate([high, low], axis=0))
    pieces = [cgg, cbg1, cbg2, qbg, moments.reshape(1, -1)]
    small = lax.psum(jnp.concatenate([p.reshape(-1, 128) for p in pieces], axis=0), ("up", "lo", "fsdp")).reshape(-1)
    ends = [0]
    for p in pieces:
        ends.append(ends[-1] + p.size)
    small = [small[a:b] for a, b in zip(ends[:-1], ends[1:])]
    moments = small[4].reshape(moments.shape)
    return (
        block_out[None],
        tokens_grad[None],
        cond_grad[None],
        pair_grad,
        small[0],
        jnp.concatenate([cond_total1, cond_total2], axis=1),
        jnp.concatenate([small[1], small[2]]),
        qkvg_total,
        small[3],
        out_total,
        jnp.sum(pw * moments, axis=0),
        (moments * pair_gain).T,
        up_total,
        down_total,
    )


def solution(mesh):
    dp, fsdp = mesh.shape["dp"], mesh.shape["fsdp"]
    lo = max(1, group_size // fsdp)
    fine = Mesh(mesh.devices.reshape(dp // lo, lo, fsdp), ("up", "lo", "fsdp"))
    every = ("up", "lo", "fsdp")
    in_specs = (
        P(every, None, None),
        P(every, None, None),
        P(None, every, None, None),
        P(),
        P(),
        P(every, None, None),
        P(),
        P("fsdp", None),
        P(),
        P("fsdp", None),
        P(),
        P("fsdp", None),
        P(),
        P(),
        P("fsdp", None),
        P("fsdp", None),
    )
    out_specs = (
        P(every, None, None),
        P(every, None, None),
        P(every, None, None),
        P(None, every, None, None),
        P(),
        P("fsdp", None),
        P(),
        P("fsdp", None),
        P(),
        P("fsdp", None),
        P(),
        P(),
        P("fsdp", None),
        P("fsdp", None),
    )
    return jax.shard_map(on_device, mesh=fine, in_specs=in_specs, out_specs=out_specs, check_vma=False)
```

```python
import functools

import jax
import jax.numpy as jnp
from jax import lax
from jax.experimental import pallas as pl
from jax.experimental.pallas import tpu as pltpu
from jax.sharding import Mesh, PartitionSpec as P

f32, bf16 = jnp.float32, jnp.bfloat16
norm_eps = 1e-05
mask_fill = -1000000000.0
log2e = 1.4426950408889634
ln2 = 0.6931471805599453
head_count = 16
group_size = 8
vmem_bytes = 58 << 20
nt_dims = (((1,), (1,)), ((), ()))


def dot(a, b):
    return jnp.dot(a, b, preferred_element_type=f32)


def dot_nt(a, b):
    return lax.dot_general(a, b, nt_dims, preferred_element_type=f32)


def dot_tn(a, b):
    return lax.dot_general(a, b, (((0,), (0,)), ((), ())), preferred_element_type=f32)


def norm_parts(values):
    centered = values - jnp.mean(values, axis=-1, keepdims=True)
    variance = jnp.mean(centered * centered, axis=-1, keepdims=True)
    scale = lax.rsqrt(variance + norm_eps)
    return centered * scale, scale


def norm_back(x, u, scale):
    mean_u = jnp.mean(u, axis=-1, keepdims=True)
    mean_ux = jnp.mean(u * x, axis=-1, keepdims=True)
    return (u - mean_u - x * mean_ux) * scale


def params(**kw):
    return pltpu.CompilerParams(vmem_limit_bytes=vmem_bytes, **kw)


def whole(a):
    zero = (0,) * a.ndim
    return pl.BlockSpec(a.shape, lambda *_: zero)


MESH = pl.DeviceIdType.MESH
BITS = {"c": ("lo", 1), "x": ("lo", 2), "y": ("fsdp", 1), "z0": ("up", 1), "z1": ("up", 2)}
PEERS = (("c",), ("x",), ("y",), ("c", "x"), ("c", "y"), ("x", "y"), ("c", "x", "y"))
ORDERS = (("c", "x", "y", "z0", "z1"), ("c", "y", "z0", "z1", "x"))


def coords():
    return {a: lax.axis_index(a) for a in ("up", "lo", "fsdp")}


def bit_of(where, name):
    axis, value = BITS[name]
    return lax.rem(where[axis] // value, 2)


def across(where, *names):
    other = dict(where)
    for name in names:
        axis, value = BITS[name]
        other[axis] = other[axis] + value * (1 - 2 * bit_of(where, name))
    return other


def device(where):
    return (where["up"], where["lo"], where["fsdp"])


def place(where):
    return where["lo"] * 2 + where["fsdp"]


def greet(devices):
    barrier = pltpu.get_barrier_semaphore()
    for other in devices:
        pl.semaphore_signal(barrier, inc=1, device_id=device(other), device_id_type=MESH)
    pl.semaphore_wait(barrier, len(devices))


def remote(src, dst, send_sem, recv_sem, other):
    copy = pltpu.make_async_remote_copy(
        src_ref=src, dst_ref=dst, send_sem=send_sem, recv_sem=recv_sem, device_id=device(other), device_id_type=MESH
    )
    copy.start()
    return copy


def lane_means(values):
    total = values.shape[-1]
    group = lax.broadcasted_iota(jnp.int32, (total, total), 0) // 128 == lax.broadcasted_iota(jnp.int32, (total, total), 1) // 128
    return dot(values, jnp.where(group, 1.0 / 128, 0.0).astype(bf16))


def pair_norm(*blocks):
    x = jnp.concatenate(blocks, axis=-1)
    centered = x.astype(f32) - lane_means(x)
    variance = lane_means((centered * centered).astype(bf16))
    scale = lax.rsqrt(variance + norm_eps)
    return centered * scale, scale


def pair_fwd_kernel(rows, counts_ref, x_ref, pw_ref, gain_ref, out_ref, scr_ref):
    step = pl.program_id(0)
    steps_each = pl.num_programs(0) // 2
    limit = counts_ref[step // steps_each]
    heads, length = scr_ref.shape[0], scr_ref.shape[2]
    valid = lax.broadcasted_iota(jnp.int32, (heads, length), 1) < limit
    pw = pw_ref[...]
    gain = gain_ref[...]
    for r in range(rows):
        low = (pair_norm(x_ref[0, r])[0] * gain).astype(bf16)
        bias = dot_nt(pw, low)
        scr_ref[:, r, :] = jnp.where(valid, bias * log2e, mask_fill)
    out_ref[:, 0] = scr_ref[...].astype(bf16)


def pair_fwd(counts, pair, pw_t, gain):
    _, total, length, width = pair.shape
    rows = 8 if total % 8 == 0 else total
    steps = total // rows
    heads = pw_t.shape[0]
    return pl.pallas_call(
        functools.partial(pair_fwd_kernel, rows),
        grid_spec=pltpu.PrefetchScalarGridSpec(
            num_scalar_prefetch=1,
            grid=(2 * steps,),
            in_specs=[
                pl.BlockSpec((1, rows, length, width), lambda i, _: (i // steps, i % steps, 0, 0)),
                whole(pw_t),
                whole(gain),
            ],
            out_specs=pl.BlockSpec((heads, 1, rows, length), lambda i, _: (0, i // steps, i % steps, 0)),
            scratch_shapes=[pltpu.VMEM((heads, rows, length), f32)],
        ),
        out_shape=jax.ShapeDtypeStruct((heads, 2, total, length), bf16),
        compiler_params=params(),
        cost_estimate=pl.CostEstimate(flops=2 * pair.size * 300, bytes_accessed=pair.size * 2, transcendentals=pair.size),
        name="pair_fwd",
    )(counts, pair, pw_t, gain)


def pair_bwd_kernel(rows, x_ref, bg_ref, a_ref, out_ref, q_ref, low_buf):
    @pl.when(pl.program_id(0) == 0)
    def _():
        q_ref[...] = jnp.zeros_like(q_ref)

    width = out_ref.shape[-1]
    heads, _, _, length = bg_ref.shape
    grads = bg_ref[:, 0].astype(f32).reshape(heads * rows, length)
    turned = grads.T.astype(bf16)
    u_all = dot(jnp.concatenate([turned, turned], axis=1), a_ref[...])
    step = 2 - rows % 2
    for r in range(0, rows, step):
        x_hat, scale = pair_norm(*(x_ref[0, r + t] for t in range(step)))
        low_buf[:, r * width : (r + step) * width] = x_hat.astype(bf16)
        u = u_all[:, r * width : (r + step) * width]
        grad = (u - x_hat * lane_means((u * x_hat).astype(bf16))) * scale
        for t in range(step):
            out_ref[0, r + t] = grad[:, t * width : (t + 1) * width]
    q_ref[...] += dot(grads.astype(bf16), low_buf[...])


def pair_bwd(pair, bias_grad, high, low):
    _, total, length, width = pair.shape
    rows = 8 if total % 8 == 0 else total
    steps = total // rows
    heads = bias_grad.shape[0]
    eye = jnp.eye(rows, dtype=bf16)
    both = jnp.stack([high, low])
    weights = (both[:, :, None, None, :] * eye[None, None, :, :, None]).reshape(2 * heads * rows, rows * width)
    grad, moments = pl.pallas_call(
        functools.partial(pair_bwd_kernel, rows),
        grid=(2 * steps,),
        in_specs=[
            pl.BlockSpec((1, rows, length, width), lambda i: (i // steps, i % steps, 0, 0)),
            pl.BlockSpec((heads, 1, rows, length), lambda i: (0, i // steps, i % steps, 0)),
            whole(weights),
        ],
        out_specs=[
            pl.BlockSpec((1, rows, length, width), lambda i: (i // steps, i % steps, 0, 0)),
            pl.BlockSpec((heads * rows, rows * width), lambda i: (0, 0)),
        ],
        out_shape=[
            jax.ShapeDtypeStruct(pair.shape, f32),
            jax.ShapeDtypeStruct((heads * rows, rows * width), f32),
        ],
        scratch_shapes=[pltpu.VMEM((length, rows * width), bf16)],
        compiler_params=params(),
        cost_estimate=pl.CostEstimate(flops=2 * pair.size * 500, bytes_accessed=pair.size * 6, transcendentals=pair.size),
        name="pair_bwd",
    )(pair, bias_grad, weights)
    moments = moments.reshape(heads, rows, rows, width)
    return grad, sum(moments[:, r, r] for r in range(rows))


class Mover:
    def __init__(self, where, own, other, send, recv):
        self.where, self.own, self.other, self.send, self.recv = where, own, other, send, recv
        self.quarter = own.shape[0] // 4
        self.copies = []

    def go(self, k, name, src, at):
        rows = pl.ds(at * self.quarter, self.quarter)
        self.copies.append(
            remote(src.at[rows], self.other.at[rows], self.send.at[k], self.recv.at[k], across(self.where, name))
        )

    def first(self):
        self.go(0, "y", self.own, self.where["lo"])

    def second(self):
        self.go(1, "x", self.other, self.where["lo"])
        self.go(2, "c", self.other, self.where["lo"])

    def third(self):
        self.copies[1].wait_recv()
        self.go(3, "c", self.other, across(self.where, "x")["lo"])

    def last(self):
        self.copies[2].wait_recv()
        self.copies[3].wait_recv()
        for copy in self.copies:
            copy.wait_send()


def start_kernel(n_w, counts, pw, gain, pair, *refs):
    owns, others, spread = refs[:n_w], refs[n_w : 2 * n_w], refs[2 * n_w]
    x_buf, low_buf, bias_f, bias_v, x_sems, w_send, w_recv, b_send, b_recv, b_sem = refs[2 * n_w + 1 :]
    where = coords()
    peers = [across(where, *names) for names in PEERS]
    total = pair.shape[1]
    length, width = pair.shape[2:]
    heads = bias_f.shape[0]
    groups = 2 * total // 8

    def fetch(g, slot):
        return pltpu.make_async_copy(
            pair.at[(g * 8) // total, pl.ds(lax.rem(g * 8, total), 8)], x_buf.at[slot], x_sems.at[slot]
        )

    fetch(0, 0).start()
    greet(peers)
    movers = [Mover(where, owns[i], others[i], w_send.at[i], w_recv.at[i]) for i in range(n_w)]
    if movers:
        movers[0].first()

    def group(g, _):
        slot = lax.rem(g, 2)

        @pl.when(g + 1 < groups)
        def _():
            fetch(g + 1, 1 - slot).start()

        fetch(g, slot).wait()
        for r in range(0, 8, 2):
            x_hat, _ = pair_norm(x_buf[slot, r], x_buf[slot, r + 1])
            low_buf[:, r * width : (r + 2) * width] = (x_hat * gain[...]).astype(bf16)
        bias = dot(low_buf[...], pw[...]).T
        limit = counts[(g * 8) // total]
        valid = lax.broadcasted_iota(jnp.int32, bias.shape, 1) < limit
        bias = jnp.where(valid, bias * log2e, mask_fill)
        bias_f[:, pl.ds(pl.multiple_of(g * 8, 8), 8), :] = bias.reshape(heads, 8, length)
        return 0

    lax.fori_loop(0, groups, group, 0)
    each = heads // (len(PEERS) + 1)
    bias_v[...] = bias_f[...].astype(bf16).reshape(bias_v.shape)

    keep = pltpu.make_async_copy(bias_v.at[place(where)], spread.at[place(where)], b_sem)
    keep.start()
    sent = []

    def send_bias():
        for k, peer in enumerate(peers):
            sent.append(remote(bias_v.at[place(peer)], spread.at[place(where)], b_send.at[k], b_recv.at[k], peer))

    for i in range(n_w):
        movers[i].copies[0].wait_recv()
        if i + 1 < n_w:
            movers[i + 1].first()
        movers[i].second()
        if i == 0:
            send_bias()
        if i:
            movers[i - 1].third()
    if not sent:
        send_bias()
    if n_w:
        movers[-1].third()
    keep.wait()
    for copy in sent:
        copy.wait()
    for m in movers:
        m.last()


def start(counts, pair, pw_big, gain, owns):
    heads, length, width = 16, pair.shape[2], pair.shape[3]
    rows = 2 * pair.shape[1]
    n = len(owns)
    any_spec = pl.BlockSpec(memory_space=pl.ANY)
    vm = pl.BlockSpec(memory_space=pltpu.VMEM)
    return pl.pallas_call(
        functools.partial(start_kernel, n),
        in_specs=[pl.BlockSpec(memory_space=pltpu.SMEM), vm, vm, any_spec] + [any_spec] * n,
        out_specs=[any_spec] * (n + 1),
        out_shape=[jax.ShapeDtypeStruct(w.shape, bf16) for w in owns]
        + [jax.ShapeDtypeStruct((8, heads // 8, rows, length), bf16)],
        scratch_shapes=[
            pltpu.VMEM((2, 8, length, width), bf16),
            pltpu.VMEM((length, 8 * width), bf16),
            pltpu.VMEM((heads, rows, length), f32),
            pltpu.VMEM((8, heads // 8, rows, length), bf16),
            pltpu.SemaphoreType.DMA((2,)),
            pltpu.SemaphoreType.DMA((n, 4)),
            pltpu.SemaphoreType.DMA((n, 4)),
            pltpu.SemaphoreType.DMA((7,)),
            pltpu.SemaphoreType.DMA((7,)),
            pltpu.SemaphoreType.DMA,
        ],
        compiler_params=pltpu.CompilerParams(vmem_limit_bytes=vmem_bytes, collective_id=2, has_side_effects=True),
        name="start",
    )(counts, pw_big, gain, pair, *owns)


def big_weights(pw):
    width, heads = pw.shape
    eye = jnp.eye(8, dtype=pw.dtype)
    return (eye[:, None, None, :] * pw[None, :, :, None]).reshape(8 * width, heads * 8)


def attn_kernel(rb, owner_ref, x_ref, bias_ref, y_ref, bg_ref, acc_ref):
    n = pl.program_id(0)
    c = owner_ref[n]
    length, hd = x_ref.shape[-1], x_ref.shape[-2]
    up, bz = bias_ref.shape[0], bias_ref.shape[2]

    @pl.when(n == 0)
    def _():
        acc_ref[...] = jnp.zeros_like(acc_ref)

    k_t, v_t = x_ref[0, 1], x_ref[0, 2]
    v_ext = jnp.concatenate([v_t, jnp.ones((16, length), bf16)], axis=0)
    dv = dk = 0.0
    for r in range(length // rb):
        sl = slice(r * rb, (r + 1) * rb)
        q_t = x_ref[0, 0, :, sl]
        q = q_t.T
        dm = x_ref[0, 3, :, sl].astype(f32).T
        z0 = r * rb // bz
        bias = jnp.concatenate([bias_ref[z0 + t, c].astype(f32) for t in range(rb // bz)], axis=0)
        s = dot(q, k_t) + bias
        e = jnp.exp2(s - jnp.max(s, axis=-1, keepdims=True))
        eb = e.astype(bf16)
        mx = dot_nt(eb, v_ext)
        inv = 1.0 / mx[:, hd : hd + 1]
        mixed = mx[:, :hd] * inv
        d = jnp.sum(mixed * dm, axis=-1, keepdims=True) * inv
        dms = (dm * inv).astype(bf16)
        ds = e * (dot(dms, v_t) - d)
        dsb = ds.astype(bf16)
        acc_ref[c, sl, :] += ds
        dq = dot_nt(dsb, k_t)
        dv = dv + dot(dms.T, eb)
        dk = dk + dot(q_t, dsb)
        y_ref[0, 0, :, sl] = mixed.T.astype(bf16)
        y_ref[0, 1, :, sl] = (dq * hd**-0.5).T.astype(bf16)
    y_ref[0, 2] = (dk * ln2).astype(bf16)
    y_ref[0, 3] = dv.astype(bf16)

    @pl.when(n == pl.num_programs(0) - 1)
    def _():
        for z in range(up):
            for cc in range(2):
                bg_ref[z, cc] = acc_ref[cc, z * bz : (z + 1) * bz, :].astype(bf16)


def attention(owner, x, bias):
    n, four, hd, length = x.shape
    return pl.pallas_call(
        functools.partial(attn_kernel, length // 2),
        grid_spec=pltpu.PrefetchScalarGridSpec(
            num_scalar_prefetch=1,
            grid=(n,),
            in_specs=[
                pl.BlockSpec((1, four, hd, length), lambda i, _: (i, 0, 0, 0)),
                pl.BlockSpec(bias.shape, lambda i, _: (0, 0, 0, 0)),
            ],
            out_specs=[
                pl.BlockSpec((1, four, hd, length), lambda i, _: (i, 0, 0, 0)),
                pl.BlockSpec(bias.shape, lambda i, _: (0, 0, 0, 0)),
            ],
            scratch_shapes=[pltpu.VMEM((2, length, length), f32)],
        ),
        out_shape=[jax.ShapeDtypeStruct(x.shape, bf16), jax.ShapeDtypeStruct(bias.shape, bf16)],
        compiler_params=params(),
        cost_estimate=pl.CostEstimate(
            flops=12 * n * length * length * 256, bytes_accessed=x.size * 4 + bias.size * 4, transcendentals=n * length * length
        ),
        name="attention",
    )(owner, x, bias)


def pick(flag, a, b):
    return jnp.where(flag == 0, a, b)


def split_dot(flag, x, own, other):
    half = own.shape[0]
    first, second = x[:, :half], x[:, half:]
    return dot(pick(flag, first, second), own[...]) + dot(pick(flag, second, first), other[...])


def split_dot_nt(flag, x, own, other):
    a, b = dot_nt(x, own[...]), dot_nt(x, other[...])
    return jnp.concatenate([pick(flag, a, b), pick(flag, b, a)], axis=-1)


def front_kernel(
    flag_ref, tok, cond, og, cgain, wc0, wc1, cb, wq0, wq1, qb, wo0, wo1,
    *outs,
):
    *xs, sg_o, gg_o, s1_o, g1_o, first_o = outs
    flag = flag_ref[0]
    width = tok.shape[-1]
    hd = width // head_count
    slots = len(xs)
    peers = head_count // slots
    cond_low = (norm_parts(cond[...].astype(f32))[0] * cgain[...]).astype(bf16)
    modul = split_dot(flag, cond_low, wc0, wc1) + cb[...]
    s1 = jax.nn.sigmoid(modul[:, :width])
    g1 = jax.nn.sigmoid(modul[:, 2 * width :])
    tn, _ = norm_parts(tok[...].astype(f32))
    first = (s1 * tn + modul[:, width : 2 * width]).astype(bf16)
    proj = split_dot(flag, first, wq0, wq1)
    q = (proj[:, :width] + qb[...]) * (hd**-0.5 * log2e)
    sg = jax.nn.sigmoid(proj[:, 3 * width :])
    ga = (og[...].astype(f32) * g1).astype(bf16)
    gg = split_dot_nt(flag, ga, wo0, wo1)
    dm = sg * gg
    sg_o[...] = sg.astype(bf16)
    gg_o[...] = gg.astype(bf16)
    s1_o[...] = s1.astype(bf16)
    g1_o[...] = g1.astype(bf16)
    first_o[...] = first
    for i, part in enumerate((q, proj[:, width : 2 * width], proj[:, 2 * width : 3 * width], dm)):
        turned = part.T.astype(bf16).reshape(peers, slots, hd, part.shape[0])
        for t in range(slots):
            xs[t][:, i] = turned[:, t]


def half_spec(a, h):
    return pl.BlockSpec((a.shape[0], a.shape[1] // 2), lambda *_: (0, h))


def row_spec(a, rb):
    return pl.BlockSpec((rb, a.shape[1]), lambda i, *_: (i, 0))


def front(flag, tok, cond, og, cgain, wc, cb, wq, qb, wo, slots):
    length, width = tok.shape
    rb = 256
    peers, hd = head_count // slots, width // head_count
    small = jax.ShapeDtypeStruct((length, width), bf16)
    payload = jax.ShapeDtypeStruct((peers, 4, hd, length), bf16)
    return pl.pallas_call(
        front_kernel,
        grid_spec=pltpu.PrefetchScalarGridSpec(
            num_scalar_prefetch=1,
            grid=(length // rb,),
            in_specs=[row_spec(tok, rb), row_spec(cond, rb), row_spec(og, rb)]
            + [whole(cgain)]
            + [half_spec(a, 0) for a in wc]
            + [whole(a) for a in (cb, *wq, qb, *wo)],
            out_specs=[pl.BlockSpec((peers, 4, hd, rb), lambda i, _: (0, 0, 0, i))] * slots + [row_spec(tok, rb)] * 5,
        ),
        out_shape=[payload] * slots + [small] * 5,
        compiler_params=params(),
        cost_estimate=pl.CostEstimate(flops=2 * length * width * width * 7, bytes_accessed=20 << 20, transcendentals=length * width * 4),
        name="front",
    )(flag, tok, cond, og, cgain, *wc, cb, *wq, qb, *wo)


def trans_kernel(
    flag_ref, tok, cond, og, cgain, wc0, wc1, cb, wu0, wu1, wd0, wd1,
    part_o, u2_o, dcond_o, ml_o, cn_o, second_o, hid_o, act_o, gt_o, cbg_o,
):
    flag = flag_ref[0]
    width = tok.shape[-1]
    cond_low = (norm_parts(cond[...].astype(f32))[0] * cgain[...]).astype(bf16)
    cn_o[...] = cond_low
    modul = split_dot(flag, cond_low, wc0, wc1) + cb[...]
    s2 = jax.nn.sigmoid(modul[:, :width])
    g2 = jax.nn.sigmoid(modul[:, 2 * width :])
    tokens = tok[...].astype(f32)
    tn, _ = norm_parts(tokens)
    second = (s2 * tn + modul[:, width : 2 * width]).astype(bf16)
    second_o[...] = second
    hidden = split_dot(flag, second, wu0, wu1)
    ff = hidden.shape[1] // 2
    h_gate, h_up = hidden[:, :ff], hidden[:, ff:]
    sig = jax.nn.sigmoid(h_gate)
    silu = h_gate * sig
    act = (silu * h_up).astype(bf16)
    act_o[...] = act
    trans_out = split_dot(flag, act, wd0, wd1)
    part_o[...] = tokens + g2 * trans_out
    g = og[...].astype(f32)
    gt = (g * g2).astype(bf16)
    gt_o[...] = gt
    grad_act = split_dot_nt(flag, gt, wd0, wd1)
    hid = jnp.concatenate(
        [(grad_act * h_up * (sig * (1.0 + h_gate * (1.0 - sig)))).astype(bf16), (grad_act * silu).astype(bf16)], axis=-1
    )
    hid_o[...] = hid
    grad_second = split_dot_nt(flag, hid, wu0, wu1)
    u2_o[...] = (grad_second * s2).astype(bf16)
    grads = jnp.concatenate(
        [grad_second * tn * (s2 * (1.0 - s2)), grad_second, g * trans_out * (g2 * (1.0 - g2))], axis=-1
    )
    low = grads.astype(bf16)
    ml_o[...] = low

    @pl.when(pl.program_id(0) == 0)
    def _():
        cbg_o[...] = jnp.zeros_like(cbg_o)

    cbg_o[...] += jnp.sum(grads, axis=0, keepdims=True)
    dcond_o[...] = split_dot_nt(flag, low, wc0, wc1)


def transition(flag, tok, cond, og, cgain, wc, cb, wu, wd):
    length, width = tok.shape
    rb = 256
    cs, mw = cond.shape[1], cb.shape[1]
    ff2 = wu[0].shape[1]

    def out(w, dtype):
        return jax.ShapeDtypeStruct((length, w), dtype)

    shapes = [
        out(width, f32), out(width, bf16), out(cs, f32), out(mw, bf16), out(cs, bf16), out(width, bf16),
        out(ff2, bf16), out(ff2 // 2, bf16), out(width, bf16),
    ]
    return pl.pallas_call(
        trans_kernel,
        grid_spec=pltpu.PrefetchScalarGridSpec(
            num_scalar_prefetch=1,
            grid=(length // rb,),
            in_specs=[row_spec(tok, rb), row_spec(cond, rb), row_spec(og, rb)]
            + [whole(cgain)]
            + [half_spec(a, 1) for a in wc]
            + [whole(a) for a in (cb, *wu, *wd)],
            out_specs=[row_spec(s, rb) for s in shapes] + [pl.BlockSpec((1, mw), lambda i, _: (0, 0))],
        ),
        out_shape=shapes + [jax.ShapeDtypeStruct((1, mw), f32)],
        compiler_params=params(),
        cost_estimate=pl.CostEstimate(flops=2 * length * width * width * 15, bytes_accessed=40 << 20, transcendentals=length * width * 6),
        name="transition",
    )(flag, tok, cond, og, cgain, *wc, cb, *wu, *wd)


def back_kernel(slots, flag_ref, *refs):
    ys = refs[:slots]
    (
        sg, gg, s1, g1, part, u2, dcond2, tok, cond, og, cgain, wc0, wc1, wq0, wq1, wo0, wo1,
        out_o, tg_o, cg_o, gated_o, ga_o, gp_o, ml_o, qbg_o, cbg_o, cgg_o,
    ) = refs[slots:]
    flag = flag_ref[0]
    rb, width = tok.shape
    hd = width // head_count
    peers = head_count // slots

    def heads(i):
        stacked = jnp.stack([y[:, i] for y in ys], axis=1)
        return stacked.reshape(width, rb).astype(f32).T

    mixed = heads(0)
    sgv = sg[...].astype(f32)
    g1v = g1[...].astype(f32)
    gated = (sgv * mixed).astype(bf16)
    gated_o[...] = gated
    attn_out = split_dot(flag, gated, wo0, wo1)
    out_o[...] = part[...] + g1v * attn_out
    g = og[...].astype(f32)
    ga_o[...] = (g * g1v).astype(bf16)
    dg = gg[...].astype(f32) * mixed * (sgv * (1.0 - sgv))
    dq = heads(1)
    grad_proj = jnp.concatenate([dq.astype(bf16), heads(2).astype(bf16), heads(3).astype(bf16), dg.astype(bf16)], axis=-1)
    gp_o[...] = grad_proj
    grad_first = split_dot_nt(flag, grad_proj, wq0, wq1)
    s1v = s1[...].astype(f32)
    tn, tscale = norm_parts(tok[...].astype(f32))
    grads = jnp.concatenate(
        [grad_first * tn * (s1v * (1.0 - s1v)), grad_first, g * attn_out * (g1v * (1.0 - g1v))], axis=-1
    )
    low = grads.astype(bf16)
    ml_o[...] = low
    tg_o[...] = g + norm_back(tn, grad_first * s1v + u2[...].astype(f32), tscale)
    dcond = split_dot_nt(flag, low, wc0, wc1) + dcond2[...]
    cx, cscale = norm_parts(cond[...].astype(f32))
    cg_o[...] = norm_back(cx, dcond * cgain[...], cscale)

    @pl.when(pl.program_id(0) == 0)
    def _():
        qbg_o[...] = jnp.zeros_like(qbg_o)
        cbg_o[...] = jnp.zeros_like(cbg_o)
        cgg_o[...] = jnp.zeros_like(cgg_o)

    qbg_o[...] += jnp.sum(dq, axis=0, keepdims=True)
    cbg_o[...] += jnp.sum(grads, axis=0, keepdims=True)
    cgg_o[...] += jnp.sum(dcond * cx, axis=0, keepdims=True)


def back(flag, ys, sg, gg, s1, g1, part, u2, dcond2, tok, cond, og, cgain, wc, wq, wo):
    length, width = tok.shape
    rb = 256
    cs, mw = cond.shape[1], wc[0].shape[1] // 2
    rows = (sg, gg, s1, g1, part, u2, dcond2, tok, cond, og)
    consts = (*wq, *wo)

    def out(w, dtype):
        return jax.ShapeDtypeStruct((length, w), dtype)

    shapes = [
        out(width, f32), out(width, f32), out(cs, f32), out(width, bf16), out(width, bf16), out(wq[0].shape[1], bf16), out(mw, bf16),
    ]
    small = [jax.ShapeDtypeStruct((1, w), f32) for w in (width, mw, cs)]
    return pl.pallas_call(
        functools.partial(back_kernel, len(ys)),
        grid_spec=pltpu.PrefetchScalarGridSpec(
            num_scalar_prefetch=1,
            grid=(length // rb,),
            in_specs=[pl.BlockSpec(y.shape[:3] + (rb,), lambda i, _: (0, 0, 0, i)) for y in ys]
            + [row_spec(a, rb) for a in rows]
            + [whole(cgain)]
            + [half_spec(a, 0) for a in wc]
            + [whole(a) for a in consts],
            out_specs=[row_spec(s, rb) for s in shapes] + [pl.BlockSpec(s.shape, lambda i, _: (0, 0)) for s in small],
        ),
        out_shape=shapes + small,
        compiler_params=params(),
        cost_estimate=pl.CostEstimate(flops=2 * length * width * width * 7, bytes_accessed=40 << 20, transcendentals=length * width),
        name="back",
    )(flag, *ys, *rows, cgain, *wc, *consts)


def wgrad_kernel(shape, lhs, rhs, out_ref, turned):
    @pl.when(pl.program_id(0) == 0)
    def _():
        turned[...] = lhs[...].T

    out_ref[...] = dot(turned[...], rhs[...]).astype(bf16).reshape(out_ref.shape)


def wgrad(lhs, rhs):
    length, k = lhs.shape
    n = rhs.shape[1]
    row_groups = k // 96
    col_groups = 16 // row_groups
    piece = n // col_groups
    cols = piece if piece <= 1536 else piece // 2
    steps = n // cols
    per = piece // cols
    return pl.pallas_call(
        functools.partial(wgrad_kernel, None),
        grid=(steps,),
        in_specs=[whole(lhs), pl.BlockSpec((length, cols), lambda i: (0, i))],
        out_specs=pl.BlockSpec((2, row_groups, 48, cols), lambda i: (0, i // per, 0, i % per)),
        out_shape=jax.ShapeDtypeStruct((2, 16, 48, piece), bf16),
        scratch_shapes=[pltpu.VMEM((k, length), bf16)],
        compiler_params=params(),
        cost_estimate=pl.CostEstimate(flops=2 * length * k * n, bytes_accessed=2 * (length * (k + n) + k * n), transcendentals=0),
        name="wgrad",
    )(lhs, rhs)


def laid_out(pieces, rows):
    _, _, cols = pieces.shape
    row_groups = rows // 48
    blocks = pieces.reshape(16 // row_groups, rows, cols).astype(f32)
    return jnp.concatenate([blocks[t] for t in range(blocks.shape[0])], axis=1)


def reduce_kernel(plan, n_in, *refs):
    ins, (small, *outs), scratch = refs[:n_in], refs[n_in : 2 * n_in + 2], refs[2 * n_in + 2 :]
    small_o, outs = outs[0], outs[1:]
    n = len(plan)
    xs, rs = scratch[:n], scratch[n : 2 * n]
    sbuf, load_sems, send_sems, recv_sems, keep_sems, s_send, s_recv = scratch[2 * n :]
    where = coords()

    loads = []
    for i, (a, c0, w, order) in enumerate(plan):
        src = ins[a]
        at = ORDERS[order].index("y")
        before = 1 << at
        run = 32 >> (at + 1)
        mine = []
        for b in range(before):
            for f in range(2):
                mine.append(
                    pltpu.make_async_copy(
                        src.at[f, pl.ds(b * run, run), :, pl.ds(c0, w)],
                        xs[i].at[pl.ds((b * 2 + f) * run, run)],
                        load_sems.at[i, b * 2 + f],
                    )
                )
        for cp in mine:
            cp.start()
        loads.append(mine)
    sbuf[0] = small[...]
    greet([across(where, name) for name in BITS])

    base = [0] * n
    size = [32] * n
    roff = [0] * n
    pend = [None] * n
    sends = []

    def rs_start(i, k):
        name = ORDERS[plan[i][3]][k]
        half = size[i] // 2
        b = bit_of(where, name)
        copy = remote(
            xs[i].at[pl.ds(base[i] + (1 - b) * half, half)],
            rs[i].at[pl.ds(roff[i], half)],
            send_sems.at[i, k],
            recv_sems.at[i, k],
            across(where, name),
        )
        sends.append(copy)
        pend[i] = copy
        base[i] = base[i] + b * half
        size[i] = half

    def rs_finish(i, k):
        pend[i].wait_recv()
        half, b0, r0 = size[i], base[i], roff[i]

        def body(j, _):
            xs[i][b0 + j] = (xs[i][b0 + j].astype(f32) + rs[i][r0 + j].astype(f32)).astype(bf16)
            return 0

        lax.fori_loop(0, half, body, 0)
        roff[i] = r0 + half

    place = [None] * n

    def ag_begin(i):
        a, c0, w, order = plan[i]
        p = 0
        for name in ORDERS[order]:
            if name != "y":
                p = p * 2 + bit_of(where, name)
        place[i] = p
        copy = pltpu.make_async_copy(
            xs[i].at[pl.ds(base[i], 1)], outs[a].at[pl.ds(p, 1), :, pl.ds(c0, w)], keep_sems.at[i]
        )
        copy.start()
        copy.wait()

    def ag_start(i, j):
        a, c0, w, order = plan[i]
        name = [m for m in ORDERS[order] if m != "y"][3 - j]
        block = 1 << j
        start = place[i] - lax.rem(place[i], block)
        ref = outs[a].at[pl.ds(start, block), :, pl.ds(c0, w)]
        copy = remote(ref, ref, send_sems.at[i, 5 + j], recv_sems.at[i, 5 + j], across(where, name))
        sends.append(copy)
        pend[i] = copy

    def advance(i, k):
        if k == 0:
            for cp in loads[i]:
                cp.wait()
            rs_start(i, 0)
        elif k < 5:
            rs_finish(i, k - 1)
            rs_start(i, k)
        elif k == 5:
            rs_finish(i, 4)
            ag_begin(i)
            ag_start(i, 0)
        elif k < 9:
            pend[i].wait_recv()
            ag_start(i, k - 5)
        else:
            pend[i].wait_recv()

    def small_step(k):
        if k > 0:
            scopy[k - 1].wait_recv()
            sbuf[2 * k] = sbuf[2 * k - 2] + sbuf[2 * k - 1]
        if k < 5:
            name = list(BITS)[k]
            copy = remote(sbuf.at[2 * k], sbuf.at[2 * k + 1], s_send.at[k], s_recv.at[k], across(where, name))
            sends.append(copy)
            scopy.append(copy)

    scopy = []
    for t in range(10):
        for i in range(n):
            advance(i, t)
            if i == 0 and t < 6:
                small_step(t)
    small_o[...] = sbuf[10]
    for copy in sends:
        copy.wait_send()


def reduce_all(arrays, small, plan):
    n = len(plan)
    shapes = [jax.ShapeDtypeStruct(a.shape[1:], bf16) for a in arrays]
    return pl.pallas_call(
        functools.partial(reduce_kernel, plan, len(arrays)),
        out_shape=[jax.ShapeDtypeStruct(small.shape, f32)] + shapes,
        in_specs=[pl.BlockSpec(memory_space=pl.ANY)] * len(arrays) + [pl.BlockSpec(memory_space=pltpu.VMEM)],
        out_specs=[pl.BlockSpec(memory_space=pltpu.VMEM)] + [pl.BlockSpec(memory_space=pl.ANY)] * len(arrays),
        scratch_shapes=[pltpu.VMEM((32, 48, w), bf16) for _, _, w, _ in plan]
        + [pltpu.VMEM((31, 48, w), bf16) for _, _, w, _ in plan]
        + [
            pltpu.VMEM((11,) + small.shape, f32),
            pltpu.SemaphoreType.DMA((n, 8)),
            pltpu.SemaphoreType.DMA((n, 9)),
            pltpu.SemaphoreType.DMA((n, 9)),
            pltpu.SemaphoreType.DMA((n,)),
            pltpu.SemaphoreType.DMA((5,)),
            pltpu.SemaphoreType.DMA((5,)),
        ],
        compiler_params=pltpu.CompilerParams(vmem_limit_bytes=vmem_bytes, collective_id=1, has_side_effects=True),
        name="reduce_grads",
    )(*arrays, small)


reduce_plan = (
    (0, 0, 768, 0),
    (0, 768, 768, 1),
    (1, 0, 640, 0),
    (1, 640, 512, 1),
    (2, 0, 384, 1),
    (3, 0, 768, 0),
    (3, 768, 768, 1),
    (4, 0, 384, 0),
    (4, 384, 384, 1),
)


def on_device(
    tokens, cond, pair, counts, owner, out_grad, cond_gain, cond_weight, cond_bias, qkvg_weight, query_bias,
    out_weight, pair_gain, pair_weight, up_weight, down_weight,
):
    ups, los, ffs = lax.axis_size("up"), lax.axis_size("lo"), lax.axis_size("fsdp")
    plane = ("lo", "fsdp")
    members = los * ffs
    slots = head_count // members
    length, width = tokens.shape[1:]
    rows = pair.shape[1]
    fs = lax.axis_index("fsdp")
    direct = ffs == 2 and los == 4 and ups == 4

    def halves(w):
        full = lax.all_gather(w, "fsdp", axis=0, tiled=True)
        half = full.shape[0] // 2
        return full[:half], full[half:]

    flag = (fs if direct else jnp.zeros((), jnp.int32)).astype(jnp.int32).reshape(1)
    wide = 3 * width

    def spread(got):
        mine = got.reshape(members, 2, rows, length).transpose(1, 0, 2, 3).reshape(2, members * rows, length)
        return lax.all_gather(mine, "up", axis=0, tiled=False)

    matrices = (cond_weight, qkvg_weight, out_weight, up_weight, down_weight)
    if direct:
        *others, spreads = start(counts, pair, big_weights(pair_weight), jnp.tile(pair_gain, 2)[None], matrices)
        wc, wq, wo, wu, wd = zip(matrices, others)
    else:
        bias = pair_fwd(counts, pair, pair_weight.T, pair_gain[None])
        bias = bias.reshape(members, slots, 2 * rows, length)
        spreads = lax.all_to_all(bias, plane, 0, 0, tiled=True)
        wc, wq, wo, wu, wd = [halves(w) for w in matrices]
    biases = [spread(spreads[:, t]) for t in range(slots)]

    tok, cnd, og = tokens[0], cond[0], out_grad[0]
    cgain = cond_gain[None]
    *xs, sg, gg, s1, g1, first = front(
        flag, tok, cnd, og, cgain, wc, cond_bias[None, :wide], wq, query_bias[None], wo, slots
    )
    xs[0] = lax.all_to_all(xs[0], plane, 0, 0, tiled=True)
    part, u2, dcond2, ml2, cn, second, hid, act, gt, cbg2 = transition(
        flag, tok, cnd, og, cgain, wc, cond_bias[None, wide:], wu, wd
    )
    *xs, hid = lax.optimization_barrier((*xs, hid))
    xs = [xs[0]] + [lax.all_to_all(x, plane, 0, 0, tiled=True) for x in xs[1:]]

    def fold(g):
        k, n = g.shape
        if k == width:
            return g
        if k > width:
            times = k // width
            parts = g.reshape(ffs, times, width // ffs, n)
            return jnp.concatenate([parts[:, t] for t in range(times)], axis=-1).reshape(width, n * times)
        times = width // k
        parts = g.reshape(ffs, k // ffs, times, n // times)
        return jnp.concatenate([parts[:, :, t] for t in range(times)], axis=1).reshape(width, n // times)

    def unfold(h, k, n):
        rows_each = width // ffs
        if k == width:
            return h
        if k > width:
            times = k // width
            return jnp.concatenate([h[:, t * n : (t + 1) * n] for t in range(times)], axis=0)
        times = width // k
        step = rows_each // times
        return jnp.concatenate([h[t * step : (t + 1) * step] for t in range(times)], axis=1)

    def reduced(grads):
        folded = [fold(g) for g in grads]
        mine = lax.psum_scatter(
            jnp.concatenate(folded, axis=1), ("fsdp", "up", "lo"), scatter_dimension=0, tiled=True
        )
        full = lax.all_gather(mine, ("up", "lo"), axis=0, tiled=True)
        outs, at = [], 0
        for g, h in zip(grads, folded):
            outs.append(unfold(full[:, at : at + h.shape[1]], *g.shape).astype(f32))
            at += h.shape[1]
        return outs

    if direct:
        early = [wgrad(second, hid), wgrad(act, gt)]
        xs[0], *early = lax.optimization_barrier((xs[0], *early))
    else:
        up_total, down_total = reduced([dot_tn(second, hid).astype(bf16), dot_tn(act, gt).astype(bf16)])

    owners = lax.dynamic_slice_in_dim(owner, lax.axis_index("up") * members, members)
    ys, bias_grads = [], []
    for t in range(slots):
        y, bg = attention(owners, xs[t], biases[t])
        ys.append(lax.all_to_all(y, plane, 0, 0, tiled=True))
        mine = lax.psum_scatter(bg, "up", scatter_dimension=0, tiled=True)
        mine = mine.reshape(2, members, rows, length).transpose(1, 0, 2, 3)
        bias_grads.append(lax.all_to_all(mine, plane, 0, 0, tiled=True))

    block_out, tokens_grad, cond_grad, gated, ga, gp, ml1, qbg, cbg1, cgg = back(
        flag, ys, sg, gg, s1, g1, part, u2, dcond2, tok, cnd, og, cgain, wc, wq, wo
    )
    ml = jnp.concatenate([ml1, ml2], axis=1)
    if not direct:
        qkvg_total, out_total, cond_total = reduced(
            [dot_tn(first, gp).astype(bf16), dot_tn(gated, ga).astype(bf16), dot_tn(cn, ml).astype(bf16)]
        )

    bias_grad = jnp.stack(bias_grads, axis=1).reshape(head_count, 2, rows, length)
    pw = pair_weight.astype(f32).T
    scaled = pw * pair_gain
    centered = scaled - jnp.mean(scaled, axis=-1, keepdims=True)
    high = centered.astype(bf16)
    low = (centered - high.astype(f32)).astype(bf16)
    pair_grad, moments = pair_bwd(pair, bias_grad, high, low)
    pieces = [cgg, cbg1, cbg2, qbg, moments.reshape(1, -1)]
    stacked = jnp.concatenate([p.reshape(-1, 128) for p in pieces], axis=0)
    if direct:
        height = -(-stacked.shape[0] // 8) * 8
        stacked = jnp.pad(stacked, ((0, height - stacked.shape[0]), (0, 0)))
        late = [wgrad(first, gp), wgrad(cn, ml), wgrad(gated, ga)]
        stacked, *totals = reduce_all(late + early, stacked, reduce_plan)
        qkvg_total, cond_total, out_total, up_total, down_total = [
            laid_out(p, w.shape[0]) for p, w in zip(totals, (qkvg_weight, cond_weight, out_weight, up_weight, down_weight))
        ]
    else:
        stacked = lax.psum(stacked, ("up", "lo", "fsdp"))
    small = stacked.reshape(-1)
    ends = [0]
    for p in pieces:
        ends.append(ends[-1] + p.size)
    small = [small[a:b] for a, b in zip(ends[:-1], ends[1:])]
    moments = small[4].reshape(moments.shape)
    return (
        block_out[None],
        tokens_grad[None],
        cond_grad[None],
        pair_grad,
        small[0],
        cond_total,
        jnp.concatenate([small[1], small[2]]),
        qkvg_total,
        small[3],
        out_total,
        jnp.sum(pw * moments, axis=0),
        (moments * pair_gain).T,
        up_total,
        down_total,
    )


def solution(mesh):
    dp, fsdp = mesh.shape["dp"], mesh.shape["fsdp"]
    lo = max(1, group_size // fsdp)
    fine = Mesh(mesh.devices.reshape(dp // lo, lo, fsdp), ("up", "lo", "fsdp"))
    every = ("up", "lo", "fsdp")
    in_specs = (
        P(every, None, None),
        P(every, None, None),
        P(None, every, None, None),
        P(),
        P(),
        P(every, None, None),
        P(),
        P("fsdp", None),
        P(),
        P("fsdp", None),
        P(),
        P("fsdp", None),
        P(),
        P(),
        P("fsdp", None),
        P("fsdp", None),
    )
    out_specs = (
        P(every, None, None),
        P(every, None, None),
        P(every, None, None),
        P(None, every, None, None),
        P(),
        P("fsdp", None),
        P(),
        P("fsdp", None),
        P(),
        P("fsdp", None),
        P(),
        P(),
        P("fsdp", None),
        P("fsdp", None),
    )
    return jax.shard_map(on_device, mesh=fine, in_specs=in_specs, out_specs=out_specs, check_vma=False)
```

```python
import functools

import jax
import jax.numpy as jnp
from jax import lax
from jax.experimental import pallas as pl
from jax.experimental.pallas import tpu as pltpu
from jax.sharding import Mesh, PartitionSpec as P

f32, bf16 = jnp.float32, jnp.bfloat16
norm_eps = 1e-05
mask_fill = -1000000000.0
log2e = 1.4426950408889634
ln2 = 0.6931471805599453
head_count = 16
group_size = 8
vmem_bytes = 58 << 20
nt_dims = (((1,), (1,)), ((), ()))


def dot(a, b):
    return jnp.dot(a, b, preferred_element_type=f32)


def dot_nt(a, b):
    return lax.dot_general(a, b, nt_dims, preferred_element_type=f32)


def dot_tn(a, b):
    return lax.dot_general(a, b, (((0,), (0,)), ((), ())), preferred_element_type=f32)


def norm_parts(values):
    centered = values - jnp.mean(values, axis=-1, keepdims=True)
    variance = jnp.mean(centered * centered, axis=-1, keepdims=True)
    scale = lax.rsqrt(variance + norm_eps)
    return centered * scale, scale


def norm_back(x, u, scale):
    mean_u = jnp.mean(u, axis=-1, keepdims=True)
    mean_ux = jnp.mean(u * x, axis=-1, keepdims=True)
    return (u - mean_u - x * mean_ux) * scale


def params(**kw):
    return pltpu.CompilerParams(vmem_limit_bytes=vmem_bytes, **kw)


def whole(a):
    zero = (0,) * a.ndim
    return pl.BlockSpec(a.shape, lambda *_: zero)


MESH = pl.DeviceIdType.MESH
BITS = {"c": ("lo", 1), "x": ("lo", 2), "y": ("fsdp", 1), "z0": ("up", 1), "z1": ("up", 2)}
PEERS = (("c",), ("x",), ("y",), ("c", "x"), ("c", "y"), ("x", "y"), ("c", "x", "y"))
SAMPLE_ORDER = (("x",), ("y",), ("x", "y"), ("c", "x"), ("c", "y"), ("c", "x", "y"), ("c",), ())
SUM_ORDERS = (("c", "x", "y", "z0", "z1"), ("c", "y", "z0", "x", "z1"), ("c", "z0", "x", "y", "z1"))
COPY_ORDERS = (("z1", "z0", "x", "c"), ("x", "z1", "z0", "c"))


def coords():
    return {a: lax.axis_index(a) for a in ("up", "lo", "fsdp")}


def bit_of(where, name):
    axis, value = BITS[name]
    return lax.rem(where[axis] // value, 2)


def across(where, *names):
    other = dict(where)
    for name in names:
        axis, value = BITS[name]
        other[axis] = other[axis] + value * (1 - 2 * bit_of(where, name))
    return other


def device(where):
    return (where["up"], where["lo"], where["fsdp"])


def place(where):
    return where["lo"] * 2 + where["fsdp"]


def greet(devices):
    barrier = pltpu.get_barrier_semaphore()
    for other in devices:
        pl.semaphore_signal(barrier, inc=1, device_id=device(other), device_id_type=MESH)
    pl.semaphore_wait(barrier, len(devices))


def remote(src, dst, send_sem, recv_sem, other):
    copy = pltpu.make_async_remote_copy(
        src_ref=src, dst_ref=dst, send_sem=send_sem, recv_sem=recv_sem, device_id=device(other), device_id_type=MESH
    )
    copy.start()
    return copy


def lane_means(values):
    total = values.shape[-1]
    group = lax.broadcasted_iota(jnp.int32, (total, total), 0) // 128 == lax.broadcasted_iota(jnp.int32, (total, total), 1) // 128
    return dot(values, jnp.where(group, 1.0 / 128, 0.0).astype(bf16))


def pair_norm(*blocks):
    x = jnp.concatenate(blocks, axis=-1)
    centered = x.astype(f32) - lane_means(x)
    variance = lane_means((centered * centered).astype(bf16))
    scale = lax.rsqrt(variance + norm_eps)
    return centered * scale, scale


def pair_fwd_kernel(rows, counts_ref, x_ref, pw_ref, gain_ref, out_ref, scr_ref):
    step = pl.program_id(0)
    steps_each = pl.num_programs(0) // 2
    limit = counts_ref[step // steps_each]
    heads, length = scr_ref.shape[0], scr_ref.shape[2]
    valid = lax.broadcasted_iota(jnp.int32, (heads, length), 1) < limit
    pw = pw_ref[...]
    gain = gain_ref[...]
    for r in range(rows):
        low = (pair_norm(x_ref[0, r])[0] * gain).astype(bf16)
        bias = dot_nt(pw, low)
        scr_ref[:, r, :] = jnp.where(valid, bias * log2e, mask_fill)
    out_ref[:, 0] = scr_ref[...].astype(bf16)


def pair_fwd(counts, pair, pw_t, gain):
    _, total, length, width = pair.shape
    rows = 8 if total % 8 == 0 else total
    steps = total // rows
    heads = pw_t.shape[0]
    return pl.pallas_call(
        functools.partial(pair_fwd_kernel, rows),
        grid_spec=pltpu.PrefetchScalarGridSpec(
            num_scalar_prefetch=1,
            grid=(2 * steps,),
            in_specs=[
                pl.BlockSpec((1, rows, length, width), lambda i, _: (i // steps, i % steps, 0, 0)),
                whole(pw_t),
                whole(gain),
            ],
            out_specs=pl.BlockSpec((heads, 1, rows, length), lambda i, _: (0, i // steps, i % steps, 0)),
            scratch_shapes=[pltpu.VMEM((heads, rows, length), f32)],
        ),
        out_shape=jax.ShapeDtypeStruct((heads, 2, total, length), bf16),
        compiler_params=params(),
        cost_estimate=pl.CostEstimate(flops=2 * pair.size * 300, bytes_accessed=pair.size * 2, transcendentals=pair.size),
        name="pair_fwd",
    )(counts, pair, pw_t, gain)


def pair_bwd_kernel(rows, x_ref, bg_ref, a_ref, out_ref, q_ref, low_buf):
    @pl.when(pl.program_id(0) == 0)
    def _():
        q_ref[...] = jnp.zeros_like(q_ref)

    width = out_ref.shape[-1]
    heads, _, _, length = bg_ref.shape
    grads = bg_ref[:, 0].astype(f32).reshape(heads * rows, length)
    turned = grads.T.astype(bf16)
    u_all = dot(jnp.concatenate([turned, turned], axis=1), a_ref[...])
    step = 2 - rows % 2
    for r in range(0, rows, step):
        x_hat, scale = pair_norm(*(x_ref[0, r + t] for t in range(step)))
        low_buf[:, r * width : (r + step) * width] = x_hat.astype(bf16)
        u = u_all[:, r * width : (r + step) * width]
        grad = (u - x_hat * lane_means((u * x_hat).astype(bf16))) * scale
        for t in range(step):
            out_ref[0, r + t] = grad[:, t * width : (t + 1) * width]
    q_ref[...] += dot(grads.astype(bf16), low_buf[...])


def pair_bwd(pair, bias_grad, high, low):
    _, total, length, width = pair.shape
    rows = 8 if total % 8 == 0 else total
    steps = total // rows
    heads = bias_grad.shape[0]
    eye = jnp.eye(rows, dtype=bf16)
    both = jnp.stack([high, low])
    weights = (both[:, :, None, None, :] * eye[None, None, :, :, None]).reshape(2 * heads * rows, rows * width)
    grad, moments = pl.pallas_call(
        functools.partial(pair_bwd_kernel, rows),
        grid=(2 * steps,),
        in_specs=[
            pl.BlockSpec((1, rows, length, width), lambda i: (i // steps, i % steps, 0, 0)),
            pl.BlockSpec((heads, 1, rows, length), lambda i: (0, i // steps, i % steps, 0)),
            whole(weights),
        ],
        out_specs=[
            pl.BlockSpec((1, rows, length, width), lambda i: (i // steps, i % steps, 0, 0)),
            pl.BlockSpec((heads * rows, rows * width), lambda i: (0, 0)),
        ],
        out_shape=[
            jax.ShapeDtypeStruct(pair.shape, f32),
            jax.ShapeDtypeStruct((heads * rows, rows * width), f32),
        ],
        scratch_shapes=[pltpu.VMEM((length, rows * width), bf16)],
        compiler_params=params(),
        cost_estimate=pl.CostEstimate(flops=2 * pair.size * 500, bytes_accessed=pair.size * 6, transcendentals=pair.size),
        name="pair_bwd",
    )(pair, bias_grad, weights)
    moments = moments.reshape(heads, rows, rows, width)
    return grad, sum(moments[:, r, r] for r in range(rows))


class Mover:
    def __init__(self, where, order, own, full, stage, send, recv, keep):
        self.where, self.order, self.own, self.full, self.send, self.recv = where, order, own, full, send, recv
        self.half = own.shape[0]
        self.piece = self.half >> len(order)
        self.mine = sum(bit_of(where, name) << j for j, name in enumerate(order))
        self.copies = []
        self.kept = [
            pltpu.make_async_copy(own, stage, keep.at[0]),
            pltpu.make_async_copy(stage, full.at[pl.ds(where["fsdp"] * self.half, self.half)], keep.at[1]),
        ]

    def stage(self, k):
        if k:
            self.kept[k - 1].wait()
        if k < 2:
            self.kept[k].start()

    def advance(self, k):
        if k:
            self.copies[k - 1].wait_recv()
        if k == 0:
            name, src_at = "y", self.mine * self.piece
            at, size = self.where["fsdp"] * self.half + src_at, self.piece
            src = self.own.at[pl.ds(src_at, size)]
        elif k <= len(self.order):
            name, size = self.order[k - 1], self.piece << (k - 1)
            at = (1 - self.where["fsdp"]) * self.half + self.mine * self.piece // size * size
            src = self.full.at[pl.ds(at, size)]
        else:
            return
        dst = self.full.at[pl.ds(at, size)]
        self.copies.append(remote(src, dst, self.send.at[k], self.recv.at[k], across(self.where, name)))

    def finish(self):
        self.stage(2)
        for copy in self.copies:
            copy.wait_send()


MOVES = (("x", "c"), ("x", "z0", "c"), ("x", "z0", "c"), ("z0", "x", "c"), ("x", "z0", "c"))


def start_kernel(n_w, counts, pw, gain, pair, *refs):
    owns, others, spread = refs[:n_w], refs[n_w : 2 * n_w], refs[2 * n_w]
    *stages, x_buf, low_buf, bias_f, bias_v, x_sems, w_send, w_recv, w_keep, b_send, b_recv, b_sem = refs[2 * n_w + 1 :]
    where = coords()
    peers = [across(where, *names) for names in PEERS]
    total = pair.shape[1]
    length, width = pair.shape[2:]
    heads = bias_f.shape[0]
    groups = 2 * total // 8

    def fetch(g, slot):
        return pltpu.make_async_copy(
            pair.at[(g * 8) // total, pl.ds(lax.rem(g * 8, total), 8)], x_buf.at[slot], x_sems.at[slot]
        )

    fetch(0, 0).start()
    greet(peers + [across(where, "z0")])
    movers = [Mover(where, MOVES[i], owns[i], others[i], stages[i], w_send.at[i], w_recv.at[i], w_keep.at[i]) for i in range(n_w)]
    for m in movers:
        m.advance(0)
    for m in movers:
        m.stage(0)

    def group(g, _):
        slot = lax.rem(g, 2)

        @pl.when(g + 1 < groups)
        def _():
            fetch(g + 1, 1 - slot).start()

        fetch(g, slot).wait()
        for r in range(0, 8, 2):
            x_hat, _ = pair_norm(x_buf[slot, r], x_buf[slot, r + 1])
            low_buf[:, r * width : (r + 2) * width] = (x_hat * gain[...]).astype(bf16)
        bias = dot(low_buf[...], pw[...]).T
        limit = counts[(g * 8) // total]
        valid = lax.broadcasted_iota(jnp.int32, bias.shape, 1) < limit
        bias = jnp.where(valid, bias * log2e, mask_fill)
        bias_f[:, pl.ds(pl.multiple_of(g * 8, 8), 8), :] = bias.reshape(heads, 8, length)
        return 0

    third = groups // 3
    for k in range(3):
        lax.fori_loop(k * third, (k + 1) * third, group, 0)
        movers[k].advance(1)
    for m in movers:
        m.stage(1)
    bias_v[...] = bias_f[...].astype(bf16).reshape(bias_v.shape)

    keep = pltpu.make_async_copy(bias_v.at[place(where)], spread.at[place(where)], b_sem)
    keep.start()
    sent = []

    def send_bias():
        for k, peer in enumerate(peers):
            sent.append(remote(bias_v.at[place(peer)], spread.at[place(where)], b_send.at[k], b_recv.at[k], peer))

    for m in movers[3:]:
        m.advance(1)
    send_bias()
    for k in range(2, 5):
        for m in movers:
            if k <= len(m.order) + 1:
                m.advance(k)
    keep.wait()
    for copy in sent:
        copy.wait()
    for m in movers:
        m.finish()


def start(counts, pair, pw_big, gain, owns):
    heads, length, width = 16, pair.shape[2], pair.shape[3]
    rows = 2 * pair.shape[1]
    n = len(owns)
    any_spec = pl.BlockSpec(memory_space=pl.ANY)
    vm = pl.BlockSpec(memory_space=pltpu.VMEM)
    return pl.pallas_call(
        functools.partial(start_kernel, n),
        in_specs=[pl.BlockSpec(memory_space=pltpu.SMEM), vm, vm, any_spec] + [any_spec] * n,
        out_specs=[any_spec] * (n + 1),
        out_shape=[jax.ShapeDtypeStruct((2 * w.shape[0], w.shape[1]), bf16) for w in owns]
        + [jax.ShapeDtypeStruct((8, heads // 8, rows, length), bf16)],
        scratch_shapes=[pltpu.VMEM(w.shape, bf16) for w in owns]
        + [
            pltpu.VMEM((2, 8, length, width), bf16),
            pltpu.VMEM((length, 8 * width), bf16),
            pltpu.VMEM((heads, rows, length), f32),
            pltpu.VMEM((8, heads // 8, rows, length), bf16),
            pltpu.SemaphoreType.DMA((2,)),
            pltpu.SemaphoreType.DMA((n, 4)),
            pltpu.SemaphoreType.DMA((n, 4)),
            pltpu.SemaphoreType.DMA((n, 2)),
            pltpu.SemaphoreType.DMA((7,)),
            pltpu.SemaphoreType.DMA((7,)),
            pltpu.SemaphoreType.DMA,
        ],
        compiler_params=pltpu.CompilerParams(vmem_limit_bytes=vmem_bytes, collective_id=2, has_side_effects=True),
        name="start",
    )(counts, pw_big, gain, pair, *owns)


def big_weights(pw):
    width, heads = pw.shape
    eye = jnp.eye(8, dtype=pw.dtype)
    return (eye[:, None, None, :] * pw[None, :, :, None]).reshape(8 * width, heads * 8)


def attend(rb, c, x_ref, y_ref, bias_ref, add):
    length, hd = x_ref.shape[-1], x_ref.shape[-2]
    bz = bias_ref.shape[2]
    k_t, v_t = x_ref[1], x_ref[2]
    v_ext = jnp.concatenate([v_t, jnp.ones((16, length), bf16)], axis=0)
    dv = dk = 0.0
    for r in range(length // rb):
        sl = slice(r * rb, (r + 1) * rb)
        q_t = x_ref[0, :, sl]
        q = q_t.T
        dm = x_ref[3, :, sl].astype(f32).T
        z0 = r * rb // bz
        bias = jnp.concatenate([bias_ref[z0 + t, c].astype(f32) for t in range(rb // bz)], axis=0)
        s = dot(q, k_t) + bias
        e = jnp.exp2(s - jnp.max(s, axis=-1, keepdims=True))
        eb = e.astype(bf16)
        mx = dot_nt(eb, v_ext)
        inv = 1.0 / mx[:, hd : hd + 1]
        mixed = mx[:, :hd] * inv
        d = jnp.sum(mixed * dm, axis=-1, keepdims=True) * inv
        dms = (dm * inv).astype(bf16)
        ds = e * (dot(dms, v_t) - d)
        dsb = ds.astype(bf16)
        add(sl, ds)
        dq = dot_nt(dsb, k_t)
        dv = dv + dot(dms.T, eb)
        dk = dk + dot(q_t, dsb)
        y_ref[0, :, sl] = mixed.T.astype(bf16)
        y_ref[1, :, sl] = (dq * hd**-0.5).T.astype(bf16)
    y_ref[2] = (dk * ln2).astype(bf16)
    y_ref[3] = dv.astype(bf16)


def attn_kernel(rb, owner_ref, x_ref, bias_ref, y_ref, bg_ref, acc_ref):
    n = pl.program_id(0)
    c = owner_ref[n]
    up, bz = bias_ref.shape[0], bias_ref.shape[2]

    @pl.when(n == 0)
    def _():
        acc_ref[...] = jnp.zeros_like(acc_ref)

    def add(sl, ds):
        acc_ref[c, sl, :] += ds

    attend(rb, c, x_ref.at[0], y_ref.at[0], bias_ref, add)

    @pl.when(n == pl.num_programs(0) - 1)
    def _():
        for z in range(up):
            for cc in range(2):
                bg_ref[z, cc] = acc_ref[cc, z * bz : (z + 1) * bz, :].astype(bf16)


def sending_attn_kernel(
    rb, slot, owner_ref, x_ref, bias_ref, y_ref, bg_ref, both, second, x_buf, y_buf, x_sems, y_send, y_recv, y_keep
):
    step = pl.program_id(0)
    steps = pl.num_programs(0)
    where = coords()
    up, bz = bias_ref.shape[0], bias_ref.shape[2]

    def partner(k):
        other = dict(where)
        for name in ("c", "x", "y"):
            axis, value = BITS[name]
            flip = sum(jnp.where(k == i, 1, 0) for i, names in enumerate(SAMPLE_ORDER) if name in names)
            other[axis] = other[axis] + flip * value * (1 - 2 * bit_of(where, name))
        return other

    def fetch(k):
        return pltpu.make_async_copy(
            x_ref.at[place(partner(k)), pl.ds(slot * 4, 4)], x_buf.at[lax.rem(k, 2)], x_sems.at[lax.rem(k, 2)]
        )

    def sent(k, to):
        return pltpu.make_async_remote_copy(
            src_ref=y_buf.at[k],
            dst_ref=y_ref.at[place(to)],
            send_sem=y_send.at[k],
            recv_sem=y_recv.at[k],
            device_id=device(partner(k)),
            device_id_type=MESH,
        )

    keep = pltpu.make_async_copy(y_buf.at[len(PEERS)], y_ref.at[place(where)], y_keep)

    @pl.when(step == 0)
    def _():
        fetch(0).start()
        both[...] = jnp.zeros_like(both)
        second[...] = jnp.zeros_like(second)
        greet([across(where, *names) for names in PEERS])

    @pl.when(step + 1 < steps)
    def _():
        fetch(step + 1).start()

    fetch(step).wait()
    c = owner_ref[place(partner(step))]
    weight = c.astype(f32)

    def add(sl, ds):
        both[sl, :] += ds
        second[sl, :] += ds * weight

    attend(rb, c, x_buf.at[lax.rem(step, 2)], y_buf.at[step], bias_ref, add)

    @pl.when(step < steps - 1)
    def _():
        sent(step, where).start()

    @pl.when(step == steps - 1)
    def _():
        keep.start()
        for z in range(up):
            sl = slice(z * bz, (z + 1) * bz)
            bg_ref[z, 0] = (both[sl, :] - second[sl, :]).astype(bf16)
            bg_ref[z, 1] = second[sl, :].astype(bf16)
        keep.wait()
        for k in range(len(PEERS)):
            sent(k, partner(k)).wait_recv()
            sent(k, where).wait_send()


def sending_attention(owner, x, bias, slot):
    n, _, hd, length = x.shape
    any_spec = pl.BlockSpec(memory_space=pl.ANY)
    vm = pl.BlockSpec(memory_space=pltpu.VMEM)
    return pl.pallas_call(
        functools.partial(sending_attn_kernel, length // 2, slot),
        grid=(n,),
        in_specs=[pl.BlockSpec(memory_space=pltpu.SMEM), any_spec, vm],
        out_specs=[any_spec, vm],
        out_shape=[jax.ShapeDtypeStruct((n, 4, hd, length), bf16), jax.ShapeDtypeStruct(bias.shape, bf16)],
        scratch_shapes=[
            pltpu.VMEM((length, length), f32),
            pltpu.VMEM((length, length), f32),
            pltpu.VMEM((2, 4, hd, length), bf16),
            pltpu.VMEM((n, 4, hd, length), bf16),
            pltpu.SemaphoreType.DMA((2,)),
            pltpu.SemaphoreType.DMA((n,)),
            pltpu.SemaphoreType.DMA((n,)),
            pltpu.SemaphoreType.DMA,
        ],
        compiler_params=params(collective_id=3 + slot, has_side_effects=True),
        cost_estimate=pl.CostEstimate(
            flops=12 * n * length * length * 256, bytes_accessed=x.size * 2 + bias.size * 4, transcendentals=n * length * length
        ),
        name="attention_and_send",
    )(owner, x, bias)


def attention(owner, x, bias, slot):
    n, _, hd, length = x.shape
    four = 4
    return pl.pallas_call(
        functools.partial(attn_kernel, length // 2),
        grid_spec=pltpu.PrefetchScalarGridSpec(
            num_scalar_prefetch=1,
            grid=(n,),
            in_specs=[
                pl.BlockSpec((1, four, hd, length), lambda i, _: (i, slot, 0, 0)),
                pl.BlockSpec(bias.shape, lambda i, _: (0, 0, 0, 0)),
            ],
            out_specs=[
                pl.BlockSpec((1, four, hd, length), lambda i, _: (i, 0, 0, 0)),
                pl.BlockSpec(bias.shape, lambda i, _: (0, 0, 0, 0)),
            ],
            scratch_shapes=[pltpu.VMEM((2, length, length), f32)],
        ),
        out_shape=[jax.ShapeDtypeStruct((n, four, hd, length), bf16), jax.ShapeDtypeStruct(bias.shape, bf16)],
        compiler_params=params(),
        cost_estimate=pl.CostEstimate(
            flops=12 * n * length * length * 256, bytes_accessed=x.size * 2 + bias.size * 4, transcendentals=n * length * length
        ),
        name="attention",
    )(owner, x, bias)


def front_kernel(
    tok, cond, og, cgain, wc, cb, wq, qb, wo,
    *outs,
):
    x_o, sg_o, gg_o, s1_o, g1_o, first_o = outs
    width = tok.shape[-1]
    hd = width // head_count
    peers = x_o.shape[0]
    slots = head_count // peers
    cond_low = (norm_parts(cond[...].astype(f32))[0] * cgain[...]).astype(bf16)
    modul = dot(cond_low, wc[...]) + cb[...]
    s1 = jax.nn.sigmoid(modul[:, :width])
    g1 = jax.nn.sigmoid(modul[:, 2 * width :])
    tn, _ = norm_parts(tok[...].astype(f32))
    first = (s1 * tn + modul[:, width : 2 * width]).astype(bf16)
    proj = dot(first, wq[...])
    q = (proj[:, :width] + qb[...]) * (hd**-0.5 * log2e)
    sg = jax.nn.sigmoid(proj[:, 3 * width :])
    ga = (og[...].astype(f32) * g1).astype(bf16)
    gg = dot_nt(ga, wo[...])
    dm = sg * gg
    sg_o[...] = sg.astype(bf16)
    gg_o[...] = gg.astype(bf16)
    s1_o[...] = s1.astype(bf16)
    g1_o[...] = g1.astype(bf16)
    first_o[...] = first
    for i, part in enumerate((q, proj[:, width : 2 * width], proj[:, 2 * width : 3 * width], dm)):
        turned = part.T.astype(bf16).reshape(peers, slots, hd, part.shape[0])
        for t in range(slots):
            x_o[:, t * 4 + i] = turned[:, t]


def half_spec(a, h):
    return pl.BlockSpec((a.shape[0], a.shape[1] // 2), lambda *_: (0, h))


def row_spec(a, rb):
    return pl.BlockSpec((rb, a.shape[1]), lambda i, *_: (i, 0))


def front(tok, cond, og, cgain, wc, cb, wq, qb, wo, slots):
    length, width = tok.shape
    rb = 256
    peers, hd = head_count // slots, width // head_count
    small = jax.ShapeDtypeStruct((length, width), bf16)
    payload = jax.ShapeDtypeStruct((peers, 4 * slots, hd, length), bf16)
    return pl.pallas_call(
        front_kernel,
        grid_spec=pl.GridSpec(
            grid=(length // rb,),
            in_specs=[row_spec(tok, rb), row_spec(cond, rb), row_spec(og, rb)]
            + [whole(cgain)]
            + [half_spec(wc, 0)]
            + [whole(a) for a in (cb, wq, qb, wo)],
            out_specs=[pl.BlockSpec((peers, 4 * slots, hd, rb), lambda i: (0, 0, 0, i))] + [row_spec(tok, rb)] * 5,
        ),
        out_shape=[payload] + [small] * 5,
        compiler_params=params(),
        cost_estimate=pl.CostEstimate(flops=2 * length * width * width * 7, bytes_accessed=20 << 20, transcendentals=length * width * 4),
        name="front",
    )(tok, cond, og, cgain, wc, cb, wq, qb, wo)


def trans_kernel(
    tok, cond, og, cgain, wc, cb, wu, wd,
    part_o, u2_o, dcond_o, ml_o, cn_o, second_o, hid_o, act_o, gt_o, cbg_o,
):
    width = tok.shape[-1]
    cond_low = (norm_parts(cond[...].astype(f32))[0] * cgain[...]).astype(bf16)
    cn_o[...] = cond_low
    modul = dot(cond_low, wc[...]) + cb[...]
    s2 = jax.nn.sigmoid(modul[:, :width])
    g2 = jax.nn.sigmoid(modul[:, 2 * width :])
    tokens = tok[...].astype(f32)
    tn, _ = norm_parts(tokens)
    second = (s2 * tn + modul[:, width : 2 * width]).astype(bf16)
    second_o[...] = second
    hidden = dot(second, wu[...])
    ff = hidden.shape[1] // 2
    h_gate, h_up = hidden[:, :ff], hidden[:, ff:]
    sig = jax.nn.sigmoid(h_gate)
    silu = h_gate * sig
    act = (silu * h_up).astype(bf16)
    act_o[...] = act
    trans_out = dot(act, wd[...])
    part_o[...] = tokens + g2 * trans_out
    g = og[...].astype(f32)
    gt = (g * g2).astype(bf16)
    gt_o[...] = gt
    grad_act = dot_nt(gt, wd[...])
    hid = jnp.concatenate(
        [(grad_act * h_up * (sig * (1.0 + h_gate * (1.0 - sig)))).astype(bf16), (grad_act * silu).astype(bf16)], axis=-1
    )
    hid_o[...] = hid
    grad_second = dot_nt(hid, wu[...])
    u2_o[...] = (grad_second * s2).astype(bf16)
    grads = jnp.concatenate(
        [grad_second * tn * (s2 * (1.0 - s2)), grad_second, g * trans_out * (g2 * (1.0 - g2))], axis=-1
    )
    low = grads.astype(bf16)
    ml_o[...] = low

    @pl.when(pl.program_id(0) == 0)
    def _():
        cbg_o[...] = jnp.zeros_like(cbg_o)

    cbg_o[...] += jnp.sum(grads, axis=0, keepdims=True)
    dcond_o[...] = dot_nt(low, wc[...])


def transition(tok, cond, og, cgain, wc, cb, wu, wd):
    length, width = tok.shape
    rb = 256
    cs, mw = cond.shape[1], cb.shape[1]
    ff2 = wu.shape[1]

    def out(w, dtype):
        return jax.ShapeDtypeStruct((length, w), dtype)

    shapes = [
        out(width, f32), out(width, bf16), out(cs, f32), out(mw, bf16), out(cs, bf16), out(width, bf16),
        out(ff2, bf16), out(ff2 // 2, bf16), out(width, bf16),
    ]
    return pl.pallas_call(
        trans_kernel,
        grid_spec=pl.GridSpec(
            grid=(length // rb,),
            in_specs=[row_spec(tok, rb), row_spec(cond, rb), row_spec(og, rb)]
            + [whole(cgain)]
            + [half_spec(wc, 1)]
            + [whole(a) for a in (cb, wu, wd)],
            out_specs=[row_spec(s, rb) for s in shapes] + [pl.BlockSpec((1, mw), lambda i: (0, 0))],
        ),
        out_shape=shapes + [jax.ShapeDtypeStruct((1, mw), f32)],
        compiler_params=params(),
        cost_estimate=pl.CostEstimate(flops=2 * length * width * width * 15, bytes_accessed=40 << 20, transcendentals=length * width * 6),
        name="transition",
    )(tok, cond, og, cgain, wc, cb, wu, wd)


def back_kernel(slots, *refs):
    ys = refs[:slots]
    (
        sg, gg, s1, g1, part, u2, dcond2, tok, cond, og, cgain, wc, wq, wo,
        out_o, tg_o, cg_o, gated_o, ga_o, gp_o, ml_o, qbg_o, cbg_o, cgg_o,
    ) = refs[slots:]
    rb, width = tok.shape
    hd = width // head_count
    peers = head_count // slots

    def heads(i):
        stacked = jnp.stack([y[:, i] for y in ys], axis=1)
        return stacked.reshape(width, rb).astype(f32).T

    mixed = heads(0)
    sgv = sg[...].astype(f32)
    g1v = g1[...].astype(f32)
    gated = (sgv * mixed).astype(bf16)
    gated_o[...] = gated
    attn_out = dot(gated, wo[...])
    out_o[...] = part[...] + g1v * attn_out
    g = og[...].astype(f32)
    ga_o[...] = (g * g1v).astype(bf16)
    dg = gg[...].astype(f32) * mixed * (sgv * (1.0 - sgv))
    dq = heads(1)
    grad_proj = jnp.concatenate([dq.astype(bf16), heads(2).astype(bf16), heads(3).astype(bf16), dg.astype(bf16)], axis=-1)
    gp_o[...] = grad_proj
    grad_first = dot_nt(grad_proj, wq[...])
    s1v = s1[...].astype(f32)
    tn, tscale = norm_parts(tok[...].astype(f32))
    grads = jnp.concatenate(
        [grad_first * tn * (s1v * (1.0 - s1v)), grad_first, g * attn_out * (g1v * (1.0 - g1v))], axis=-1
    )
    low = grads.astype(bf16)
    ml_o[...] = low
    tg_o[...] = g + norm_back(tn, grad_first * s1v + u2[...].astype(f32), tscale)
    dcond = dot_nt(low, wc[...]) + dcond2[...]
    cx, cscale = norm_parts(cond[...].astype(f32))
    cg_o[...] = norm_back(cx, dcond * cgain[...], cscale)

    @pl.when(pl.program_id(0) == 0)
    def _():
        qbg_o[...] = jnp.zeros_like(qbg_o)
        cbg_o[...] = jnp.zeros_like(cbg_o)
        cgg_o[...] = jnp.zeros_like(cgg_o)

    qbg_o[...] += jnp.sum(dq, axis=0, keepdims=True)
    cbg_o[...] += jnp.sum(grads, axis=0, keepdims=True)
    cgg_o[...] += jnp.sum(dcond * cx, axis=0, keepdims=True)


def back(ys, sg, gg, s1, g1, part, u2, dcond2, tok, cond, og, cgain, wc, wq, wo):
    length, width = tok.shape
    rb = 256
    cs, mw = cond.shape[1], wc.shape[1] // 2
    rows = (sg, gg, s1, g1, part, u2, dcond2, tok, cond, og)
    consts = (wq, wo)

    def out(w, dtype):
        return jax.ShapeDtypeStruct((length, w), dtype)

    shapes = [
        out(width, f32), out(width, f32), out(cs, f32), out(width, bf16), out(width, bf16), out(wq.shape[1], bf16), out(mw, bf16),
    ]
    small = [jax.ShapeDtypeStruct((1, w), f32) for w in (width, mw, cs)]
    return pl.pallas_call(
        functools.partial(back_kernel, len(ys)),
        grid_spec=pl.GridSpec(
            grid=(length // rb,),
            in_specs=[pl.BlockSpec(y.shape[:3] + (rb,), lambda i: (0, 0, 0, i)) for y in ys]
            + [row_spec(a, rb) for a in rows]
            + [whole(cgain)]
            + [half_spec(wc, 0)]
            + [whole(a) for a in consts],
            out_specs=[row_spec(s, rb) for s in shapes] + [pl.BlockSpec(s.shape, lambda i: (0, 0)) for s in small],
        ),
        out_shape=shapes + small,
        compiler_params=params(),
        cost_estimate=pl.CostEstimate(flops=2 * length * width * width * 7, bytes_accessed=40 << 20, transcendentals=length * width),
        name="back",
    )(*ys, *rows, cgain, wc, *consts)


def wgrad_kernel(steps, lhs, *refs):
    *rhs, out_ref, turned = refs
    step = pl.program_id(0)

    @pl.when(step == 0)
    def _():
        turned[...] = lhs[...].T

    for k, r in enumerate(rhs):

        @pl.when(step // steps == k)
        def _():
            out_ref[...] = dot(turned[...], r[...]).astype(bf16).reshape(out_ref.shape)


def wgrad(lhs, *rhs):
    length, k = lhs.shape
    n = sum(r.shape[1] for r in rhs)
    row_groups = k // 96
    col_groups = 16 // row_groups
    piece = n // col_groups
    cols = piece if piece <= 1536 else piece // 2
    steps = n // cols
    each = steps // len(rhs)
    per = piece // cols

    def rhs_spec(t):
        return pl.BlockSpec((length, cols), lambda i: (0, jnp.clip(i - t * each, 0, each - 1)))

    return pl.pallas_call(
        functools.partial(wgrad_kernel, each),
        grid=(steps,),
        in_specs=[whole(lhs)] + [rhs_spec(t) for t in range(len(rhs))],
        out_specs=pl.BlockSpec((2, row_groups, 48, cols), lambda i: (0, i // per, 0, i % per)),
        out_shape=jax.ShapeDtypeStruct((2, 16, 48, piece), bf16),
        scratch_shapes=[pltpu.VMEM((k, length), bf16)],
        compiler_params=params(),
        cost_estimate=pl.CostEstimate(flops=2 * length * k * n, bytes_accessed=2 * (length * (k + n) + k * n), transcendentals=0),
        name="wgrad",
    )(lhs, *rhs)


def laid_out(pieces, rows):
    cols = pieces.shape[-1]
    row_groups = rows // 48
    blocks = pieces.reshape(16 // row_groups, rows, cols).astype(f32)
    return jnp.concatenate([blocks[t] for t in range(blocks.shape[0])], axis=1)


class Reducer:
    stages = 10

    def __init__(self, where, plan, ins, outs, xs, rs, load_sems, send_sems, recv_sems, keep_sems):
        self.where, self.plan, self.ins, self.outs, self.xs, self.rs = where, plan, ins, outs, xs, rs
        self.load_sems, self.send_sems, self.recv_sems, self.keep_sems = load_sems, send_sems, recv_sems, keep_sems
        n = len(plan)
        self.base, self.size, self.off, self.pending = [0] * n, [32] * n, [0] * n, [None] * n
        self.sends = []
        self.loads = [self.load(i) if ins else [] for i in range(n)]

    @staticmethod
    def scratch(plan):
        n = len(plan)
        return (
            [pltpu.VMEM((32, 48, w), bf16) for _, _, w, _, _ in plan]
            + [pltpu.VMEM((31, 48, w), bf16) for _, _, w, _, _ in plan]
            + [pltpu.SemaphoreType.DMA((n, 16))]
            + [pltpu.SemaphoreType.DMA((n, 9))] * 2
            + [pltpu.SemaphoreType.DMA((n,))]
        )

    def load(self, i):
        a, c0, w, order, _ = self.plan[i]
        at = SUM_ORDERS[order].index("y")
        run = 32 >> (at + 1)
        copies = []
        for b in range(1 << at):
            for f in range(2):
                copy = pltpu.make_async_copy(
                    self.ins[a].at[f, pl.ds(b * run, run), :, pl.ds(c0, w)],
                    self.xs[i].at[pl.ds((b * 2 + f) * run, run)],
                    self.load_sems.at[i, b * 2 + f],
                )
                copy.start()
                copies.append(copy)
        return copies

    def store(self, i, first_piece, rows):
        order = self.plan[i][3]
        low = 4 - SUM_ORDERS[order].index("y")
        row_groups = rows.shape[0] // 96
        for f in range(2):
            for g in range(row_groups):
                p = first_piece + g
                at = ((p >> low) * 2 + f) << low | p & ((1 << low) - 1)
                r0 = (f * row_groups + g) * 48
                self.xs[i][at] = rows[r0 : r0 + 48, :]

    def send(self, i, k, src, dst, name):
        copy = remote(src, dst, self.send_sems.at[i, k], self.recv_sems.at[i, k], across(self.where, name))
        self.sends.append(copy)
        self.pending[i] = copy

    def sum_start(self, i, k):
        name = SUM_ORDERS[self.plan[i][3]][k]
        half = self.size[i] // 2
        b = bit_of(self.where, name)
        src = self.xs[i].at[pl.ds(self.base[i] + (1 - b) * half, half)]
        self.send(i, k, src, self.rs[i].at[pl.ds(self.off[i], half)], name)
        self.base[i] = self.base[i] + b * half
        self.size[i] = half

    def sum_finish(self, i):
        self.pending[i].wait_recv()
        half, b0, r0 = self.size[i], self.base[i], self.off[i]
        x, r = self.xs[i], self.rs[i]

        def body(j, _):
            x[b0 + j] = (x[b0 + j].astype(f32) + r[r0 + j].astype(f32)).astype(bf16)
            return 0

        lax.fori_loop(0, half, body, 0)
        self.off[i] = r0 + half

    def block(self, i, done):
        a, c0, w, order, _ = self.plan[i]
        at = [
            slice(None) if name in done else bit_of(self.where, name) for name in SUM_ORDERS[order] if name != "y"
        ]
        return self.outs[a].at[(*at, slice(None), pl.ds(c0, w))]

    def copy_start(self, i, j):
        names = COPY_ORDERS[self.plan[i][4]]
        ref = self.block(i, names[:j])
        self.send(i, 5 + j, ref, ref, names[j])

    def advance(self, i, k):
        if k == 0:
            for copy in self.loads[i]:
                copy.wait()
            self.sum_start(i, 0)
        elif k < 5:
            self.sum_finish(i)
            self.sum_start(i, k)
        elif k == 5:
            self.sum_finish(i)
            keep = pltpu.make_async_copy(self.xs[i].at[self.base[i]], self.block(i, ()), self.keep_sems.at[i])
            keep.start()
            keep.wait()
            self.copy_start(i, 0)
        else:
            self.pending[i].wait_recv()
            if k < 9:
                self.copy_start(i, k - 5)

    def finish(self):
        for copy in self.sends:
            copy.wait_send()


class SmallSum:
    def __init__(self, where, buf, send_sems, recv_sems):
        self.where, self.buf, self.send_sems, self.recv_sems = where, buf, send_sems, recv_sems
        self.copies = []

    def advance(self, k):
        if k > 0:
            self.copies[k - 1].wait_recv()
            self.buf[2 * k] = self.buf[2 * k - 2] + self.buf[2 * k - 1]
        if k < 5:
            src, dst = self.buf.at[2 * k], self.buf.at[2 * k + 1]
            self.copies.append(
                remote(src, dst, self.send_sems.at[k], self.recv_sems.at[k], across(self.where, list(BITS)[k]))
            )


def reduce_kernel(n_left, *refs):
    refs = list(refs)

    def take(n):
        out, refs[:] = refs[:n], refs[n:]
        return out

    early_in, acts, (small, small_o) = take(2), take(7), take(2)
    late_out, early_out = take(3), take(2)
    n_late, n_early = len(late_plan), len(early_plan)
    late_scratch, early_scratch = take(2 * n_late + 4), take(2 * n_early + 4)
    bufs, (sbuf, s_send, s_recv, a_sems) = take(7), take(4)
    where = coords()
    loads = [pltpu.make_async_copy(src, dst, a_sems.at[i]) for i, (src, dst) in enumerate(zip(acts, bufs))]

    def reducer(plan, ins, outs, scratch):
        n = len(plan)
        return Reducer(where, plan, ins, outs, scratch[:n], scratch[n : 2 * n], *scratch[2 * n :])

    early = reducer(early_plan, early_in, early_out, early_scratch)
    for copy in loads:
        copy.start()
    late = reducer(late_plan, None, late_out, late_scratch)
    sbuf[0] = small[...]
    greet([across(where, name) for name in BITS])
    small_sum = SmallSum(where, sbuf, s_send, s_recv)
    small_sum.advance(0)
    for i in range(n_early):
        early.advance(i, 0)

    first, gp, cn, ml1, ml2, gated, ga = bufs
    sides = ((first, (gp,)), (cn, (ml1, ml2)), (gated, (ga,)))
    turned = {}
    waited = set()

    def ready(k):
        if k not in waited:
            loads[k].wait()
            waited.add(k)

    for i, (a, c0, w, _, _) in enumerate(late_plan):
        lhs, rhs = sides[a]
        k0 = (0, 2, 5)[a]
        for k in range(k0, k0 + 1 + len(rhs)):
            ready(k)
        if a not in turned:
            turned[a] = lhs[...].T
        row_groups = turned[a].shape[0] // 96
        total = sum(r.shape[1] for r in rhs)
        piece = total * row_groups // 16
        for g in range(16 // row_groups):
            c = g * piece
            r = rhs[c // rhs[0].shape[1]]
            c = c % rhs[0].shape[1] + c0
            late.store(i, g * row_groups, dot(turned[a], r[:, c : c + w]).astype(bf16))
        late.advance(i, 0)
        if i in (1, 4):
            for e in range(n_early):
                early.advance(e, 1 + i // 4)
    for k in range(1, Reducer.stages):
        for i in range(n_late):
            late.advance(i, k)
        if k + 2 < Reducer.stages:
            for i in range(n_early):
                early.advance(i, k + 2)
        if k < 6:
            small_sum.advance(k)
    small_o[...] = sbuf[10]
    for copy in late.sends + early.sends + small_sum.copies:
        copy.wait_send()


def reduce_all(early, acts, small):
    widths = (1536, 1152, 384, 1536, 768)
    shapes = [jax.ShapeDtypeStruct((2, 2, 2, 2, 48, w), bf16) for w in widths]
    any_spec = pl.BlockSpec(memory_space=pl.ANY)
    vm = pl.BlockSpec(memory_space=pltpu.VMEM)
    return pl.pallas_call(
        functools.partial(reduce_kernel, None),
        out_shape=[jax.ShapeDtypeStruct(small.shape, f32)] + shapes,
        in_specs=[any_spec] * (len(early) + len(acts)) + [vm],
        out_specs=[vm] + [any_spec] * len(shapes),
        scratch_shapes=Reducer.scratch(late_plan)
        + Reducer.scratch(early_plan)
        + [pltpu.VMEM(a.shape, bf16) for a in acts]
        + [
            pltpu.VMEM((11,) + small.shape, f32),
            pltpu.SemaphoreType.DMA((5,)),
            pltpu.SemaphoreType.DMA((5,)),
            pltpu.SemaphoreType.DMA((len(acts),)),
        ],
        compiler_params=params(collective_id=1, has_side_effects=True),
        name="reduce_grads",
    )(*early, *acts, small)


def small_kernel(x, out, buf, send_sems, recv_sems):
    where = coords()
    buf[0] = x[...]
    greet([across(where, name) for name in BITS])
    total = SmallSum(where, buf, send_sems, recv_sems)
    for k in range(6):
        total.advance(k)
    out[...] = buf[10]
    for copy in total.copies:
        copy.wait_send()


def small_sum(x):
    return pl.pallas_call(
        small_kernel,
        out_shape=jax.ShapeDtypeStruct(x.shape, f32),
        in_specs=[pl.BlockSpec(memory_space=pltpu.VMEM)],
        out_specs=pl.BlockSpec(memory_space=pltpu.VMEM),
        scratch_shapes=[
            pltpu.VMEM((11,) + x.shape, f32),
            pltpu.SemaphoreType.DMA((5,)),
            pltpu.SemaphoreType.DMA((5,)),
        ],
        compiler_params=params(collective_id=5, has_side_effects=True),
        name="small_sum",
    )(x)


late_plan = (
    (0, 0, 1024, 0, 0),
    (0, 1024, 512, 1, 1),
    (1, 0, 512, 1, 1),
    (1, 512, 640, 2, 0),
    (2, 0, 384, 2, 1),
)
early_plan = ((0, 0, 768, 0, 0), (0, 768, 768, 1, 1), (1, 0, 768, 2, 0))


def on_device(
    tokens, cond, pair, counts, owner, out_grad, cond_gain, cond_weight, cond_bias, qkvg_weight, query_bias,
    out_weight, pair_gain, pair_weight, up_weight, down_weight,
):
    ups, los, ffs = lax.axis_size("up"), lax.axis_size("lo"), lax.axis_size("fsdp")
    plane = ("lo", "fsdp")
    members = los * ffs
    slots = head_count // members
    length, width = tokens.shape[1:]
    rows = pair.shape[1]
    direct = ffs == 2 and los == 4 and ups == 4

    wide = 3 * width

    def spread(got):
        mine = got.reshape(members, 2, rows, length).transpose(1, 0, 2, 3).reshape(2, members * rows, length)
        return lax.all_gather(mine, "up", axis=0, tiled=False)

    matrices = (cond_weight, qkvg_weight, out_weight, up_weight, down_weight)
    if direct:
        wc, wq, wo, wu, wd, spreads = start(
            counts, pair, big_weights(pair_weight), jnp.tile(pair_gain, 2)[None], matrices
        )
    else:
        bias = pair_fwd(counts, pair, pair_weight.T, pair_gain[None])
        bias = bias.reshape(members, slots, 2 * rows, length)
        spreads = lax.all_to_all(bias, plane, 0, 0, tiled=True)
        wc, wq, wo, wu, wd = [lax.all_gather(w, "fsdp", axis=0, tiled=True) for w in matrices]
    biases = [spread(spreads[:, t]) for t in range(slots)]

    tok, cnd, og = tokens[0], cond[0], out_grad[0]
    cgain = cond_gain[None]
    x, sg, gg, s1, g1, first = front(
        tok, cnd, og, cgain, wc, cond_bias[None, :wide], wq, query_bias[None], wo, slots
    )
    x = lax.all_to_all(x, plane, 0, 0, tiled=True)
    part, u2, dcond2, ml2, cn, second, hid, act, gt, cbg2 = transition(
        tok, cnd, og, cgain, wc, cond_bias[None, wide:], wu, wd
    )
    def fold(g):
        k, n = g.shape
        if k == width:
            return g
        if k > width:
            times = k // width
            parts = g.reshape(ffs, times, width // ffs, n)
            return jnp.concatenate([parts[:, t] for t in range(times)], axis=-1).reshape(width, n * times)
        times = width // k
        parts = g.reshape(ffs, k // ffs, times, n // times)
        return jnp.concatenate([parts[:, :, t] for t in range(times)], axis=1).reshape(width, n // times)

    def unfold(h, k, n):
        rows_each = width // ffs
        if k == width:
            return h
        if k > width:
            times = k // width
            return jnp.concatenate([h[:, t * n : (t + 1) * n] for t in range(times)], axis=0)
        times = width // k
        step = rows_each // times
        return jnp.concatenate([h[t * step : (t + 1) * step] for t in range(times)], axis=1)

    def reduced(grads):
        folded = [fold(g) for g in grads]
        mine = lax.psum_scatter(
            jnp.concatenate(folded, axis=1), ("fsdp", "up", "lo"), scatter_dimension=0, tiled=True
        )
        full = lax.all_gather(mine, ("up", "lo"), axis=0, tiled=True)
        outs, at = [], 0
        for g, h in zip(grads, folded):
            outs.append(unfold(full[:, at : at + h.shape[1]], *g.shape).astype(f32))
            at += h.shape[1]
        return outs

    if direct:
        early = [wgrad(second, hid), wgrad(act, gt)]
        x, *early = lax.optimization_barrier((x, *early))
    else:
        up_total, down_total = reduced([dot_tn(second, hid).astype(bf16), dot_tn(act, gt).astype(bf16)])

    owners = lax.dynamic_slice_in_dim(owner, lax.axis_index("up") * members, members)
    ys, bias_grads = [], []
    for t in range(slots):
        if direct:
            y, bg = sending_attention(owners, x, biases[t], t)
        else:
            y, bg = attention(owners, x, biases[t], t)
            y = lax.all_to_all(y, plane, 0, 0, tiled=True)
        ys.append(y)
        mine = lax.psum_scatter(bg, "up", scatter_dimension=0, tiled=True)
        bias_grads.append(mine.reshape(2, members, rows, length).transpose(1, 0, 2, 3))

    block_out, tokens_grad, cond_grad, gated, ga, gp, ml1, qbg, cbg1, cgg = back(
        ys, sg, gg, s1, g1, part, u2, dcond2, tok, cnd, og, cgain, wc, wq, wo
    )
    if not direct:
        ml = jnp.concatenate([ml1, ml2], axis=1)
        qkvg_total, out_total, cond_total = reduced(
            [dot_tn(first, gp).astype(bf16), dot_tn(gated, ga).astype(bf16), dot_tn(cn, ml).astype(bf16)]
        )

    pieces = [cgg, cbg1, cbg2, qbg]
    stacked = jnp.concatenate([p.reshape(-1, 128) for p in pieces], axis=0)
    if direct:
        height = -(-stacked.shape[0] // 8) * 8
        stacked = jnp.pad(stacked, ((0, height - stacked.shape[0]), (0, 0)))
        stacked, *totals = reduce_all(early, (first, gp, cn, ml1, ml2, gated, ga), stacked)
        *bias_grads, stacked = lax.optimization_barrier((*bias_grads, stacked))
        qkvg_total, cond_total, out_total, up_total, down_total = [
            laid_out(p, w.shape[0]) for p, w in zip(totals, (qkvg_weight, cond_weight, out_weight, up_weight, down_weight))
        ]
    else:
        stacked = lax.psum(stacked, ("up", "lo", "fsdp"))
    bias_grad = lax.all_to_all(jnp.stack(bias_grads, axis=1), plane, 0, 0, tiled=True)
    bias_grad = bias_grad.reshape(head_count, 2, rows, length)
    pw = pair_weight.astype(f32).T
    scaled = pw * pair_gain
    centered = scaled - jnp.mean(scaled, axis=-1, keepdims=True)
    high = centered.astype(bf16)
    low = (centered - high.astype(f32)).astype(bf16)
    pair_grad, moments = pair_bwd(pair, bias_grad, high, low)
    moments = small_sum(moments) if direct else lax.psum(moments, ("up", "lo", "fsdp"))
    small = stacked.reshape(-1)
    ends = [0]
    for p in pieces:
        ends.append(ends[-1] + p.size)
    small = [small[a:b] for a, b in zip(ends[:-1], ends[1:])]
    return (
        block_out[None],
        tokens_grad[None],
        cond_grad[None],
        pair_grad,
        small[0],
        cond_total,
        jnp.concatenate([small[1], small[2]]),
        qkvg_total,
        small[3],
        out_total,
        jnp.sum(pw * moments, axis=0),
        (moments * pair_gain).T,
        up_total,
        down_total,
    )


def solution(mesh):
    dp, fsdp = mesh.shape["dp"], mesh.shape["fsdp"]
    lo = max(1, group_size // fsdp)
    fine = Mesh(mesh.devices.reshape(dp // lo, lo, fsdp), ("up", "lo", "fsdp"))
    every = ("up", "lo", "fsdp")
    in_specs = (
        P(every, None, None),
        P(every, None, None),
        P(None, every, None, None),
        P(),
        P(),
        P(every, None, None),
        P(),
        P("fsdp", None),
        P(),
        P("fsdp", None),
        P(),
        P("fsdp", None),
        P(),
        P(),
        P("fsdp", None),
        P("fsdp", None),
    )
    out_specs = (
        P(every, None, None),
        P(every, None, None),
        P(every, None, None),
        P(None, every, None, None),
        P(),
        P("fsdp", None),
        P(),
        P("fsdp", None),
        P(),
        P("fsdp", None),
        P(),
        P(),
        P("fsdp", None),
        P("fsdp", None),
    )
    return jax.shard_map(on_device, mesh=fine, in_specs=in_specs, out_specs=out_specs, check_vma=False)
```

```python
import functools

import jax
import jax.numpy as jnp
from jax import lax
from jax.experimental import pallas as pl
from jax.experimental.pallas import tpu as pltpu
from jax.sharding import Mesh, PartitionSpec as P

f32, bf16 = jnp.float32, jnp.bfloat16
norm_eps = 1e-05
mask_fill = -1000000000.0
log2e = 1.4426950408889634
ln2 = 0.6931471805599453
head_count = 16
group_size = 8
vmem_bytes = 58 << 20
nt_dims = (((1,), (1,)), ((), ()))


def dot(a, b):
    return jnp.dot(a, b, preferred_element_type=f32)


def dot_nt(a, b):
    return lax.dot_general(a, b, nt_dims, preferred_element_type=f32)


def dot_tn(a, b):
    return lax.dot_general(a, b, (((0,), (0,)), ((), ())), preferred_element_type=f32)


def norm_parts(values):
    centered = values - jnp.mean(values, axis=-1, keepdims=True)
    variance = jnp.mean(centered * centered, axis=-1, keepdims=True)
    scale = lax.rsqrt(variance + norm_eps)
    return centered * scale, scale


def norm_back(x, u, scale):
    mean_u = jnp.mean(u, axis=-1, keepdims=True)
    mean_ux = jnp.mean(u * x, axis=-1, keepdims=True)
    return (u - mean_u - x * mean_ux) * scale


def params(**kw):
    return pltpu.CompilerParams(vmem_limit_bytes=vmem_bytes, **kw)


def whole(a):
    zero = (0,) * a.ndim
    return pl.BlockSpec(a.shape, lambda *_: zero)


MESH = pl.DeviceIdType.MESH
BITS = {"c": ("lo", 1), "x": ("lo", 2), "y": ("fsdp", 1), "z0": ("up", 1), "z1": ("up", 2)}
PEERS = (("c",), ("x",), ("y",), ("c", "x"), ("c", "y"), ("x", "y"), ("c", "x", "y"))
SAMPLE_ORDER = (("x",), ("y",), ("x", "y"), ("c", "x"), ("c", "y"), ("c", "x", "y"), ("c",), ())
SUM_ORDERS = (
    ("c", "x", "y", "z0", "z1"),
    ("c", "x", "z0", "y", "z1"),
    ("c", "y", "x", "z0", "z1"),
    ("c", "z0", "y", "z1", "x"),
)
COPY_ORDERS = (
    ("x", "z0", "z1", "c"),
    ("z0", "z1", "x", "c"),
    ("z1", "x", "z0", "c"),
    ("z1", "z0", "x", "c"),
)


def coords():
    return {a: lax.axis_index(a) for a in ("up", "lo", "fsdp")}


def bit_of(where, name):
    axis, value = BITS[name]
    return lax.rem(where[axis] // value, 2)


def across(where, *names):
    other = dict(where)
    for name in names:
        axis, value = BITS[name]
        other[axis] = other[axis] + value * (1 - 2 * bit_of(where, name))
    return other


def device(where):
    return (where["up"], where["lo"], where["fsdp"])


def place(where):
    return where["lo"] * 2 + where["fsdp"]


def greet(devices):
    barrier = pltpu.get_barrier_semaphore()
    for other in devices:
        pl.semaphore_signal(barrier, inc=1, device_id=device(other), device_id_type=MESH)
    pl.semaphore_wait(barrier, len(devices))


def remote(src, dst, send_sem, recv_sem, other):
    copy = pltpu.make_async_remote_copy(
        src_ref=src, dst_ref=dst, send_sem=send_sem, recv_sem=recv_sem, device_id=device(other), device_id_type=MESH
    )
    copy.start()
    return copy


def lane_means(values):
    total = values.shape[-1]
    group = lax.broadcasted_iota(jnp.int32, (total, total), 0) // 128 == lax.broadcasted_iota(jnp.int32, (total, total), 1) // 128
    return dot(values, jnp.where(group, 1.0 / 128, 0.0).astype(bf16))


def pair_norm(*blocks):
    x = jnp.concatenate(blocks, axis=-1)
    centered = x.astype(f32) - lane_means(x)
    variance = lane_means((centered * centered).astype(bf16))
    scale = lax.rsqrt(variance + norm_eps)
    return centered * scale, scale


def pair_fwd_kernel(rows, counts_ref, x_ref, pw_ref, gain_ref, out_ref, scr_ref):
    step = pl.program_id(0)
    steps_each = pl.num_programs(0) // 2
    limit = counts_ref[step // steps_each]
    heads, length = scr_ref.shape[0], scr_ref.shape[2]
    valid = lax.broadcasted_iota(jnp.int32, (heads, length), 1) < limit
    pw = pw_ref[...]
    gain = gain_ref[...]
    for r in range(rows):
        low = (pair_norm(x_ref[0, r])[0] * gain).astype(bf16)
        bias = dot_nt(pw, low)
        scr_ref[:, r, :] = jnp.where(valid, bias * log2e, mask_fill)
    out_ref[:, 0] = scr_ref[...].astype(bf16)


def pair_fwd(counts, pair, pw_t, gain):
    _, total, length, width = pair.shape
    rows = 8 if total % 8 == 0 else total
    steps = total // rows
    heads = pw_t.shape[0]
    return pl.pallas_call(
        functools.partial(pair_fwd_kernel, rows),
        grid_spec=pltpu.PrefetchScalarGridSpec(
            num_scalar_prefetch=1,
            grid=(2 * steps,),
            in_specs=[
                pl.BlockSpec((1, rows, length, width), lambda i, _: (i // steps, i % steps, 0, 0)),
                whole(pw_t),
                whole(gain),
            ],
            out_specs=pl.BlockSpec((heads, 1, rows, length), lambda i, _: (0, i // steps, i % steps, 0)),
            scratch_shapes=[pltpu.VMEM((heads, rows, length), f32)],
        ),
        out_shape=jax.ShapeDtypeStruct((heads, 2, total, length), bf16),
        compiler_params=params(),
        cost_estimate=pl.CostEstimate(flops=2 * pair.size * 300, bytes_accessed=pair.size * 2, transcendentals=pair.size),
        name="pair_fwd",
    )(counts, pair, pw_t, gain)


def pair_bwd_kernel(rows, x_ref, bg_ref, a_ref, out_ref, *sums):
    if sums:
        q_ref, low_buf = sums

        @pl.when(pl.program_id(0) == 0)
        def _():
            q_ref[...] = jnp.zeros_like(q_ref)

    width = out_ref.shape[-1]
    heads, _, _, length = bg_ref.shape
    grads = bg_ref[:, 0].astype(f32).reshape(heads * rows, length)
    turned = grads.T.astype(bf16)
    u_all = dot(jnp.concatenate([turned, turned], axis=1), a_ref[...])
    step = 2 - rows % 2
    for r in range(0, rows, step):
        x_hat, scale = pair_norm(*(x_ref[0, r + t] for t in range(step)))
        if sums:
            low_buf[:, r * width : (r + step) * width] = x_hat.astype(bf16)
        u = u_all[:, r * width : (r + step) * width]
        grad = (u - x_hat * lane_means((u * x_hat).astype(bf16))) * scale
        for t in range(step):
            out_ref[0, r + t] = grad[:, t * width : (t + 1) * width]
    if sums:
        q_ref[...] += dot(grads.astype(bf16), low_buf[...])


def pair_bwd(pair, bias_grad, high, low, with_sums):
    _, total, length, width = pair.shape
    rows = 8 if total % 8 == 0 else total
    steps = total // rows
    heads = bias_grad.shape[0]
    eye = jnp.eye(rows, dtype=bf16)
    both = jnp.stack([high, low])
    weights = (both[:, :, None, None, :] * eye[None, None, :, :, None]).reshape(2 * heads * rows, rows * width)
    grad, *moments = pl.pallas_call(
        functools.partial(pair_bwd_kernel, rows),
        grid=(2 * steps,),
        in_specs=[
            pl.BlockSpec((1, rows, length, width), lambda i: (i // steps, i % steps, 0, 0)),
            pl.BlockSpec((heads, 1, rows, length), lambda i: (0, i // steps, i % steps, 0)),
            whole(weights),
        ],
        out_specs=[
            pl.BlockSpec((1, rows, length, width), lambda i: (i // steps, i % steps, 0, 0)),
            pl.BlockSpec((heads * rows, rows * width), lambda i: (0, 0)),
        ][: 1 + with_sums],
        out_shape=[
            jax.ShapeDtypeStruct(pair.shape, f32),
            jax.ShapeDtypeStruct((heads * rows, rows * width), f32),
        ][: 1 + with_sums],
        scratch_shapes=[pltpu.VMEM((length, rows * width), bf16)][:with_sums],
        compiler_params=params(),
        cost_estimate=pl.CostEstimate(flops=2 * pair.size * 500, bytes_accessed=pair.size * 6, transcendentals=pair.size),
        name="pair_bwd",
    )(pair, bias_grad, weights)
    if not moments:
        return grad, None
    moments = moments[0].reshape(heads, rows, rows, width)
    return grad, sum(moments[:, r, r] for r in range(rows))


class Mover:
    def __init__(self, where, order, own, full, stage, send, recv, keep):
        self.where, self.order, self.own, self.full, self.send, self.recv = where, order, own, full, send, recv
        self.half = own.shape[0]
        self.piece = self.half >> len(order)
        self.mine = sum(bit_of(where, name) << j for j, name in enumerate(order))
        self.copies = []
        self.kept = [
            pltpu.make_async_copy(own, stage, keep.at[0]),
            pltpu.make_async_copy(stage, full.at[pl.ds(where["fsdp"] * self.half, self.half)], keep.at[1]),
        ]

    def stage(self, k):
        if k:
            self.kept[k - 1].wait()
        if k < 2:
            self.kept[k].start()

    def advance(self, k):
        if k:
            self.copies[k - 1].wait_recv()
        if k == 0:
            name, src_at = "y", self.mine * self.piece
            at, size = self.where["fsdp"] * self.half + src_at, self.piece
            src = self.own.at[pl.ds(src_at, size)]
        elif k <= len(self.order):
            name, size = self.order[k - 1], self.piece << (k - 1)
            at = (1 - self.where["fsdp"]) * self.half + self.mine * self.piece // size * size
            src = self.full.at[pl.ds(at, size)]
        else:
            return
        dst = self.full.at[pl.ds(at, size)]
        self.copies.append(remote(src, dst, self.send.at[k], self.recv.at[k], across(self.where, name)))

    def finish(self):
        self.stage(2)
        for copy in self.copies:
            copy.wait_send()


MOVES = (("x", "c"), ("x", "z0", "c"), ("x", "z0", "c"), ("z0", "x", "c"), ("x", "z0", "c"))


def start_kernel(n_w, counts, pw, gain, pair, *refs):
    owns, others, spread = refs[:n_w], refs[n_w : 2 * n_w], refs[2 * n_w]
    *stages, x_buf, low_buf, bias_f, bias_v, x_sems, w_send, w_recv, w_keep, b_send, b_recv, b_sem = refs[2 * n_w + 1 :]
    where = coords()
    peers = [across(where, *names) for names in PEERS]
    total = pair.shape[1]
    length, width = pair.shape[2:]
    heads = bias_f.shape[0]
    groups = 2 * total // 8

    def fetch(g, slot):
        return pltpu.make_async_copy(
            pair.at[(g * 8) // total, pl.ds(lax.rem(g * 8, total), 8)], x_buf.at[slot], x_sems.at[slot]
        )

    fetch(0, 0).start()
    greet(peers + [across(where, "z0")])
    movers = [Mover(where, MOVES[i], owns[i], others[i], stages[i], w_send.at[i], w_recv.at[i], w_keep.at[i]) for i in range(n_w)]
    for m in movers:
        m.advance(0)
    for m in movers:
        m.stage(0)

    def group(g, _):
        slot = lax.rem(g, 2)

        @pl.when(g + 1 < groups)
        def _():
            fetch(g + 1, 1 - slot).start()

        fetch(g, slot).wait()
        for r in range(0, 8, 2):
            x_hat, _ = pair_norm(x_buf[slot, r], x_buf[slot, r + 1])
            low_buf[:, r * width : (r + 2) * width] = (x_hat * gain[...]).astype(bf16)
        bias = dot(low_buf[...], pw[...]).T
        limit = counts[(g * 8) // total]
        valid = lax.broadcasted_iota(jnp.int32, bias.shape, 1) < limit
        bias = jnp.where(valid, bias * log2e, mask_fill)
        bias_f[:, pl.ds(pl.multiple_of(g * 8, 8), 8), :] = bias.reshape(heads, 8, length)
        return 0

    third = groups // 3
    for k in range(3):
        lax.fori_loop(k * third, (k + 1) * third, group, 0)
        movers[k].advance(1)
    for m in movers:
        m.stage(1)
    bias_v[...] = bias_f[...].astype(bf16).reshape(bias_v.shape)

    keep = pltpu.make_async_copy(bias_v.at[place(where)], spread.at[place(where)], b_sem)
    keep.start()
    sent = []

    def send_bias():
        for k, peer in enumerate(peers):
            sent.append(remote(bias_v.at[place(peer)], spread.at[place(where)], b_send.at[k], b_recv.at[k], peer))

    for m in movers[3:]:
        m.advance(1)
    send_bias()
    for k in range(2, 5):
        for m in movers:
            if k <= len(m.order) + 1:
                m.advance(k)
    keep.wait()
    for copy in sent:
        copy.wait()
    for m in movers:
        m.finish()


def start(counts, pair, pw_big, gain, owns):
    heads, length, width = 16, pair.shape[2], pair.shape[3]
    rows = 2 * pair.shape[1]
    n = len(owns)
    any_spec = pl.BlockSpec(memory_space=pl.ANY)
    vm = pl.BlockSpec(memory_space=pltpu.VMEM)
    return pl.pallas_call(
        functools.partial(start_kernel, n),
        in_specs=[pl.BlockSpec(memory_space=pltpu.SMEM), vm, vm, any_spec] + [any_spec] * n,
        out_specs=[any_spec] * (n + 1),
        out_shape=[jax.ShapeDtypeStruct((2 * w.shape[0], w.shape[1]), bf16) for w in owns]
        + [jax.ShapeDtypeStruct((8, heads // 8, rows, length), bf16)],
        scratch_shapes=[pltpu.VMEM(w.shape, bf16) for w in owns]
        + [
            pltpu.VMEM((2, 8, length, width), bf16),
            pltpu.VMEM((length, 8 * width), bf16),
            pltpu.VMEM((heads, rows, length), f32),
            pltpu.VMEM((8, heads // 8, rows, length), bf16),
            pltpu.SemaphoreType.DMA((2,)),
            pltpu.SemaphoreType.DMA((n, 4)),
            pltpu.SemaphoreType.DMA((n, 4)),
            pltpu.SemaphoreType.DMA((n, 2)),
            pltpu.SemaphoreType.DMA((7,)),
            pltpu.SemaphoreType.DMA((7,)),
            pltpu.SemaphoreType.DMA,
        ],
        compiler_params=pltpu.CompilerParams(vmem_limit_bytes=vmem_bytes, collective_id=2, has_side_effects=True),
        name="start",
    )(counts, pw_big, gain, pair, *owns)


def big_weights(pw):
    width, heads = pw.shape
    eye = jnp.eye(8, dtype=pw.dtype)
    return (eye[:, None, None, :] * pw[None, :, :, None]).reshape(8 * width, heads * 8)


def attend(rb, c, x_ref, y_ref, bias_ref, add):
    length, hd = x_ref.shape[-1], x_ref.shape[-2]
    bz = bias_ref.shape[2]
    k_t, v_t = x_ref[1], x_ref[2]
    v_ext = jnp.concatenate([v_t, jnp.ones((16, length), bf16)], axis=0)
    dv = dk = 0.0
    for r in range(length // rb):
        sl = slice(r * rb, (r + 1) * rb)
        q_t = x_ref[0, :, sl]
        q = q_t.T
        dm = x_ref[3, :, sl].astype(f32).T
        z0 = r * rb // bz
        bias = jnp.concatenate([bias_ref[z0 + t, c].astype(f32) for t in range(rb // bz)], axis=0)
        s = dot(q, k_t) + bias
        e = jnp.exp2(s - jnp.max(s, axis=-1, keepdims=True))
        eb = e.astype(bf16)
        mx = dot_nt(eb, v_ext)
        inv = 1.0 / mx[:, hd : hd + 1]
        mixed = mx[:, :hd] * inv
        d = jnp.sum(mixed * dm, axis=-1, keepdims=True) * inv
        dms = (dm * inv).astype(bf16)
        ds = e * (dot(dms, v_t) - d)
        dsb = ds.astype(bf16)
        add(sl, ds)
        dq = dot_nt(dsb, k_t)
        dv = dv + dot(dms.T, eb)
        dk = dk + dot(q_t, dsb)
        y_ref[0, :, sl] = mixed.T.astype(bf16)
        y_ref[1, :, sl] = (dq * hd**-0.5).T.astype(bf16)
    y_ref[2] = (dk * ln2).astype(bf16)
    y_ref[3] = dv.astype(bf16)


def attn_kernel(rb, owner_ref, x_ref, bias_ref, y_ref, bg_ref, acc_ref):
    n = pl.program_id(0)
    c = owner_ref[n]
    up, bz = bias_ref.shape[0], bias_ref.shape[2]

    @pl.when(n == 0)
    def _():
        acc_ref[...] = jnp.zeros_like(acc_ref)

    def add(sl, ds):
        acc_ref[c, sl, :] += ds

    attend(rb, c, x_ref.at[0], y_ref.at[0], bias_ref, add)

    @pl.when(n == pl.num_programs(0) - 1)
    def _():
        for z in range(up):
            for cc in range(2):
                bg_ref[z, cc] = acc_ref[cc, z * bz : (z + 1) * bz, :].astype(bf16)


def sending_attn_kernel(
    rb, slot, owner_ref, x_ref, bias_ref, y_ref, bg_ref, both, second, x_buf, y_buf, x_sems, y_send, y_recv, y_keep
):
    step = pl.program_id(0)
    steps = pl.num_programs(0)
    where = coords()
    up, bz = bias_ref.shape[0], bias_ref.shape[2]

    def partner(k):
        other = dict(where)
        for name in ("c", "x", "y"):
            axis, value = BITS[name]
            flip = sum(jnp.where(k == i, 1, 0) for i, names in enumerate(SAMPLE_ORDER) if name in names)
            other[axis] = other[axis] + flip * value * (1 - 2 * bit_of(where, name))
        return other

    def fetch(k):
        return pltpu.make_async_copy(
            x_ref.at[place(partner(k)), pl.ds(slot * 4, 4)], x_buf.at[lax.rem(k, 2)], x_sems.at[lax.rem(k, 2)]
        )

    def sent(k, to):
        return pltpu.make_async_remote_copy(
            src_ref=y_buf.at[k],
            dst_ref=y_ref.at[place(to)],
            send_sem=y_send.at[k],
            recv_sem=y_recv.at[k],
            device_id=device(partner(k)),
            device_id_type=MESH,
        )

    keep = pltpu.make_async_copy(y_buf.at[len(PEERS)], y_ref.at[place(where)], y_keep)

    @pl.when(step == 0)
    def _():
        fetch(0).start()
        both[...] = jnp.zeros_like(both)
        second[...] = jnp.zeros_like(second)
        greet([across(where, *names) for names in PEERS])

    @pl.when(step + 1 < steps)
    def _():
        fetch(step + 1).start()

    fetch(step).wait()
    c = owner_ref[place(partner(step))]
    weight = c.astype(f32)

    def add(sl, ds):
        both[sl, :] += ds
        second[sl, :] += ds * weight

    attend(rb, c, x_buf.at[lax.rem(step, 2)], y_buf.at[step], bias_ref, add)

    @pl.when(step < steps - 1)
    def _():
        sent(step, where).start()

    @pl.when(step == steps - 1)
    def _():
        keep.start()
        for z in range(up):
            sl = slice(z * bz, (z + 1) * bz)
            bg_ref[z, 0] = (both[sl, :] - second[sl, :]).astype(bf16)
            bg_ref[z, 1] = second[sl, :].astype(bf16)
        keep.wait()
        for k in range(len(PEERS)):
            sent(k, partner(k)).wait_recv()
            sent(k, where).wait_send()


def sending_attention(owner, x, bias, slot):
    n, _, hd, length = x.shape
    any_spec = pl.BlockSpec(memory_space=pl.ANY)
    vm = pl.BlockSpec(memory_space=pltpu.VMEM)
    return pl.pallas_call(
        functools.partial(sending_attn_kernel, length // 2, slot),
        grid=(n,),
        in_specs=[pl.BlockSpec(memory_space=pltpu.SMEM), any_spec, vm],
        out_specs=[any_spec, vm],
        out_shape=[jax.ShapeDtypeStruct((n, 4, hd, length), bf16), jax.ShapeDtypeStruct(bias.shape, bf16)],
        scratch_shapes=[
            pltpu.VMEM((length, length), f32),
            pltpu.VMEM((length, length), f32),
            pltpu.VMEM((2, 4, hd, length), bf16),
            pltpu.VMEM((n, 4, hd, length), bf16),
            pltpu.SemaphoreType.DMA((2,)),
            pltpu.SemaphoreType.DMA((n,)),
            pltpu.SemaphoreType.DMA((n,)),
            pltpu.SemaphoreType.DMA,
        ],
        compiler_params=params(collective_id=3 + slot, has_side_effects=True),
        cost_estimate=pl.CostEstimate(
            flops=12 * n * length * length * 256, bytes_accessed=x.size * 2 + bias.size * 4, transcendentals=n * length * length
        ),
        name="attention_and_send",
    )(owner, x, bias)


def attention(owner, x, bias, slot):
    n, _, hd, length = x.shape
    four = 4
    return pl.pallas_call(
        functools.partial(attn_kernel, length // 2),
        grid_spec=pltpu.PrefetchScalarGridSpec(
            num_scalar_prefetch=1,
            grid=(n,),
            in_specs=[
                pl.BlockSpec((1, four, hd, length), lambda i, _: (i, slot, 0, 0)),
                pl.BlockSpec(bias.shape, lambda i, _: (0, 0, 0, 0)),
            ],
            out_specs=[
                pl.BlockSpec((1, four, hd, length), lambda i, _: (i, 0, 0, 0)),
                pl.BlockSpec(bias.shape, lambda i, _: (0, 0, 0, 0)),
            ],
            scratch_shapes=[pltpu.VMEM((2, length, length), f32)],
        ),
        out_shape=[jax.ShapeDtypeStruct((n, four, hd, length), bf16), jax.ShapeDtypeStruct(bias.shape, bf16)],
        compiler_params=params(),
        cost_estimate=pl.CostEstimate(
            flops=12 * n * length * length * 256, bytes_accessed=x.size * 2 + bias.size * 4, transcendentals=n * length * length
        ),
        name="attention",
    )(owner, x, bias)


def front_kernel(
    tok, cond, og, cgain, wc, cb, wq, qb, wo,
    *outs,
):
    x_o, sg_o, gg_o, s1_o, g1_o, first_o = outs
    width = tok.shape[-1]
    hd = width // head_count
    peers = x_o.shape[0]
    slots = head_count // peers
    cond_low = (norm_parts(cond[...].astype(f32))[0] * cgain[...]).astype(bf16)
    modul = dot(cond_low, wc[...]) + cb[...]
    s1 = jax.nn.sigmoid(modul[:, :width])
    g1 = jax.nn.sigmoid(modul[:, 2 * width :])
    tn, _ = norm_parts(tok[...].astype(f32))
    first = (s1 * tn + modul[:, width : 2 * width]).astype(bf16)
    proj = dot(first, wq[...])
    q = (proj[:, :width] + qb[...]) * (hd**-0.5 * log2e)
    sg = jax.nn.sigmoid(proj[:, 3 * width :])
    ga = (og[...].astype(f32) * g1).astype(bf16)
    gg = dot_nt(ga, wo[...])
    dm = sg * gg
    sg_o[...] = sg.astype(bf16)
    gg_o[...] = gg.astype(bf16)
    s1_o[...] = s1.astype(bf16)
    g1_o[...] = g1.astype(bf16)
    first_o[...] = first
    for i, part in enumerate((q, proj[:, width : 2 * width], proj[:, 2 * width : 3 * width], dm)):
        turned = part.T.astype(bf16).reshape(peers, slots, hd, part.shape[0])
        for t in range(slots):
            x_o[:, t * 4 + i] = turned[:, t]


def half_spec(a, h):
    return pl.BlockSpec((a.shape[0], a.shape[1] // 2), lambda *_: (0, h))


def row_spec(a, rb):
    return pl.BlockSpec((rb, a.shape[1]), lambda i, *_: (i, 0))


def front(tok, cond, og, cgain, wc, cb, wq, qb, wo, slots):
    length, width = tok.shape
    rb = 256
    peers, hd = head_count // slots, width // head_count
    small = jax.ShapeDtypeStruct((length, width), bf16)
    payload = jax.ShapeDtypeStruct((peers, 4 * slots, hd, length), bf16)
    return pl.pallas_call(
        front_kernel,
        grid_spec=pl.GridSpec(
            grid=(length // rb,),
            in_specs=[row_spec(tok, rb), row_spec(cond, rb), row_spec(og, rb)]
            + [whole(cgain)]
            + [half_spec(wc, 0)]
            + [whole(a) for a in (cb, wq, qb, wo)],
            out_specs=[pl.BlockSpec((peers, 4 * slots, hd, rb), lambda i: (0, 0, 0, i))] + [row_spec(tok, rb)] * 5,
        ),
        out_shape=[payload] + [small] * 5,
        compiler_params=params(),
        cost_estimate=pl.CostEstimate(flops=2 * length * width * width * 7, bytes_accessed=20 << 20, transcendentals=length * width * 4),
        name="front",
    )(tok, cond, og, cgain, wc, cb, wq, qb, wo)


def trans_kernel(
    tok, cond, og, cgain, wc, cb, wu, wd,
    part_o, u2_o, dcond_o, ml_o, cn_o, second_o, hid_o, act_o, gt_o, cbg_o,
):
    width = tok.shape[-1]
    cond_low = (norm_parts(cond[...].astype(f32))[0] * cgain[...]).astype(bf16)
    cn_o[...] = cond_low
    modul = dot(cond_low, wc[...]) + cb[...]
    s2 = jax.nn.sigmoid(modul[:, :width])
    g2 = jax.nn.sigmoid(modul[:, 2 * width :])
    tokens = tok[...].astype(f32)
    tn, _ = norm_parts(tokens)
    second = (s2 * tn + modul[:, width : 2 * width]).astype(bf16)
    second_o[...] = second
    hidden = dot(second, wu[...])
    ff = hidden.shape[1] // 2
    h_gate, h_up = hidden[:, :ff], hidden[:, ff:]
    sig = jax.nn.sigmoid(h_gate)
    silu = h_gate * sig
    act = (silu * h_up).astype(bf16)
    act_o[...] = act
    trans_out = dot(act, wd[...])
    part_o[...] = tokens + g2 * trans_out
    g = og[...].astype(f32)
    gt = (g * g2).astype(bf16)
    gt_o[...] = gt
    grad_act = dot_nt(gt, wd[...])
    hid = jnp.concatenate(
        [(grad_act * h_up * (sig * (1.0 + h_gate * (1.0 - sig)))).astype(bf16), (grad_act * silu).astype(bf16)], axis=-1
    )
    hid_o[...] = hid
    grad_second = dot_nt(hid, wu[...])
    u2_o[...] = (grad_second * s2).astype(bf16)
    grads = jnp.concatenate(
        [grad_second * tn * (s2 * (1.0 - s2)), grad_second, g * trans_out * (g2 * (1.0 - g2))], axis=-1
    )
    low = grads.astype(bf16)
    ml_o[...] = low

    @pl.when(pl.program_id(0) == 0)
    def _():
        cbg_o[...] = jnp.zeros_like(cbg_o)

    cbg_o[...] += jnp.sum(grads, axis=0, keepdims=True)
    dcond_o[...] = dot_nt(low, wc[...])


def transition(tok, cond, og, cgain, wc, cb, wu, wd):
    length, width = tok.shape
    rb = 256
    cs, mw = cond.shape[1], cb.shape[1]
    ff2 = wu.shape[1]

    def out(w, dtype):
        return jax.ShapeDtypeStruct((length, w), dtype)

    shapes = [
        out(width, f32), out(width, bf16), out(cs, f32), out(mw, bf16), out(cs, bf16), out(width, bf16),
        out(ff2, bf16), out(ff2 // 2, bf16), out(width, bf16),
    ]
    return pl.pallas_call(
        trans_kernel,
        grid_spec=pl.GridSpec(
            grid=(length // rb,),
            in_specs=[row_spec(tok, rb), row_spec(cond, rb), row_spec(og, rb)]
            + [whole(cgain)]
            + [half_spec(wc, 1)]
            + [whole(a) for a in (cb, wu, wd)],
            out_specs=[row_spec(s, rb) for s in shapes] + [pl.BlockSpec((1, mw), lambda i: (0, 0))],
        ),
        out_shape=shapes + [jax.ShapeDtypeStruct((1, mw), f32)],
        compiler_params=params(),
        cost_estimate=pl.CostEstimate(flops=2 * length * width * width * 15, bytes_accessed=40 << 20, transcendentals=length * width * 6),
        name="transition",
    )(tok, cond, og, cgain, wc, cb, wu, wd)


def back_kernel(slots, *refs):
    ys = refs[:slots]
    (
        sg, gg, s1, g1, part, u2, dcond2, tok, cond, og, cgain, wc, wq, wo,
        out_o, tg_o, cg_o, gated_o, ga_o, gp_o, ml_o, qbg_o, cbg_o, cgg_o,
    ) = refs[slots:]
    rb, width = tok.shape
    hd = width // head_count
    peers = head_count // slots

    def heads(i):
        stacked = jnp.stack([y[:, i] for y in ys], axis=1)
        return stacked.reshape(width, rb).astype(f32).T

    mixed = heads(0)
    sgv = sg[...].astype(f32)
    g1v = g1[...].astype(f32)
    gated = (sgv * mixed).astype(bf16)
    gated_o[...] = gated
    attn_out = dot(gated, wo[...])
    out_o[...] = part[...] + g1v * attn_out
    g = og[...].astype(f32)
    ga_o[...] = (g * g1v).astype(bf16)
    dg = gg[...].astype(f32) * mixed * (sgv * (1.0 - sgv))
    dq = heads(1)
    grad_proj = jnp.concatenate([dq.astype(bf16), heads(2).astype(bf16), heads(3).astype(bf16), dg.astype(bf16)], axis=-1)
    gp_o[...] = grad_proj
    grad_first = dot_nt(grad_proj, wq[...])
    s1v = s1[...].astype(f32)
    tn, tscale = norm_parts(tok[...].astype(f32))
    grads = jnp.concatenate(
        [grad_first * tn * (s1v * (1.0 - s1v)), grad_first, g * attn_out * (g1v * (1.0 - g1v))], axis=-1
    )
    low = grads.astype(bf16)
    ml_o[...] = low
    tg_o[...] = g + norm_back(tn, grad_first * s1v + u2[...].astype(f32), tscale)
    dcond = dot_nt(low, wc[...]) + dcond2[...]
    cx, cscale = norm_parts(cond[...].astype(f32))
    cg_o[...] = norm_back(cx, dcond * cgain[...], cscale)

    @pl.when(pl.program_id(0) == 0)
    def _():
        qbg_o[...] = jnp.zeros_like(qbg_o)
        cbg_o[...] = jnp.zeros_like(cbg_o)
        cgg_o[...] = jnp.zeros_like(cgg_o)

    qbg_o[...] += jnp.sum(dq, axis=0, keepdims=True)
    cbg_o[...] += jnp.sum(grads, axis=0, keepdims=True)
    cgg_o[...] += jnp.sum(dcond * cx, axis=0, keepdims=True)


def back(ys, sg, gg, s1, g1, part, u2, dcond2, tok, cond, og, cgain, wc, wq, wo):
    length, width = tok.shape
    rb = 256
    cs, mw = cond.shape[1], wc.shape[1] // 2
    rows = (sg, gg, s1, g1, part, u2, dcond2, tok, cond, og)
    consts = (wq, wo)

    def out(w, dtype):
        return jax.ShapeDtypeStruct((length, w), dtype)

    shapes = [
        out(width, f32), out(width, f32), out(cs, f32), out(width, bf16), out(width, bf16), out(wq.shape[1], bf16), out(mw, bf16),
    ]
    small = [jax.ShapeDtypeStruct((1, w), f32) for w in (width, mw, cs)]
    return pl.pallas_call(
        functools.partial(back_kernel, len(ys)),
        grid_spec=pl.GridSpec(
            grid=(length // rb,),
            in_specs=[pl.BlockSpec(y.shape[:3] + (rb,), lambda i: (0, 0, 0, i)) for y in ys]
            + [row_spec(a, rb) for a in rows]
            + [whole(cgain)]
            + [half_spec(wc, 0)]
            + [whole(a) for a in consts],
            out_specs=[row_spec(s, rb) for s in shapes] + [pl.BlockSpec(s.shape, lambda i: (0, 0)) for s in small],
        ),
        out_shape=shapes + small,
        compiler_params=params(),
        cost_estimate=pl.CostEstimate(flops=2 * length * width * width * 7, bytes_accessed=40 << 20, transcendentals=length * width),
        name="back",
    )(*ys, *rows, cgain, wc, *consts)


def wgrad_kernel(steps, lhs, *refs):
    *rhs, out_ref, turned = refs
    step = pl.program_id(0)

    @pl.when(step == 0)
    def _():
        turned[...] = lhs[...].T

    for k, r in enumerate(rhs):

        @pl.when(step // steps == k)
        def _():
            out_ref[...] = dot(turned[...], r[...]).astype(bf16).reshape(out_ref.shape)


def wgrad(lhs, *rhs):
    length, k = lhs.shape
    n = sum(r.shape[1] for r in rhs)
    row_groups = k // 96
    col_groups = 16 // row_groups
    piece = n // col_groups
    cols = piece if piece <= 1536 else piece // 2
    steps = n // cols
    each = steps // len(rhs)
    per = piece // cols

    def rhs_spec(t):
        return pl.BlockSpec((length, cols), lambda i: (0, jnp.clip(i - t * each, 0, each - 1)))

    return pl.pallas_call(
        functools.partial(wgrad_kernel, each),
        grid=(steps,),
        in_specs=[whole(lhs)] + [rhs_spec(t) for t in range(len(rhs))],
        out_specs=pl.BlockSpec((2, row_groups, 48, cols), lambda i: (0, i // per, 0, i % per)),
        out_shape=jax.ShapeDtypeStruct((2, 16, 48, piece), bf16),
        scratch_shapes=[pltpu.VMEM((k, length), bf16)],
        compiler_params=params(),
        cost_estimate=pl.CostEstimate(flops=2 * length * k * n, bytes_accessed=2 * (length * (k + n) + k * n), transcendentals=0),
        name="wgrad",
    )(lhs, *rhs)


def laid_out(pieces, rows):
    cols = pieces.shape[-1]
    row_groups = rows // 48
    blocks = pieces.reshape(16 // row_groups, rows, cols).astype(f32)
    return jnp.concatenate([blocks[t] for t in range(blocks.shape[0])], axis=1)


class Reducer:
    stages = 10

    def __init__(self, where, plan, ins, outs, xs, rs, load_sems, send_sems, recv_sems, keep_sems):
        self.where, self.plan, self.ins, self.outs, self.xs, self.rs = where, plan, ins, outs, xs, rs
        self.load_sems, self.send_sems, self.recv_sems, self.keep_sems = load_sems, send_sems, recv_sems, keep_sems
        n = len(plan)
        self.base, self.size, self.off, self.pending = [0] * n, [32] * n, [0] * n, [None] * n
        self.sends = []
        self.loads = [self.load(i) if ins else [] for i in range(n)]

    @staticmethod
    def scratch(plan):
        n = len(plan)
        return (
            [pltpu.VMEM((32, 48, w), bf16) for _, _, w, _, _ in plan]
            + [pltpu.VMEM((31, 48, w), bf16) for _, _, w, _, _ in plan]
            + [pltpu.SemaphoreType.DMA((n, 16))]
            + [pltpu.SemaphoreType.DMA((n, 9))] * 2
            + [pltpu.SemaphoreType.DMA((n,))]
        )

    def load(self, i):
        a, c0, w, order, _ = self.plan[i]
        at = SUM_ORDERS[order].index("y")
        run = 32 >> (at + 1)
        copies = []
        for b in range(1 << at):
            for f in range(2):
                copy = pltpu.make_async_copy(
                    self.ins[a].at[f, pl.ds(b * run, run), :, pl.ds(c0, w)],
                    self.xs[i].at[pl.ds((b * 2 + f) * run, run)],
                    self.load_sems.at[i, b * 2 + f],
                )
                copy.start()
                copies.append(copy)
        return copies

    def store(self, i, first_piece, rows):
        order = self.plan[i][3]
        low = 4 - SUM_ORDERS[order].index("y")
        row_groups = rows.shape[0] // 96
        for f in range(2):
            for g in range(row_groups):
                p = first_piece + g
                at = ((p >> low) * 2 + f) << low | p & ((1 << low) - 1)
                r0 = (f * row_groups + g) * 48
                self.xs[i][at] = rows[r0 : r0 + 48, :]

    def send(self, i, k, src, dst, name):
        copy = remote(src, dst, self.send_sems.at[i, k], self.recv_sems.at[i, k], across(self.where, name))
        self.sends.append(copy)
        self.pending[i] = copy

    def sum_start(self, i, k):
        name = SUM_ORDERS[self.plan[i][3]][k]
        half = self.size[i] // 2
        b = bit_of(self.where, name)
        src = self.xs[i].at[pl.ds(self.base[i] + (1 - b) * half, half)]
        self.send(i, k, src, self.rs[i].at[pl.ds(self.off[i], half)], name)
        self.base[i] = self.base[i] + b * half
        self.size[i] = half

    def sum_finish(self, i):
        self.pending[i].wait_recv()
        half, b0, r0 = self.size[i], self.base[i], self.off[i]
        x, r = self.xs[i], self.rs[i]

        def body(j, _):
            x[b0 + j] = (x[b0 + j].astype(f32) + r[r0 + j].astype(f32)).astype(bf16)
            return 0

        lax.fori_loop(0, half, body, 0)
        self.off[i] = r0 + half

    def block(self, i, done):
        a, c0, w, order, _ = self.plan[i]
        at = [
            slice(None) if name in done else bit_of(self.where, name) for name in SUM_ORDERS[order] if name != "y"
        ]
        return self.outs[a].at[(*at, slice(None), pl.ds(c0, w))]

    def copy_start(self, i, j):
        names = COPY_ORDERS[self.plan[i][4]]
        ref = self.block(i, names[:j])
        self.send(i, 5 + j, ref, ref, names[j])

    def advance(self, i, k):
        if k == 0:
            for copy in self.loads[i]:
                copy.wait()
            self.sum_start(i, 0)
        elif k < 5:
            self.sum_finish(i)
            self.sum_start(i, k)
        elif k == 5:
            self.sum_finish(i)
            keep = pltpu.make_async_copy(self.xs[i].at[self.base[i]], self.block(i, ()), self.keep_sems.at[i])
            keep.start()
            keep.wait()
            self.copy_start(i, 0)
        else:
            self.pending[i].wait_recv()
            if k < 9:
                self.copy_start(i, k - 5)

    def finish(self):
        for copy in self.sends:
            copy.wait_send()


class SmallSum:
    def __init__(self, where, buf, send_sems, recv_sems):
        self.where, self.buf, self.send_sems, self.recv_sems = where, buf, send_sems, recv_sems
        self.copies = []

    def advance(self, k):
        if k > 0:
            self.copies[k - 1].wait_recv()
            self.buf[2 * k] = self.buf[2 * k - 2] + self.buf[2 * k - 1]
        if k < 5:
            src, dst = self.buf.at[2 * k], self.buf.at[2 * k + 1]
            self.copies.append(
                remote(src, dst, self.send_sems.at[k], self.recv_sems.at[k], across(self.where, list(BITS)[k]))
            )


class BiasHome:
    def __init__(self, where, raw, done, home_out, home, kept, got, last, done_v, out, load_sems, send_sems, recv_sems):
        self.where, self.raw, self.home, self.kept, self.got, self.last = where, raw, home, kept, got, last
        self.done_v, self.out, self.send_sems, self.recv_sems = done_v, out, send_sems, recv_sems
        self.z0, self.z1 = bit_of(where, "z0"), bit_of(where, "z1")
        self.loads = [
            pltpu.make_async_copy(raw.at[:, self.z0], kept, load_sems.at[0]),
            pltpu.make_async_copy(done, done_v, load_sems.at[1]),
        ]
        self.keep = pltpu.make_async_copy(out.at[place(where)], home.at[place(where)], load_sems.at[2])
        self.written = pltpu.make_async_copy(home, home_out, load_sems.at[3])
        self.copies = []

    @staticmethod
    def scratch(block, members):
        plane, length = block[1], block[2]
        rows = pltpu.VMEM((members, 2, 2 * plane // members, length), bf16)
        return [
            rows,
            pltpu.VMEM((2,) + block, bf16),
            pltpu.VMEM((2,) + block, bf16),
            pltpu.VMEM(block, bf16),
            pltpu.VMEM(block, bf16),
            rows,
            pltpu.SemaphoreType.DMA((4,)),
            pltpu.SemaphoreType.DMA((2 + len(PEERS),)),
            pltpu.SemaphoreType.DMA((2 + len(PEERS),)),
        ]

    def send(self, k, src, dst, other):
        self.copies.append(remote(src, dst, self.send_sems.at[k], self.recv_sems.at[k], other))

    def lay(self, slot, value):
        members, _, rows, _ = self.out.shape
        each = rows // 2
        for m in range(members):
            part = [value[c, m * each : (m + 1) * each, :] for c in range(2)]
            self.out[m, slot] = jnp.concatenate(part, axis=0).astype(bf16)

    def advance(self, k):
        if k == 0:
            self.send(0, self.raw.at[:, 1 - self.z0], self.got, across(self.where, "z0"))
        elif k == 1:
            self.loads[0].wait()
            self.copies[0].wait_recv()
            self.kept[...] = (self.kept[...].astype(f32) + self.got[...].astype(f32)).astype(bf16)
            self.send(1, self.kept.at[1 - self.z1], self.last, across(self.where, "z1"))
            self.loads[1].wait()
            self.lay(0, self.done_v[...].astype(f32))
        elif k == 2:
            self.copies[1].wait_recv()
            self.lay(1, self.kept[self.z1].astype(f32) + self.last[...].astype(f32))
            for j, names in enumerate(PEERS):
                peer = across(self.where, *names)
                self.send(2 + j, self.out.at[place(peer)], self.home.at[place(self.where)], peer)
            self.keep.start()
        elif k == 3:
            self.keep.wait()
            for copy in self.copies[2:]:
                copy.wait_recv()
            self.written.start()


def reduce_kernel(n_left, *refs):
    refs = list(refs)

    def take(n):
        out, refs[:] = refs[:n], refs[n:]
        return out

    early_in, acts, (raw, done, pair), (small, small_o) = take(2), take(7), take(3), take(2)
    late_out, early_out, (home,) = take(3), take(2), take(1)
    n_late, n_early = len(late_plan), len(early_plan)
    late_scratch, early_scratch = take(2 * n_late + 4), take(2 * n_early + 4)
    bufs, (sbuf, s_send, s_recv, a_sems) = take(7), take(4)
    where = coords()
    bias = BiasHome(where, raw, done, home, *take(9))
    (moment_buf, p_sems) = take(2)
    loads = [pltpu.make_async_copy(src, dst, a_sems.at[i]) for i, (src, dst) in enumerate(zip(acts, bufs))]

    def reducer(plan, ins, outs, scratch):
        n = len(plan)
        return Reducer(where, plan, ins, outs, scratch[:n], scratch[n : 2 * n], *scratch[2 * n :])

    early = reducer(early_plan, early_in, early_out, early_scratch)
    for copy in loads:
        copy.start()
    late = reducer(late_plan, None, late_out, late_scratch)
    for copy in bias.loads:
        copy.start()
    sbuf[0] = small[...]
    greet([across(where, *names) for names in PEERS + (("z0",), ("z1",))])
    small_sum = SmallSum(where, sbuf, s_send, s_recv)
    bias.advance(0)

    first, gp, cn, ml1, ml2, gated, ga = bufs
    sides = ((first, (gp,)), (cn, (ml1, ml2)), (gated, (ga,)))
    turned = {}
    waited = set()

    def ready(k):
        if k not in waited:
            loads[k].wait()
            waited.add(k)

    def multiply(i):
        a, c0, w, _, _ = late_plan[i]
        lhs, rhs = sides[a]
        k0 = (0, 2, 5)[a]
        for k in range(k0, k0 + 1 + len(rhs)):
            ready(k)
        if a not in turned:
            turned[a] = lhs[...].T
        row_groups = turned[a].shape[0] // 96
        total = sum(r.shape[1] for r in rhs)
        piece = total * row_groups // 16
        for g in range(16 // row_groups):
            c = g * piece
            r = rhs[c // rhs[0].shape[1]]
            c = c % rhs[0].shape[1] + c0
            late.store(i, g * row_groups, dot(turned[a], r[:, c : c + w]).astype(bf16))

    pair_rows, length, width = pair.shape[1:]
    heads = bias.home.shape[0] * bias.home.shape[1]

    def pair_copy(c, r):
        return pltpu.make_async_copy(pair.at[c, r], gp.at[:, pl.ds(r * width, width)], p_sems.at[r])

    def moments(c):
        for r in range(pair_rows):
            pair_copy(c, r).wait()
        for r in range(0, pair_rows, 2):
            cols = slice(r * width, (r + 2) * width)
            gp[:, cols] = pair_norm(gp[:, cols])[0].astype(bf16)
        total = 0.0
        for g in range(0, pair_rows, 8):
            grads = bias.home[...].astype(f32)[:, :, c * pair_rows + g : c * pair_rows + g + 8, :]
            total += dot(grads.reshape(heads * 8, length).astype(bf16), gp[:, g * width : (g + 8) * width])
        if c == 0:
            for r in range(pair_rows):
                pair_copy(1, r).start()
            moment_buf[...] = total
        else:
            total = total + moment_buf[...]
            row = lax.rem(lax.broadcasted_iota(jnp.int32, (heads * 8, width), 0), 8)
            own = sum(jnp.where(row == r, total[:, r * width : (r + 1) * width], 0.0) for r in range(8))
            sbuf[0, small.shape[0] - heads :, :] = jnp.sum(own.reshape(heads, 8, width), axis=1)

    stage = {}
    multiplied = 0
    for at, s in enumerate(schedule):
        k = stage.get(s, 0)
        stage[s] = k + 1
        if s == -2:
            small_sum.advance(k)
        elif s == -1:
            bias.advance(k + 1)
            if k > 1:
                moments(k - 2)
        elif s < n_late:
            if k == 0:
                multiply(s)
                multiplied += late_plan[s][0] == 0
                if late_plan[s][0] == 0 and multiplied == sum(p[0] == 0 for p in late_plan):
                    for r in range(pair_rows):
                        pair_copy(0, r).start()
            late.advance(s, k)
        else:
            early.advance(s - n_late, k)
    bias.written.wait()
    small_o[...] = sbuf[10]
    for copy in late.sends + early.sends + small_sum.copies + bias.copies:
        copy.wait_send()


def reduce_all(early, acts, raw, done, pair, small):
    raw = raw.reshape((2, 2) + raw.shape[1:])
    block = done.shape
    members = group_size
    widths = (1536, 1152, 384, 1536, 768)
    shapes = [jax.ShapeDtypeStruct((2, 2, 2, 2, 48, w), bf16) for w in widths]
    any_spec = pl.BlockSpec(memory_space=pl.ANY)
    vm = pl.BlockSpec(memory_space=pltpu.VMEM)
    return pl.pallas_call(
        functools.partial(reduce_kernel, None),
        out_shape=[jax.ShapeDtypeStruct(small.shape, f32)]
        + shapes
        + [jax.ShapeDtypeStruct((members, 2, 2 * block[1] // members, block[2]), bf16)],
        in_specs=[any_spec] * (len(early) + len(acts) + 3) + [vm],
        out_specs=[vm] + [any_spec] * (len(shapes) + 1),
        scratch_shapes=Reducer.scratch(late_plan)
        + Reducer.scratch(early_plan)
        + [pltpu.VMEM(a.shape, bf16) for a in acts]
        + [
            pltpu.VMEM((11,) + small.shape, f32),
            pltpu.SemaphoreType.DMA((5,)),
            pltpu.SemaphoreType.DMA((5,)),
            pltpu.SemaphoreType.DMA((len(acts),)),
        ]
        + BiasHome.scratch(block, members)
        + [pltpu.VMEM((2 * members * 8, 8 * pair.shape[3]), f32), pltpu.SemaphoreType.DMA((pair.shape[1],))],
        compiler_params=params(collective_id=1, has_side_effects=True),
        name="reduce_grads",
    )(*early, *acts, raw, done, pair, small)


late_plan = (
    (0, 0, 768, 2, 3),
    (0, 768, 768, 2, 0),
    (1, 0, 640, 0, 2),
    (1, 640, 512, 3, 3),
    (2, 0, 384, 2, 3),
)
early_plan = (
    (0, 0, 768, 1, 3),
    (0, 768, 768, 0, 3),
    (1, 0, 384, 0, 2),
    (1, 384, 384, 2, 1),
)
schedule = (
    8, 6, 3, 8, 4, 6, 1, 4, 5, 5, 7, 1, 4, 3, 0, -1, 2, 0, 4, 6, 1, 2, 8, 5,
    7, 3, 8, 3, 6, 1, 5, 4, 7, 8, 5, 0, 2, 8, 3, 4, 7, 3, -1, 4, 6, 3, 1, 0,
    7, 6, 2, 3, 5, 6, 1, 7, -1, 8, 5, 6, 1, 2, 0, 7, -1, 4, 2, -2, 0, 7, 8, -2,
    2, 4, 5, 6, 1, 0, 3, 0, 2, 8, 4, 5, 7, 6, -2, 7, 5, 8, 1, -2, 3, 0, -2, 2,
    -2, 1, 0, 2,
)


def on_device(
    tokens, cond, pair, counts, owner, out_grad, cond_gain, cond_weight, cond_bias, qkvg_weight, query_bias,
    out_weight, pair_gain, pair_weight, up_weight, down_weight,
):
    ups, los, ffs = lax.axis_size("up"), lax.axis_size("lo"), lax.axis_size("fsdp")
    plane = ("lo", "fsdp")
    members = los * ffs
    slots = head_count // members
    length, width = tokens.shape[1:]
    rows = pair.shape[1]
    direct = ffs == 2 and los == 4 and ups == 4

    wide = 3 * width

    def spread(got):
        mine = got.reshape(members, 2, rows, length).transpose(1, 0, 2, 3).reshape(2, members * rows, length)
        return lax.all_gather(mine, "up", axis=0, tiled=False)

    matrices = (cond_weight, qkvg_weight, out_weight, up_weight, down_weight)
    if direct:
        wc, wq, wo, wu, wd, spreads = start(
            counts, pair, big_weights(pair_weight), jnp.tile(pair_gain, 2)[None], matrices
        )
    else:
        bias = pair_fwd(counts, pair, pair_weight.T, pair_gain[None])
        bias = bias.reshape(members, slots, 2 * rows, length)
        spreads = lax.all_to_all(bias, plane, 0, 0, tiled=True)
        wc, wq, wo, wu, wd = [lax.all_gather(w, "fsdp", axis=0, tiled=True) for w in matrices]
    biases = [spread(spreads[:, t]) for t in range(slots)]

    tok, cnd, og = tokens[0], cond[0], out_grad[0]
    cgain = cond_gain[None]
    x, sg, gg, s1, g1, first = front(
        tok, cnd, og, cgain, wc, cond_bias[None, :wide], wq, query_bias[None], wo, slots
    )
    x = lax.all_to_all(x, plane, 0, 0, tiled=True)
    part, u2, dcond2, ml2, cn, second, hid, act, gt, cbg2 = transition(
        tok, cnd, og, cgain, wc, cond_bias[None, wide:], wu, wd
    )
    def fold(g):
        k, n = g.shape
        if k == width:
            return g
        if k > width:
            times = k // width
            parts = g.reshape(ffs, times, width // ffs, n)
            return jnp.concatenate([parts[:, t] for t in range(times)], axis=-1).reshape(width, n * times)
        times = width // k
        parts = g.reshape(ffs, k // ffs, times, n // times)
        return jnp.concatenate([parts[:, :, t] for t in range(times)], axis=1).reshape(width, n // times)

    def unfold(h, k, n):
        rows_each = width // ffs
        if k == width:
            return h
        if k > width:
            times = k // width
            return jnp.concatenate([h[:, t * n : (t + 1) * n] for t in range(times)], axis=0)
        times = width // k
        step = rows_each // times
        return jnp.concatenate([h[t * step : (t + 1) * step] for t in range(times)], axis=1)

    def reduced(grads):
        folded = [fold(g) for g in grads]
        mine = lax.psum_scatter(
            jnp.concatenate(folded, axis=1), ("fsdp", "up", "lo"), scatter_dimension=0, tiled=True
        )
        full = lax.all_gather(mine, ("up", "lo"), axis=0, tiled=True)
        outs, at = [], 0
        for g, h in zip(grads, folded):
            outs.append(unfold(full[:, at : at + h.shape[1]], *g.shape).astype(f32))
            at += h.shape[1]
        return outs

    if direct:
        early = [wgrad(second, hid), wgrad(act, gt)]
        x, *early = lax.optimization_barrier((x, *early))
    else:
        up_total, down_total = reduced([dot_tn(second, hid).astype(bf16), dot_tn(act, gt).astype(bf16)])

    owners = lax.dynamic_slice_in_dim(owner, lax.axis_index("up") * members, members)
    ys, bias_grads = [], []
    for t in range(slots):
        if direct:
            y, bg = sending_attention(owners, x, biases[t], t)
        else:
            y, bg = attention(owners, x, biases[t], t)
            y = lax.all_to_all(y, plane, 0, 0, tiled=True)
        ys.append(y)
        if direct and t == slots - 1:
            bias_grads.append(bg)
            continue
        mine = lax.psum_scatter(bg, "up", scatter_dimension=0, tiled=True)
        bias_grads.append(mine.reshape(2, members * rows, length))

    block_out, tokens_grad, cond_grad, gated, ga, gp, ml1, qbg, cbg1, cgg = back(
        ys, sg, gg, s1, g1, part, u2, dcond2, tok, cnd, og, cgain, wc, wq, wo
    )
    if not direct:
        ml = jnp.concatenate([ml1, ml2], axis=1)
        qkvg_total, out_total, cond_total = reduced(
            [dot_tn(first, gp).astype(bf16), dot_tn(gated, ga).astype(bf16), dot_tn(cn, ml).astype(bf16)]
        )

    pieces = [cgg, cbg1, cbg2, qbg]
    stacked = jnp.concatenate([p.reshape(-1, 128) for p in pieces], axis=0)
    if direct:
        height = -(-stacked.shape[0] // 8) * 8 + head_count
        stacked = jnp.pad(stacked, ((0, height - stacked.shape[0]), (0, 0)))
        stacked, *totals, bias_grad = reduce_all(
            early, (first, gp, cn, ml1, ml2, gated, ga), bias_grads[1], bias_grads[0], pair, stacked
        )
        qkvg_total, cond_total, out_total, up_total, down_total = [
            laid_out(p, w.shape[0]) for p, w in zip(totals, (qkvg_weight, cond_weight, out_weight, up_weight, down_weight))
        ]
    else:
        stacked = lax.psum(stacked, ("up", "lo", "fsdp"))
        split = [b.reshape(2, members, rows, length).transpose(1, 0, 2, 3) for b in bias_grads]
        bias_grad = lax.all_to_all(jnp.stack(split, axis=1), plane, 0, 0, tiled=True)
    bias_grad = bias_grad.reshape(head_count, 2, rows, length)
    pw = pair_weight.astype(f32).T
    scaled = pw * pair_gain
    centered = scaled - jnp.mean(scaled, axis=-1, keepdims=True)
    high = centered.astype(bf16)
    low = (centered - high.astype(f32)).astype(bf16)
    pair_grad, moments = pair_bwd(pair, bias_grad, high, low, not direct)
    moments = stacked[-head_count:] if direct else lax.psum(moments, ("up", "lo", "fsdp"))
    small = stacked.reshape(-1)
    ends = [0]
    for p in pieces:
        ends.append(ends[-1] + p.size)
    small = [small[a:b] for a, b in zip(ends[:-1], ends[1:])]
    return (
        block_out[None],
        tokens_grad[None],
        cond_grad[None],
        pair_grad,
        small[0],
        cond_total,
        jnp.concatenate([small[1], small[2]]),
        qkvg_total,
        small[3],
        out_total,
        jnp.sum(pw * moments, axis=0),
        (moments * pair_gain).T,
        up_total,
        down_total,
    )


def solution(mesh):
    dp, fsdp = mesh.shape["dp"], mesh.shape["fsdp"]
    lo = max(1, group_size // fsdp)
    fine = Mesh(mesh.devices.reshape(dp // lo, lo, fsdp), ("up", "lo", "fsdp"))
    every = ("up", "lo", "fsdp")
    in_specs = (
        P(every, None, None),
        P(every, None, None),
        P(None, every, None, None),
        P(),
        P(),
        P(every, None, None),
        P(),
        P("fsdp", None),
        P(),
        P("fsdp", None),
        P(),
        P("fsdp", None),
        P(),
        P(),
        P("fsdp", None),
        P("fsdp", None),
    )
    out_specs = (
        P(every, None, None),
        P(every, None, None),
        P(every, None, None),
        P(None, every, None, None),
        P(),
        P("fsdp", None),
        P(),
        P("fsdp", None),
        P(),
        P("fsdp", None),
        P(),
        P(),
        P("fsdp", None),
        P("fsdp", None),
    )
    return jax.shard_map(on_device, mesh=fine, in_specs=in_specs, out_specs=out_specs, check_vma=False)
```

```python
import functools

import jax
import jax.numpy as jnp
from jax import lax
from jax.experimental import pallas as pl
from jax.experimental.pallas import tpu as pltpu
from jax.sharding import Mesh, PartitionSpec as P

f32, bf16 = jnp.float32, jnp.bfloat16
norm_eps = 1e-05
mask_fill = -1000000000.0
log2e = 1.4426950408889634
ln2 = 0.6931471805599453
head_count = 16
group_size = 8
vmem_bytes = 58 << 20
nt_dims = (((1,), (1,)), ((), ()))


def dot(a, b):
    return jnp.dot(a, b, preferred_element_type=f32)


def dot_nt(a, b):
    return lax.dot_general(a, b, nt_dims, preferred_element_type=f32)


def dot_tn(a, b):
    return lax.dot_general(a, b, (((0,), (0,)), ((), ())), preferred_element_type=f32)


def norm_parts(values):
    centered = values - jnp.mean(values, axis=-1, keepdims=True)
    variance = jnp.mean(centered * centered, axis=-1, keepdims=True)
    scale = lax.rsqrt(variance + norm_eps)
    return centered * scale, scale


def norm_back(x, u, scale):
    mean_u = jnp.mean(u, axis=-1, keepdims=True)
    mean_ux = jnp.mean(u * x, axis=-1, keepdims=True)
    return (u - mean_u - x * mean_ux) * scale


def params(**kw):
    return pltpu.CompilerParams(vmem_limit_bytes=vmem_bytes, **kw)


def whole(a):
    zero = (0,) * a.ndim
    return pl.BlockSpec(a.shape, lambda *_: zero)


MESH = pl.DeviceIdType.MESH
BITS = {"c": ("lo", 1), "x": ("lo", 2), "y": ("fsdp", 1), "z0": ("up", 1), "z1": ("up", 2)}
PEERS = (("c",), ("x",), ("y",), ("c", "x"), ("c", "y"), ("x", "y"), ("c", "x", "y"))
SAMPLE_ORDER = (("x",), ("y",), ("x", "y"), ("c", "x"), ("c", "y"), ("c", "x", "y"), ("c",), ())
SUM_ORDERS = (
    ("c", "x", "y", "z0", "z1"),
    ("c", "x", "z0", "y", "z1"),
    ("c", "y", "x", "z0", "z1"),
    ("c", "z0", "y", "z1", "x"),
)
COPY_ORDERS = (
    ("x", "z0", "z1", "c"),
    ("z0", "z1", "x", "c"),
    ("z1", "x", "z0", "c"),
    ("z1", "z0", "x", "c"),
)


def coords():
    return {a: lax.axis_index(a) for a in ("up", "lo", "fsdp")}


def bit_of(where, name):
    axis, value = BITS[name]
    return lax.rem(where[axis] // value, 2)


def across(where, *names):
    other = dict(where)
    for name in names:
        axis, value = BITS[name]
        other[axis] = other[axis] + value * (1 - 2 * bit_of(where, name))
    return other


def device(where):
    return (where["up"], where["lo"], where["fsdp"])


def place(where):
    return where["lo"] * 2 + where["fsdp"]


def greet(devices):
    barrier = pltpu.get_barrier_semaphore()
    for other in devices:
        pl.semaphore_signal(barrier, inc=1, device_id=device(other), device_id_type=MESH)
    pl.semaphore_wait(barrier, len(devices))


def remote(src, dst, send_sem, recv_sem, other):
    copy = pltpu.make_async_remote_copy(
        src_ref=src, dst_ref=dst, send_sem=send_sem, recv_sem=recv_sem, device_id=device(other), device_id_type=MESH
    )
    copy.start()
    return copy


def lane_means(values):
    total = values.shape[-1]
    group = lax.broadcasted_iota(jnp.int32, (total, total), 0) // 128 == lax.broadcasted_iota(jnp.int32, (total, total), 1) // 128
    return dot(values, jnp.where(group, 1.0 / 128, 0.0).astype(bf16))


def pair_norm(*blocks):
    x = jnp.concatenate(blocks, axis=-1)
    centered = x.astype(f32) - lane_means(x)
    variance = lane_means((centered * centered).astype(bf16))
    scale = lax.rsqrt(variance + norm_eps)
    return centered * scale, scale


def pair_fwd_kernel(rows, counts_ref, x_ref, pw_ref, gain_ref, out_ref, scr_ref):
    step = pl.program_id(0)
    steps_each = pl.num_programs(0) // 2
    limit = counts_ref[step // steps_each]
    heads, length = scr_ref.shape[0], scr_ref.shape[2]
    valid = lax.broadcasted_iota(jnp.int32, (heads, length), 1) < limit
    pw = pw_ref[...]
    gain = gain_ref[...]
    for r in range(rows):
        low = (pair_norm(x_ref[0, r])[0] * gain).astype(bf16)
        bias = dot_nt(pw, low)
        scr_ref[:, r, :] = jnp.where(valid, bias * log2e, mask_fill)
    out_ref[:, 0] = scr_ref[...].astype(bf16)


def pair_fwd(counts, pair, pw_t, gain):
    _, total, length, width = pair.shape
    rows = 8 if total % 8 == 0 else total
    steps = total // rows
    heads = pw_t.shape[0]
    return pl.pallas_call(
        functools.partial(pair_fwd_kernel, rows),
        grid_spec=pltpu.PrefetchScalarGridSpec(
            num_scalar_prefetch=1,
            grid=(2 * steps,),
            in_specs=[
                pl.BlockSpec((1, rows, length, width), lambda i, _: (i // steps, i % steps, 0, 0)),
                whole(pw_t),
                whole(gain),
            ],
            out_specs=pl.BlockSpec((heads, 1, rows, length), lambda i, _: (0, i // steps, i % steps, 0)),
            scratch_shapes=[pltpu.VMEM((heads, rows, length), f32)],
        ),
        out_shape=jax.ShapeDtypeStruct((heads, 2, total, length), bf16),
        compiler_params=params(),
        cost_estimate=pl.CostEstimate(flops=2 * pair.size * 300, bytes_accessed=pair.size * 2, transcendentals=pair.size),
        name="pair_fwd",
    )(counts, pair, pw_t, gain)


def small_outputs(stacked, pw, gain, _, cond_gain_o, cond_bias_o, query_bias_o, pair_gain_o, pair_weight_o):
    row = 0
    for out in (cond_gain_o, cond_bias_o, query_bias_o):
        for k in range(out.shape[0] // 128):
            out[k * 128 : (k + 1) * 128] = stacked[row, :]
            row += 1
    moments = stacked[stacked.shape[0] - head_count :, :]
    pair_gain_o[...] = jnp.sum(pw[...] * moments, axis=0)
    pair_weight_o[...] = moments * gain[...]


def pair_bwd_kernel(rows, n_pieces, x_ref, bg_ref, a_ref, *refs):
    n_small = 4 if n_pieces else 0
    smalls, refs = refs[:n_small], refs[n_small:]
    pieces, (out_ref, *refs) = refs[:n_pieces], refs[n_pieces:]
    laid, sums = refs[:n_pieces], refs[n_pieces:]
    if n_pieces:
        vectors, sums = sums, ()

        @pl.when(pl.program_id(0) == 0)
        def _():
            small_outputs(*smalls, *vectors)

    if sums:
        q_ref, low_buf = sums

        @pl.when(pl.program_id(0) == 0)
        def _():
            q_ref[...] = jnp.zeros_like(q_ref)

    if n_pieces:

        @pl.when(lax.rem(pl.program_id(0), 2) == 0)
        def _():
            for piece, full in zip(pieces, laid):
                groups, _, cols = piece.shape[0] // full.shape[0], piece.shape[1], piece.shape[2]
                for g in range(groups):
                    full[:, :, g * cols : (g + 1) * cols] = piece[g * full.shape[0] : (g + 1) * full.shape[0]].astype(f32)

    width = out_ref.shape[-1]
    heads, _, _, length = bg_ref.shape
    grads = bg_ref[:, 0].astype(f32).reshape(heads * rows, length)
    turned = grads.T.astype(bf16)
    u_all = dot(jnp.concatenate([turned, turned], axis=1), a_ref[...])
    step = 2 - rows % 2
    for r in range(0, rows, step):
        x_hat, scale = pair_norm(*(x_ref[0, r + t] for t in range(step)))
        if sums:
            low_buf[:, r * width : (r + step) * width] = x_hat.astype(bf16)
        u = u_all[:, r * width : (r + step) * width]
        grad = (u - x_hat * lane_means((u * x_hat).astype(bf16))) * scale
        for t in range(step):
            out_ref[0, r + t] = grad[:, t * width : (t + 1) * width]
    if sums:
        q_ref[...] += dot(grads.astype(bf16), low_buf[...])


def pair_bwd_weights(rows, pw, gain):
    rows = 8 if rows % 8 == 0 else rows
    heads, width = pw.shape
    scaled = pw * gain
    centered = scaled - jnp.mean(scaled, axis=-1, keepdims=True)
    high = centered.astype(bf16)
    low = (centered - high.astype(f32)).astype(bf16)
    eye = jnp.eye(rows, dtype=bf16)
    both = jnp.stack([high, low])
    weights = (both[:, :, None, None, :] * eye[None, None, :, :, None]).reshape(2 * heads * rows, rows * width)
    return weights


def pair_bwd(pair, bias_grad, weights, totals=(), heights=(), smalls=(), sizes=()):
    with_sums = not totals
    totals = [t.reshape(16, 48, t.shape[-1]) for t in totals]
    vectors = [jax.ShapeDtypeStruct(shape, f32) for shape in sizes]
    laid = [jax.ShapeDtypeStruct((h // 48, 48, 16 * 48 // h * t.shape[2]), f32) for t, h in zip(totals, heights)]

    _, total, length, width = pair.shape
    rows = 8 if total % 8 == 0 else total
    steps = total // rows
    heads = bias_grad.shape[0]
    grad, *moments = pl.pallas_call(
        functools.partial(pair_bwd_kernel, rows, len(totals)),
        grid=(2 * steps,),
        in_specs=[
            pl.BlockSpec((1, rows, length, width), lambda i: (i // steps, i % steps, 0, 0)),
            pl.BlockSpec((heads, 1, rows, length), lambda i: (0, i // steps, i % steps, 0)),
            whole(weights),
        ]
        + [whole(a) for a in smalls]
        + [pl.BlockSpec((16, 16, t.shape[2]), lambda i: (0, i // 2, 0)) for t in totals],
        out_specs=[pl.BlockSpec((1, rows, length, width), lambda i: (i // steps, i % steps, 0, 0))]
        + [pl.BlockSpec((t.shape[0], 16, t.shape[2]), lambda i: (0, i // 2, 0)) for t in laid]
        + [whole(a) for a in vectors]
        + [pl.BlockSpec((heads * rows, rows * width), lambda i: (0, 0))] * with_sums,
        out_shape=[jax.ShapeDtypeStruct(pair.shape, f32)]
        + laid
        + vectors
        + [jax.ShapeDtypeStruct((heads * rows, rows * width), f32)] * with_sums,
        scratch_shapes=[pltpu.VMEM((length, rows * width), bf16)][:with_sums],
        compiler_params=params(),
        cost_estimate=pl.CostEstimate(flops=2 * pair.size * 500, bytes_accessed=pair.size * 6, transcendentals=pair.size),
        name="pair_bwd",
    )(pair, bias_grad, weights, *smalls, *totals)
    if totals:
        return grad, [m.reshape(-1, m.shape[2]) for m in moments[: len(totals)]], moments[len(totals) :]
    moments = moments[0].reshape(heads, rows, rows, width)
    return grad, sum(moments[:, r, r] for r in range(rows))


class Mover:
    def __init__(self, where, order, own, full, stage, send, recv, keep):
        self.where, self.order, self.own, self.full, self.send, self.recv = where, order, own, full, send, recv
        self.half = own.shape[0]
        self.piece = self.half >> len(order)
        self.mine = sum(bit_of(where, name) << j for j, name in enumerate(order))
        self.copies = []
        self.kept = [
            pltpu.make_async_copy(own, stage, keep.at[0]),
            pltpu.make_async_copy(stage, full.at[pl.ds(where["fsdp"] * self.half, self.half)], keep.at[1]),
        ]

    def stage(self, k):
        if k:
            self.kept[k - 1].wait()
        if k < 2:
            self.kept[k].start()

    def advance(self, k):
        if k:
            self.copies[k - 1].wait_recv()
        if k == 0:
            name, src_at = "y", self.mine * self.piece
            at, size = self.where["fsdp"] * self.half + src_at, self.piece
            src = self.own.at[pl.ds(src_at, size)]
        elif k <= len(self.order):
            name, size = self.order[k - 1], self.piece << (k - 1)
            at = (1 - self.where["fsdp"]) * self.half + self.mine * self.piece // size * size
            src = self.full.at[pl.ds(at, size)]
        else:
            return
        dst = self.full.at[pl.ds(at, size)]
        self.copies.append(remote(src, dst, self.send.at[k], self.recv.at[k], across(self.where, name)))

    def finish(self):
        self.stage(2)
        for copy in self.copies:
            copy.wait_send()


MOVES = (("x", "c"), ("x", "z0", "c"), ("x", "z0", "c"), ("z0", "x", "c"), ("x", "z0", "c"))


def start_kernel(n_w, counts, pw, gain, pair, *refs):
    owns, others, spread = refs[:n_w], refs[n_w : 2 * n_w], refs[2 * n_w]
    *stages, x_buf, low_buf, bias_f, bias_v, x_sems, w_send, w_recv, w_keep, b_send, b_recv, b_sem = refs[2 * n_w + 1 :]
    where = coords()
    peers = [across(where, *names) for names in PEERS]
    total = pair.shape[1]
    length, width = pair.shape[2:]
    heads = bias_f.shape[0]
    groups = 2 * total // 8

    def fetch(g, slot):
        return pltpu.make_async_copy(
            pair.at[(g * 8) // total, pl.ds(lax.rem(g * 8, total), 8)], x_buf.at[slot], x_sems.at[slot]
        )

    fetch(0, 0).start()
    greet(peers + [across(where, "z0")])
    movers = [Mover(where, MOVES[i], owns[i], others[i], stages[i], w_send.at[i], w_recv.at[i], w_keep.at[i]) for i in range(n_w)]
    for m in movers:
        m.advance(0)
    for m in movers:
        m.stage(0)

    def group(g, _):
        slot = lax.rem(g, 2)

        @pl.when(g + 1 < groups)
        def _():
            fetch(g + 1, 1 - slot).start()

        fetch(g, slot).wait()
        for r in range(0, 8, 2):
            x_hat, _ = pair_norm(x_buf[slot, r], x_buf[slot, r + 1])
            low_buf[:, r * width : (r + 2) * width] = (x_hat * gain[...]).astype(bf16)
        bias = dot(low_buf[...], pw[...]).T
        limit = counts[(g * 8) // total]
        valid = lax.broadcasted_iota(jnp.int32, bias.shape, 1) < limit
        bias = jnp.where(valid, bias * log2e, mask_fill)
        bias_f[:, pl.ds(pl.multiple_of(g * 8, 8), 8), :] = bias.reshape(heads, 8, length)
        return 0

    third = groups // 3
    for k in range(3):
        lax.fori_loop(k * third, (k + 1) * third, group, 0)
        movers[k].advance(1)
    for m in movers:
        m.stage(1)
    bias_v[...] = bias_f[...].astype(bf16).reshape(bias_v.shape)

    keep = pltpu.make_async_copy(bias_v.at[place(where)], spread.at[place(where)], b_sem)
    keep.start()
    sent = []

    def send_bias():
        for k, peer in enumerate(peers):
            sent.append(remote(bias_v.at[place(peer)], spread.at[place(where)], b_send.at[k], b_recv.at[k], peer))

    for m in movers[3:]:
        m.advance(1)
    for k in range(2, 5):
        for m in movers:
            if k <= len(m.order) + 1:
                m.advance(k)
        if k == 2:
            send_bias()
    keep.wait()
    for copy in sent:
        copy.wait()
    for m in movers:
        m.finish()


def start(counts, pair, pw_big, gain, owns):
    heads, length, width = 16, pair.shape[2], pair.shape[3]
    rows = 2 * pair.shape[1]
    n = len(owns)
    any_spec = pl.BlockSpec(memory_space=pl.ANY)
    vm = pl.BlockSpec(memory_space=pltpu.VMEM)
    return pl.pallas_call(
        functools.partial(start_kernel, n),
        in_specs=[pl.BlockSpec(memory_space=pltpu.SMEM), vm, vm, any_spec] + [any_spec] * n,
        out_specs=[any_spec] * (n + 1),
        out_shape=[jax.ShapeDtypeStruct((2 * w.shape[0], w.shape[1]), bf16) for w in owns]
        + [jax.ShapeDtypeStruct((8, heads // 8, rows, length), bf16)],
        scratch_shapes=[pltpu.VMEM(w.shape, bf16) for w in owns]
        + [
            pltpu.VMEM((2, 8, length, width), bf16),
            pltpu.VMEM((length, 8 * width), bf16),
            pltpu.VMEM((heads, rows, length), f32),
            pltpu.VMEM((8, heads // 8, rows, length), bf16),
            pltpu.SemaphoreType.DMA((2,)),
            pltpu.SemaphoreType.DMA((n, 4)),
            pltpu.SemaphoreType.DMA((n, 4)),
            pltpu.SemaphoreType.DMA((n, 2)),
            pltpu.SemaphoreType.DMA((7,)),
            pltpu.SemaphoreType.DMA((7,)),
            pltpu.SemaphoreType.DMA,
        ],
        compiler_params=pltpu.CompilerParams(vmem_limit_bytes=vmem_bytes, collective_id=2, has_side_effects=True),
        name="start",
    )(counts, pw_big, gain, pair, *owns)


def big_weights(pw):
    width, heads = pw.shape
    eye = jnp.eye(8, dtype=pw.dtype)
    return (eye[:, None, None, :] * pw[None, :, :, None]).reshape(8 * width, heads * 8)


def attend(rb, c, x_ref, y_ref, bias_ref, add):
    length, hd = x_ref.shape[-1], x_ref.shape[-2]
    bz = bias_ref.shape[2]
    k_t, v_t = x_ref[1], x_ref[2]
    v_ext = jnp.concatenate([v_t, jnp.ones((16, length), bf16)], axis=0)
    dv = dk = 0.0
    for r in range(length // rb):
        sl = slice(r * rb, (r + 1) * rb)
        q_t = x_ref[0, :, sl]
        q = q_t.T
        dm = x_ref[3, :, sl].astype(f32).T
        z0 = r * rb // bz
        bias = jnp.concatenate([bias_ref[z0 + t, c].astype(f32) for t in range(rb // bz)], axis=0)
        s = dot(q, k_t) + bias
        e = jnp.exp2(s - jnp.max(s, axis=-1, keepdims=True))
        eb = e.astype(bf16)
        mx = dot_nt(eb, v_ext)
        inv = 1.0 / mx[:, hd : hd + 1]
        mixed = mx[:, :hd] * inv
        d = jnp.sum(mixed * dm, axis=-1, keepdims=True) * inv
        dms = (dm * inv).astype(bf16)
        ds = e * (dot(dms, v_t) - d)
        dsb = ds.astype(bf16)
        add(sl, ds)
        dq = dot_nt(dsb, k_t)
        dv = dv + dot(dms.T, eb)
        dk = dk + dot(q_t, dsb)
        y_ref[0, :, sl] = mixed.T.astype(bf16)
        y_ref[1, :, sl] = (dq * hd**-0.5).T.astype(bf16)
    y_ref[2] = (dk * ln2).astype(bf16)
    y_ref[3] = dv.astype(bf16)


def attn_kernel(rb, owner_ref, x_ref, bias_ref, y_ref, bg_ref, acc_ref):
    n = pl.program_id(0)
    c = owner_ref[n]
    up, bz = bias_ref.shape[0], bias_ref.shape[2]

    @pl.when(n == 0)
    def _():
        acc_ref[...] = jnp.zeros_like(acc_ref)

    def add(sl, ds):
        acc_ref[c, sl, :] += ds

    attend(rb, c, x_ref.at[0], y_ref.at[0], bias_ref, add)

    @pl.when(n == pl.num_programs(0) - 1)
    def _():
        for z in range(up):
            for cc in range(2):
                bg_ref[z, cc] = acc_ref[cc, z * bz : (z + 1) * bz, :].astype(bf16)


def sending_attn_kernel(
    rb, slot, owner_ref, x_ref, bias_ref, y_ref, bg_ref, both, second, x_buf, y_buf, x_sems, y_send, y_recv, y_keep
):
    step = pl.program_id(0)
    steps = pl.num_programs(0)
    where = coords()
    up, bz = bias_ref.shape[0], bias_ref.shape[2]

    def partner(k):
        other = dict(where)
        for name in ("c", "x", "y"):
            axis, value = BITS[name]
            flip = sum(jnp.where(k == i, 1, 0) for i, names in enumerate(SAMPLE_ORDER) if name in names)
            other[axis] = other[axis] + flip * value * (1 - 2 * bit_of(where, name))
        return other

    def fetch(k):
        return pltpu.make_async_copy(
            x_ref.at[place(partner(k)), pl.ds(slot * 4, 4)], x_buf.at[lax.rem(k, 2)], x_sems.at[lax.rem(k, 2)]
        )

    def sent(k, to):
        return pltpu.make_async_remote_copy(
            src_ref=y_buf.at[k],
            dst_ref=y_ref.at[place(to)],
            send_sem=y_send.at[k],
            recv_sem=y_recv.at[k],
            device_id=device(partner(k)),
            device_id_type=MESH,
        )

    keep = pltpu.make_async_copy(y_buf.at[len(PEERS)], y_ref.at[place(where)], y_keep)

    @pl.when(step == 0)
    def _():
        fetch(0).start()
        both[...] = jnp.zeros_like(both)
        second[...] = jnp.zeros_like(second)
        greet([across(where, *names) for names in PEERS])

    @pl.when(step + 1 < steps)
    def _():
        fetch(step + 1).start()

    fetch(step).wait()
    c = owner_ref[place(partner(step))]
    weight = c.astype(f32)

    def add(sl, ds):
        both[sl, :] += ds
        second[sl, :] += ds * weight

    attend(rb, c, x_buf.at[lax.rem(step, 2)], y_buf.at[step], bias_ref, add)

    @pl.when(step < steps - 1)
    def _():
        sent(step, where).start()

    @pl.when(step == steps - 1)
    def _():
        keep.start()
        for z in range(up):
            sl = slice(z * bz, (z + 1) * bz)
            bg_ref[z, 0] = (both[sl, :] - second[sl, :]).astype(bf16)
            bg_ref[z, 1] = second[sl, :].astype(bf16)
        keep.wait()
        for k in range(len(PEERS)):
            sent(k, partner(k)).wait_recv()
            sent(k, where).wait_send()


def sending_attention(owner, x, bias, slot):
    n, _, hd, length = x.shape
    any_spec = pl.BlockSpec(memory_space=pl.ANY)
    vm = pl.BlockSpec(memory_space=pltpu.VMEM)
    return pl.pallas_call(
        functools.partial(sending_attn_kernel, length // 2, slot),
        grid=(n,),
        in_specs=[pl.BlockSpec(memory_space=pltpu.SMEM), any_spec, vm],
        out_specs=[any_spec, vm],
        out_shape=[jax.ShapeDtypeStruct((n, 4, hd, length), bf16), jax.ShapeDtypeStruct(bias.shape, bf16)],
        scratch_shapes=[
            pltpu.VMEM((length, length), f32),
            pltpu.VMEM((length, length), f32),
            pltpu.VMEM((2, 4, hd, length), bf16),
            pltpu.VMEM((n, 4, hd, length), bf16),
            pltpu.SemaphoreType.DMA((2,)),
            pltpu.SemaphoreType.DMA((n,)),
            pltpu.SemaphoreType.DMA((n,)),
            pltpu.SemaphoreType.DMA,
        ],
        compiler_params=params(collective_id=3 + slot, has_side_effects=True),
        cost_estimate=pl.CostEstimate(
            flops=12 * n * length * length * 256, bytes_accessed=x.size * 2 + bias.size * 4, transcendentals=n * length * length
        ),
        name="attention_and_send",
    )(owner, x, bias)


def attention(owner, x, bias, slot):
    n, _, hd, length = x.shape
    four = 4
    return pl.pallas_call(
        functools.partial(attn_kernel, length // 2),
        grid_spec=pltpu.PrefetchScalarGridSpec(
            num_scalar_prefetch=1,
            grid=(n,),
            in_specs=[
                pl.BlockSpec((1, four, hd, length), lambda i, _: (i, slot, 0, 0)),
                pl.BlockSpec(bias.shape, lambda i, _: (0, 0, 0, 0)),
            ],
            out_specs=[
                pl.BlockSpec((1, four, hd, length), lambda i, _: (i, 0, 0, 0)),
                pl.BlockSpec(bias.shape, lambda i, _: (0, 0, 0, 0)),
            ],
            scratch_shapes=[pltpu.VMEM((2, length, length), f32)],
        ),
        out_shape=[jax.ShapeDtypeStruct((n, four, hd, length), bf16), jax.ShapeDtypeStruct(bias.shape, bf16)],
        compiler_params=params(),
        cost_estimate=pl.CostEstimate(
            flops=12 * n * length * length * 256, bytes_accessed=x.size * 2 + bias.size * 4, transcendentals=n * length * length
        ),
        name="attention",
    )(owner, x, bias)


def front_kernel(
    tok, cond, og, cgain, wc, cb, wq, qb, wo,
    *outs,
):
    x_o, sg_o, gg_o, s1_o, g1_o, first_o = outs
    width = tok.shape[-1]
    hd = width // head_count
    peers = x_o.shape[0]
    slots = head_count // peers
    cond_low = (norm_parts(cond[...].astype(f32))[0] * cgain[...]).astype(bf16)
    modul = dot(cond_low, wc[...]) + cb[...]
    s1 = jax.nn.sigmoid(modul[:, :width])
    g1 = jax.nn.sigmoid(modul[:, 2 * width :])
    tn, _ = norm_parts(tok[...].astype(f32))
    first = (s1 * tn + modul[:, width : 2 * width]).astype(bf16)
    proj = dot(first, wq[...])
    q = (proj[:, :width] + qb[...]) * (hd**-0.5 * log2e)
    sg = jax.nn.sigmoid(proj[:, 3 * width :])
    ga = (og[...].astype(f32) * g1).astype(bf16)
    gg = dot_nt(ga, wo[...])
    dm = sg * gg
    sg_o[...] = sg.astype(bf16)
    gg_o[...] = gg.astype(bf16)
    s1_o[...] = s1.astype(bf16)
    g1_o[...] = g1.astype(bf16)
    first_o[...] = first
    for i, part in enumerate((q, proj[:, width : 2 * width], proj[:, 2 * width : 3 * width], dm)):
        turned = part.T.astype(bf16).reshape(peers, slots, hd, part.shape[0])
        for t in range(slots):
            x_o[:, t * 4 + i] = turned[:, t]


def half_spec(a, h):
    return pl.BlockSpec((a.shape[0], a.shape[1] // 2), lambda *_: (0, h))


def row_spec(a, rb):
    return pl.BlockSpec((rb, a.shape[1]), lambda i, *_: (i, 0))


def front(tok, cond, og, cgain, wc, cb, wq, qb, wo, slots):
    length, width = tok.shape
    rb = 384
    peers, hd = head_count // slots, width // head_count
    small = jax.ShapeDtypeStruct((length, width), bf16)
    payload = jax.ShapeDtypeStruct((peers, 4 * slots, hd, length), bf16)
    return pl.pallas_call(
        front_kernel,
        grid_spec=pl.GridSpec(
            grid=(length // rb,),
            in_specs=[row_spec(tok, rb), row_spec(cond, rb), row_spec(og, rb)]
            + [whole(cgain)]
            + [half_spec(wc, 0)]
            + [whole(a) for a in (cb, wq, qb, wo)],
            out_specs=[pl.BlockSpec((peers, 4 * slots, hd, rb), lambda i: (0, 0, 0, i))] + [row_spec(tok, rb)] * 5,
        ),
        out_shape=[payload] + [small] * 5,
        compiler_params=params(),
        cost_estimate=pl.CostEstimate(flops=2 * length * width * width * 7, bytes_accessed=20 << 20, transcendentals=length * width * 4),
        name="front",
    )(tok, cond, og, cgain, wc, cb, wq, qb, wo)


def trans_kernel(
    tok, cond, og, cgain, wc, cb, wu, wd,
    part_o, u2_o, dcond_o, ml_o, cn_o, second_o, hid_o, act_o, gt_o, cbg_o,
):
    width = tok.shape[-1]
    cond_low = (norm_parts(cond[...].astype(f32))[0] * cgain[...]).astype(bf16)
    cn_o[...] = cond_low
    modul = dot(cond_low, wc[...]) + cb[...]
    s2 = jax.nn.sigmoid(modul[:, :width])
    g2 = jax.nn.sigmoid(modul[:, 2 * width :])
    tokens = tok[...].astype(f32)
    tn, _ = norm_parts(tokens)
    second = (s2 * tn + modul[:, width : 2 * width]).astype(bf16)
    second_o[...] = second
    hidden = dot(second, wu[...])
    ff = hidden.shape[1] // 2
    h_gate, h_up = hidden[:, :ff], hidden[:, ff:]
    sig = jax.nn.sigmoid(h_gate)
    silu = h_gate * sig
    act = (silu * h_up).astype(bf16)
    act_o[...] = act
    trans_out = dot(act, wd[...])
    part_o[...] = tokens + g2 * trans_out
    g = og[...].astype(f32)
    gt = (g * g2).astype(bf16)
    gt_o[...] = gt
    grad_act = dot_nt(gt, wd[...])
    hid = jnp.concatenate(
        [(grad_act * h_up * (sig * (1.0 + h_gate * (1.0 - sig)))).astype(bf16), (grad_act * silu).astype(bf16)], axis=-1
    )
    hid_o[...] = hid
    grad_second = dot_nt(hid, wu[...])
    u2_o[...] = (grad_second * s2).astype(bf16)
    grads = jnp.concatenate(
        [grad_second * tn * (s2 * (1.0 - s2)), grad_second, g * trans_out * (g2 * (1.0 - g2))], axis=-1
    )
    low = grads.astype(bf16)
    ml_o[...] = low

    @pl.when(pl.program_id(0) == 0)
    def _():
        cbg_o[...] = jnp.zeros_like(cbg_o)

    cbg_o[...] += jnp.sum(grads, axis=0, keepdims=True)
    dcond_o[...] = dot_nt(low, wc[...])


def transition(tok, cond, og, cgain, wc, cb, wu, wd):
    length, width = tok.shape
    rb = 384
    cs, mw = cond.shape[1], cb.shape[1]
    ff2 = wu.shape[1]

    def out(w, dtype):
        return jax.ShapeDtypeStruct((length, w), dtype)

    shapes = [
        out(width, f32), out(width, bf16), out(cs, f32), out(mw, bf16), out(cs, bf16), out(width, bf16),
        out(ff2, bf16), out(ff2 // 2, bf16), out(width, bf16),
    ]
    return pl.pallas_call(
        trans_kernel,
        grid_spec=pl.GridSpec(
            grid=(length // rb,),
            in_specs=[row_spec(tok, rb), row_spec(cond, rb), row_spec(og, rb)]
            + [whole(cgain)]
            + [half_spec(wc, 1)]
            + [whole(a) for a in (cb, wu, wd)],
            out_specs=[row_spec(s, rb) for s in shapes] + [pl.BlockSpec((1, mw), lambda i: (0, 0))],
        ),
        out_shape=shapes + [jax.ShapeDtypeStruct((1, mw), f32)],
        compiler_params=params(),
        cost_estimate=pl.CostEstimate(flops=2 * length * width * width * 15, bytes_accessed=40 << 20, transcendentals=length * width * 6),
        name="transition",
    )(tok, cond, og, cgain, wc, cb, wu, wd)


def back_kernel(slots, *refs):
    ys = refs[:slots]
    (
        sg, gg, s1, g1, part, u2, dcond2, tok, cond, og, cbg2, cgain, wc, wq, wo,
        out_o, tg_o, cg_o, gated_o, ga_o, gp_o, ml_o, small_o,
    ) = refs[slots:]
    rb, width = tok.shape
    hd = width // head_count
    peers = head_count // slots

    def heads(i):
        stacked = jnp.stack([y[:, i] for y in ys], axis=1)
        return stacked.reshape(width, rb).astype(f32).T

    mixed = heads(0)
    sgv = sg[...].astype(f32)
    g1v = g1[...].astype(f32)
    gated = (sgv * mixed).astype(bf16)
    gated_o[...] = gated
    attn_out = dot(gated, wo[...])
    out_o[...] = part[...] + g1v * attn_out
    g = og[...].astype(f32)
    ga_o[...] = (g * g1v).astype(bf16)
    dg = gg[...].astype(f32) * mixed * (sgv * (1.0 - sgv))
    dq = heads(1)
    grad_proj = jnp.concatenate([dq.astype(bf16), heads(2).astype(bf16), heads(3).astype(bf16), dg.astype(bf16)], axis=-1)
    gp_o[...] = grad_proj
    grad_first = dot_nt(grad_proj, wq[...])
    s1v = s1[...].astype(f32)
    tn, tscale = norm_parts(tok[...].astype(f32))
    grads = jnp.concatenate(
        [grad_first * tn * (s1v * (1.0 - s1v)), grad_first, g * attn_out * (g1v * (1.0 - g1v))], axis=-1
    )
    low = grads.astype(bf16)
    ml_o[...] = low
    tg_o[...] = g + norm_back(tn, grad_first * s1v + u2[...].astype(f32), tscale)
    dcond = dot_nt(low, wc[...]) + dcond2[...]
    cx, cscale = norm_parts(cond[...].astype(f32))
    cg_o[...] = norm_back(cx, dcond * cgain[...], cscale)

    step = pl.program_id(0)

    @pl.when(step == 0)
    def _():
        small_o[...] = jnp.zeros_like(small_o)

    row = 0
    last = jnp.where(step == pl.num_programs(0) - 1, 1.0, 0.0)
    for values in (
        jnp.sum(dcond * cx, axis=0, keepdims=True),
        jnp.sum(grads, axis=0, keepdims=True),
        cbg2[...] * last,
        jnp.sum(dq, axis=0, keepdims=True),
    ):
        for k in range(values.shape[1] // 128):
            small_o[row : row + 1, :] += values[:, k * 128 : (k + 1) * 128]
            row += 1


def back(ys, sg, gg, s1, g1, part, u2, dcond2, tok, cond, og, cbg2, cgain, wc, wq, wo):
    length, width = tok.shape
    rb = 384
    cs, mw = cond.shape[1], wc.shape[1] // 2
    rows = (sg, gg, s1, g1, part, u2, dcond2, tok, cond, og)
    consts = (wq, wo)

    def out(w, dtype):
        return jax.ShapeDtypeStruct((length, w), dtype)

    shapes = [
        out(width, f32), out(width, f32), out(cs, f32), out(width, bf16), out(width, bf16), out(wq.shape[1], bf16), out(mw, bf16),
    ]
    used = (width + 2 * mw + cs) // 128
    small = [jax.ShapeDtypeStruct((-(-used // 8) * 8 + head_count, 128), f32)]
    return pl.pallas_call(
        functools.partial(back_kernel, len(ys)),
        grid_spec=pl.GridSpec(
            grid=(length // rb,),
            in_specs=[pl.BlockSpec(y.shape[:3] + (rb,), lambda i: (0, 0, 0, i)) for y in ys]
            + [row_spec(a, rb) for a in rows]
            + [whole(cbg2), whole(cgain)]
            + [half_spec(wc, 0)]
            + [whole(a) for a in consts],
            out_specs=[row_spec(s, rb) for s in shapes] + [pl.BlockSpec(s.shape, lambda i: (0, 0)) for s in small],
        ),
        out_shape=shapes + small,
        compiler_params=params(),
        cost_estimate=pl.CostEstimate(flops=2 * length * width * width * 7, bytes_accessed=40 << 20, transcendentals=length * width),
        name="back",
    )(*ys, *rows, cbg2, cgain, wc, *consts)


def wgrad_kernel(steps, lhs, *refs):
    *rhs, out_ref, turned = refs
    step = pl.program_id(0)

    @pl.when(step == 0)
    def _():
        turned[...] = lhs[...].T

    for k, r in enumerate(rhs):

        @pl.when(step // steps == k)
        def _():
            out_ref[...] = dot(turned[...], r[...]).astype(bf16).reshape(out_ref.shape)


def wgrad(lhs, *rhs):
    length, k = lhs.shape
    n = sum(r.shape[1] for r in rhs)
    row_groups = k // 96
    col_groups = 16 // row_groups
    piece = n // col_groups
    cols = piece if piece <= 1536 else piece // 2
    steps = n // cols
    each = steps // len(rhs)
    per = piece // cols

    def rhs_spec(t):
        return pl.BlockSpec((length, cols), lambda i: (0, jnp.clip(i - t * each, 0, each - 1)))

    return pl.pallas_call(
        functools.partial(wgrad_kernel, each),
        grid=(steps,),
        in_specs=[whole(lhs)] + [rhs_spec(t) for t in range(len(rhs))],
        out_specs=pl.BlockSpec((2, row_groups, 48, cols), lambda i: (0, i // per, 0, i % per)),
        out_shape=jax.ShapeDtypeStruct((2, 16, 48, piece), bf16),
        scratch_shapes=[pltpu.VMEM((k, length), bf16)],
        compiler_params=params(),
        cost_estimate=pl.CostEstimate(flops=2 * length * k * n, bytes_accessed=2 * (length * (k + n) + k * n), transcendentals=0),
        name="wgrad",
    )(lhs, *rhs)


class Reducer:
    stages = 10

    def __init__(self, where, plan, ins, outs, xs, rs, load_sems, send_sems, recv_sems, keep_sems):
        self.where, self.plan, self.ins, self.outs, self.xs, self.rs = where, plan, ins, outs, xs, rs
        self.load_sems, self.send_sems, self.recv_sems, self.keep_sems = load_sems, send_sems, recv_sems, keep_sems
        n = len(plan)
        self.base, self.size, self.off, self.pending = [0] * n, [32] * n, [0] * n, [None] * n
        self.sends = []
        self.loads = [self.load(i) if ins else [] for i in range(n)]

    @staticmethod
    def scratch(plan):
        n = len(plan)
        return (
            [pltpu.VMEM((32, 48, w), bf16) for _, _, w, _, _ in plan]
            + [pltpu.VMEM((31, 48, w), bf16) for _, _, w, _, _ in plan]
            + [pltpu.SemaphoreType.DMA((n, 16))]
            + [pltpu.SemaphoreType.DMA((n, 9))] * 2
            + [pltpu.SemaphoreType.DMA((n,))]
        )

    def load(self, i):
        a, c0, w, order, _ = self.plan[i]
        at = SUM_ORDERS[order].index("y")
        run = 32 >> (at + 1)
        copies = []
        for b in range(1 << at):
            for f in range(2):
                copy = pltpu.make_async_copy(
                    self.ins[a].at[f, pl.ds(b * run, run), :, pl.ds(c0, w)],
                    self.xs[i].at[pl.ds((b * 2 + f) * run, run)],
                    self.load_sems.at[i, b * 2 + f],
                )
                copy.start()
                copies.append(copy)
        return copies

    def store(self, i, first_piece, rows):
        order = self.plan[i][3]
        low = 4 - SUM_ORDERS[order].index("y")
        row_groups = rows.shape[0] // 96
        for f in range(2):
            for g in range(row_groups):
                p = first_piece + g
                at = ((p >> low) * 2 + f) << low | p & ((1 << low) - 1)
                r0 = (f * row_groups + g) * 48
                self.xs[i][at] = rows[r0 : r0 + 48, :]

    def send(self, i, k, src, dst, name):
        copy = remote(src, dst, self.send_sems.at[i, k], self.recv_sems.at[i, k], across(self.where, name))
        self.sends.append(copy)
        self.pending[i] = copy

    def sum_start(self, i, k):
        name = SUM_ORDERS[self.plan[i][3]][k]
        half = self.size[i] // 2
        b = bit_of(self.where, name)
        src = self.xs[i].at[pl.ds(self.base[i] + (1 - b) * half, half)]
        self.send(i, k, src, self.rs[i].at[pl.ds(self.off[i], half)], name)
        self.base[i] = self.base[i] + b * half
        self.size[i] = half

    def sum_finish(self, i):
        self.pending[i].wait_recv()
        half, b0, r0 = self.size[i], self.base[i], self.off[i]
        x, r = self.xs[i], self.rs[i]

        def body(j, _):
            x[b0 + j] = (x[b0 + j].astype(f32) + r[r0 + j].astype(f32)).astype(bf16)
            return 0

        lax.fori_loop(0, half, body, 0)
        self.off[i] = r0 + half

    def block(self, i, done):
        a, c0, w, order, _ = self.plan[i]
        at = [
            slice(None) if name in done else bit_of(self.where, name) for name in SUM_ORDERS[order] if name != "y"
        ]
        return self.outs[a].at[(*at, slice(None), pl.ds(c0, w))]

    def copy_start(self, i, j):
        names = COPY_ORDERS[self.plan[i][4]]
        ref = self.block(i, names[:j])
        self.send(i, 5 + j, ref, ref, names[j])

    def advance(self, i, k):
        if k == 0:
            for copy in self.loads[i]:
                copy.wait()
            self.sum_start(i, 0)
        elif k < 5:
            self.sum_finish(i)
            self.sum_start(i, k)
        elif k == 5:
            self.sum_finish(i)
            keep = pltpu.make_async_copy(self.xs[i].at[self.base[i]], self.block(i, ()), self.keep_sems.at[i])
            keep.start()
            keep.wait()
            self.copy_start(i, 0)
        else:
            self.pending[i].wait_recv()
            if k < 9:
                self.copy_start(i, k - 5)

    def finish(self):
        for copy in self.sends:
            copy.wait_send()


class SmallSum:
    def __init__(self, where, buf, send_sems, recv_sems):
        self.where, self.buf, self.send_sems, self.recv_sems = where, buf, send_sems, recv_sems
        self.copies = []

    def advance(self, k):
        if k > 0:
            self.copies[k - 1].wait_recv()
            self.buf[2 * k] = self.buf[2 * k - 2] + self.buf[2 * k - 1]
        if k < 5:
            src, dst = self.buf.at[2 * k], self.buf.at[2 * k + 1]
            self.copies.append(
                remote(src, dst, self.send_sems.at[k], self.recv_sems.at[k], across(self.where, list(BITS)[k]))
            )


class BiasHome:
    def __init__(self, where, raw, done, home_out, home, kept, got, last, done_v, out, load_sems, send_sems, recv_sems):
        self.where, self.raw, self.home, self.kept, self.got, self.last = where, raw, home, kept, got, last
        self.done_v, self.out, self.send_sems, self.recv_sems = done_v, out, send_sems, recv_sems
        self.z0, self.z1 = bit_of(where, "z0"), bit_of(where, "z1")
        self.loads = [
            pltpu.make_async_copy(raw.at[:, self.z0], kept, load_sems.at[0]),
            pltpu.make_async_copy(done, done_v, load_sems.at[1]),
        ]
        self.keep = pltpu.make_async_copy(out.at[place(where)], home.at[place(where)], load_sems.at[2])
        self.written = pltpu.make_async_copy(home, home_out, load_sems.at[3])
        self.copies = []

    @staticmethod
    def scratch(block, members):
        plane, length = block[1], block[2]
        rows = pltpu.VMEM((members, 2, 2 * plane // members, length), bf16)
        return [
            rows,
            pltpu.VMEM((2,) + block, bf16),
            pltpu.VMEM((2,) + block, bf16),
            pltpu.VMEM(block, bf16),
            pltpu.VMEM(block, bf16),
            rows,
            pltpu.SemaphoreType.DMA((4,)),
            pltpu.SemaphoreType.DMA((2 + len(PEERS),)),
            pltpu.SemaphoreType.DMA((2 + len(PEERS),)),
        ]

    def send(self, k, src, dst, other):
        self.copies.append(remote(src, dst, self.send_sems.at[k], self.recv_sems.at[k], other))

    def lay(self, slot, value):
        members, _, rows, _ = self.out.shape
        each = rows // 2
        for m in range(members):
            part = [value[c, m * each : (m + 1) * each, :] for c in range(2)]
            self.out[m, slot] = jnp.concatenate(part, axis=0).astype(bf16)

    def advance(self, k):
        if k == 0:
            self.send(0, self.raw.at[:, 1 - self.z0], self.got, across(self.where, "z0"))
        elif k == 1:
            self.loads[0].wait()
            self.copies[0].wait_recv()
            self.kept[...] = (self.kept[...].astype(f32) + self.got[...].astype(f32)).astype(bf16)
            self.send(1, self.kept.at[1 - self.z1], self.last, across(self.where, "z1"))
            self.loads[1].wait()
            self.lay(0, self.done_v[...].astype(f32))
        elif k == 2:
            self.copies[1].wait_recv()
            self.lay(1, self.kept[self.z1].astype(f32) + self.last[...].astype(f32))
            for j, names in enumerate(PEERS):
                peer = across(self.where, *names)
                self.send(2 + j, self.out.at[place(peer)], self.home.at[place(self.where)], peer)
            self.keep.start()
        elif k == 3:
            self.keep.wait()
            for copy in self.copies[2:]:
                copy.wait_recv()
            self.written.start()


def reduce_kernel(n_left, *refs):
    refs = list(refs)

    def take(n):
        out, refs[:] = refs[:n], refs[n:]
        return out

    early_in, acts, (raw, done, pair), (small, small_o) = take(2), take(7), take(3), take(2)
    late_out, early_out, (home,) = take(3), take(2), take(1)
    n_late, n_early = len(late_plan), len(early_plan)
    late_scratch, early_scratch = take(2 * n_late + 4), take(2 * n_early + 4)
    bufs, (sbuf, s_send, s_recv, a_sems) = take(7), take(4)
    where = coords()
    bias = BiasHome(where, raw, done, home, *take(9))
    (moment_buf, p_sems) = take(2)
    loads = [pltpu.make_async_copy(src, dst, a_sems.at[i]) for i, (src, dst) in enumerate(zip(acts, bufs))]

    def reducer(plan, ins, outs, scratch):
        n = len(plan)
        return Reducer(where, plan, ins, outs, scratch[:n], scratch[n : 2 * n], *scratch[2 * n :])

    early = reducer(early_plan, early_in, early_out, early_scratch)
    for copy in loads:
        copy.start()
    late = reducer(late_plan, None, late_out, late_scratch)
    for copy in bias.loads:
        copy.start()
    sbuf[0] = small[...]
    greet([across(where, *names) for names in PEERS + (("z0",), ("z1",))])
    small_sum = SmallSum(where, sbuf, s_send, s_recv)
    bias.advance(0)

    first, gp, cn, ml1, ml2, gated, ga = bufs
    sides = ((first, (gp,)), (cn, (ml1, ml2)), (gated, (ga,)))
    turned = {}
    waited = set()

    def ready(k):
        if k not in waited:
            loads[k].wait()
            waited.add(k)

    def multiply(i):
        a, c0, w, _, _ = late_plan[i]
        lhs, rhs = sides[a]
        k0 = (0, 2, 5)[a]
        for k in range(k0, k0 + 1 + len(rhs)):
            ready(k)
        if a not in turned:
            turned[a] = lhs[...].T
        row_groups = turned[a].shape[0] // 96
        total = sum(r.shape[1] for r in rhs)
        piece = total * row_groups // 16
        for g in range(16 // row_groups):
            c = g * piece
            r = rhs[c // rhs[0].shape[1]]
            c = c % rhs[0].shape[1] + c0
            late.store(i, g * row_groups, dot(turned[a], r[:, c : c + w]).astype(bf16))

    pair_rows, length, width = pair.shape[1:]
    heads = bias.home.shape[0] * bias.home.shape[1]

    def pair_copy(c, r):
        return pltpu.make_async_copy(pair.at[c, r], gp.at[:, pl.ds(r * width, width)], p_sems.at[r])

    def moments(c):
        for r in range(pair_rows):
            pair_copy(c, r).wait()
        for r in range(0, pair_rows, 2):
            cols = slice(r * width, (r + 2) * width)
            gp[:, cols] = pair_norm(gp[:, cols])[0].astype(bf16)
        total = 0.0
        for g in range(0, pair_rows, 8):
            grads = bias.home[...].astype(f32)[:, :, c * pair_rows + g : c * pair_rows + g + 8, :]
            total += dot(grads.reshape(heads * 8, length).astype(bf16), gp[:, g * width : (g + 8) * width])
        if c == 0:
            for r in range(pair_rows):
                pair_copy(1, r).start()
            moment_buf[...] = total
        else:
            total = total + moment_buf[...]
            row = lax.rem(lax.broadcasted_iota(jnp.int32, (heads * 8, width), 0), 8)
            own = sum(jnp.where(row == r, total[:, r * width : (r + 1) * width], 0.0) for r in range(8))
            sbuf[0, small.shape[0] - heads :, :] = jnp.sum(own.reshape(heads, 8, width), axis=1)

    stage = {}
    multiplied = 0
    for at, s in enumerate(schedule):
        k = stage.get(s, 0)
        stage[s] = k + 1
        if s == -2:
            small_sum.advance(k)
        elif s == -1:
            bias.advance(k + 1)
            if k > 1:
                moments(k - 2)
        elif s < n_late:
            if k == 0:
                multiply(s)
                multiplied += late_plan[s][0] == 0
                if late_plan[s][0] == 0 and multiplied == sum(p[0] == 0 for p in late_plan):
                    for r in range(pair_rows):
                        pair_copy(0, r).start()
            late.advance(s, k)
        else:
            early.advance(s - n_late, k)
    bias.written.wait()
    small_o[...] = sbuf[10]
    for copy in late.sends + early.sends + small_sum.copies + bias.copies:
        copy.wait_send()


def reduce_all(early, acts, raw, done, pair, small):
    raw = raw.reshape((2, 2) + raw.shape[1:])
    block = done.shape
    members = group_size
    widths = (1536, 1152, 384, 1536, 768)
    shapes = [jax.ShapeDtypeStruct((2, 2, 2, 2, 48, w), bf16) for w in widths]
    any_spec = pl.BlockSpec(memory_space=pl.ANY)
    vm = pl.BlockSpec(memory_space=pltpu.VMEM)
    return pl.pallas_call(
        functools.partial(reduce_kernel, None),
        out_shape=[jax.ShapeDtypeStruct(small.shape, f32)]
        + shapes
        + [jax.ShapeDtypeStruct((members, 2, 2 * block[1] // members, block[2]), bf16)],
        in_specs=[any_spec] * (len(early) + len(acts) + 3) + [vm],
        out_specs=[vm] + [any_spec] * (len(shapes) + 1),
        scratch_shapes=Reducer.scratch(late_plan)
        + Reducer.scratch(early_plan)
        + [pltpu.VMEM(a.shape, bf16) for a in acts]
        + [
            pltpu.VMEM((11,) + small.shape, f32),
            pltpu.SemaphoreType.DMA((5,)),
            pltpu.SemaphoreType.DMA((5,)),
            pltpu.SemaphoreType.DMA((len(acts),)),
        ]
        + BiasHome.scratch(block, members)
        + [pltpu.VMEM((2 * members * 8, 8 * pair.shape[3]), f32), pltpu.SemaphoreType.DMA((pair.shape[1],))],
        compiler_params=params(collective_id=1, has_side_effects=True),
        name="reduce_grads",
    )(*early, *acts, raw, done, pair, small)


late_plan = (
    (0, 0, 768, 2, 3),
    (0, 768, 768, 2, 0),
    (1, 0, 640, 0, 2),
    (1, 640, 512, 3, 3),
    (2, 0, 384, 2, 3),
)
early_plan = (
    (0, 0, 768, 1, 3),
    (0, 768, 768, 0, 3),
    (1, 0, 384, 0, 2),
    (1, 384, 384, 2, 1),
)
schedule = (
    8, 6, 3, 8, 4, 6, 1, 4, 5, 5, 7, 1, 4, 3, 0, -1, 2, 0, 4, 6, 1, 2, 8, 5,
    7, 3, 8, 3, 6, 1, 5, 4, 7, 8, 5, 0, 2, 8, 3, 4, 7, 3, -1, 4, 6, 3, 1, 0,
    7, 6, 2, 3, 5, 6, 1, 7, -1, 8, 5, 6, 1, 2, 0, 7, -1, 4, 2, -2, 0, 7, 8, -2,
    2, 4, 5, 6, 1, 0, 3, 0, 2, 8, 4, 5, 7, 6, -2, 7, 5, 8, 1, -2, 3, 0, -2, 2,
    -2, 1, 0, 2,
)


def on_device(
    tokens, cond, pair, counts, owner, out_grad, cond_gain, cond_weight, cond_bias, qkvg_weight, query_bias,
    out_weight, pair_gain, pair_weight, up_weight, down_weight,
):
    ups, los, ffs = lax.axis_size("up"), lax.axis_size("lo"), lax.axis_size("fsdp")
    plane = ("lo", "fsdp")
    members = los * ffs
    slots = head_count // members
    length, width = tokens.shape[1:]
    rows = pair.shape[1]
    direct = ffs == 2 and los == 4 and ups == 4

    wide = 3 * width

    def spread(got):
        mine = got.reshape(members, 2, rows, length).transpose(1, 0, 2, 3).reshape(2, members * rows, length)
        return lax.all_gather(mine, "up", axis=0, tiled=False)

    matrices = (cond_weight, qkvg_weight, out_weight, up_weight, down_weight)
    if direct:
        wc, wq, wo, wu, wd, spreads = start(
            counts, pair, big_weights(pair_weight), jnp.tile(pair_gain, 2)[None], matrices
        )
    else:
        bias = pair_fwd(counts, pair, pair_weight.T, pair_gain[None])
        bias = bias.reshape(members, slots, 2 * rows, length)
        spreads = lax.all_to_all(bias, plane, 0, 0, tiled=True)
        wc, wq, wo, wu, wd = [lax.all_gather(w, "fsdp", axis=0, tiled=True) for w in matrices]
    biases = [spread(spreads[:, t]) for t in range(slots)]

    pw = pair_weight.astype(f32).T
    bwd_weights = pair_bwd_weights(rows, pw, pair_gain)
    tok, cnd, og = tokens[0], cond[0], out_grad[0]
    cgain = cond_gain[None]
    x, sg, gg, s1, g1, first = front(
        tok, cnd, og, cgain, wc, cond_bias[None, :wide], wq, query_bias[None], wo, slots
    )
    x = lax.all_to_all(x, plane, 0, 0, tiled=True)
    part, u2, dcond2, ml2, cn, second, hid, act, gt, cbg2 = transition(
        tok, cnd, og, cgain, wc, cond_bias[None, wide:], wu, wd
    )
    def fold(g):
        k, n = g.shape
        if k == width:
            return g
        if k > width:
            times = k // width
            parts = g.reshape(ffs, times, width // ffs, n)
            return jnp.concatenate([parts[:, t] for t in range(times)], axis=-1).reshape(width, n * times)
        times = width // k
        parts = g.reshape(ffs, k // ffs, times, n // times)
        return jnp.concatenate([parts[:, :, t] for t in range(times)], axis=1).reshape(width, n // times)

    def unfold(h, k, n):
        rows_each = width // ffs
        if k == width:
            return h
        if k > width:
            times = k // width
            return jnp.concatenate([h[:, t * n : (t + 1) * n] for t in range(times)], axis=0)
        times = width // k
        step = rows_each // times
        return jnp.concatenate([h[t * step : (t + 1) * step] for t in range(times)], axis=1)

    def reduced(grads):
        folded = [fold(g) for g in grads]
        mine = lax.psum_scatter(
            jnp.concatenate(folded, axis=1), ("fsdp", "up", "lo"), scatter_dimension=0, tiled=True
        )
        full = lax.all_gather(mine, ("up", "lo"), axis=0, tiled=True)
        outs, at = [], 0
        for g, h in zip(grads, folded):
            outs.append(unfold(full[:, at : at + h.shape[1]], *g.shape).astype(f32))
            at += h.shape[1]
        return outs

    if direct:
        early = [wgrad(second, hid), wgrad(act, gt)]
        x, bwd_weights, *early = lax.optimization_barrier((x, bwd_weights, *early))
    else:
        up_total, down_total = reduced([dot_tn(second, hid).astype(bf16), dot_tn(act, gt).astype(bf16)])

    owners = lax.dynamic_slice_in_dim(owner, lax.axis_index("up") * members, members)
    ys, bias_grads = [], []
    for t in range(slots):
        if direct:
            y, bg = sending_attention(owners, x, biases[t], t)
        else:
            y, bg = attention(owners, x, biases[t], t)
            y = lax.all_to_all(y, plane, 0, 0, tiled=True)
        ys.append(y)
        if direct and t == slots - 1:
            bias_grads.append(bg)
            continue
        mine = lax.psum_scatter(bg, "up", scatter_dimension=0, tiled=True)
        bias_grads.append(mine.reshape(2, members * rows, length))

    block_out, tokens_grad, cond_grad, gated, ga, gp, ml1, stacked = back(
        ys, sg, gg, s1, g1, part, u2, dcond2, tok, cnd, og, cbg2, cgain, wc, wq, wo
    )
    if not direct:
        ml = jnp.concatenate([ml1, ml2], axis=1)
        qkvg_total, out_total, cond_total = reduced(
            [dot_tn(first, gp).astype(bf16), dot_tn(gated, ga).astype(bf16), dot_tn(cn, ml).astype(bf16)]
        )

    if direct:
        stacked, *totals, bias_grad = reduce_all(
            early, (first, gp, cn, ml1, ml2, gated, ga), bias_grads[1], bias_grads[0], pair, stacked
        )
    else:
        stacked = lax.psum(stacked, ("up", "lo", "fsdp"))
        split = [b.reshape(2, members, rows, length).transpose(1, 0, 2, 3) for b in bias_grads]
        bias_grad = lax.all_to_all(jnp.stack(split, axis=1), plane, 0, 0, tiled=True)
    bias_grad = bias_grad.reshape(head_count, 2, rows, length)
    if direct:
        heights = [w.shape[0] for w in (qkvg_weight, cond_weight, out_weight, up_weight, down_weight)]
        smalls = (stacked, pw, pair_gain[None], pair_gain[None])
        sizes = (cond_gain.shape, cond_bias.shape, query_bias.shape, pair_gain.shape, pw.shape)
        pair_grad, laid, vectors = pair_bwd(pair, bias_grad, bwd_weights, totals, heights, smalls, sizes)
        vectors[4] = vectors[4].T
        qkvg_total, cond_total, out_total, up_total, down_total = laid
    else:
        pair_grad, moments = pair_bwd(pair, bias_grad, bwd_weights)
    moments = stacked[-head_count:] if direct else lax.psum(moments, ("up", "lo", "fsdp"))
    if not direct:
        small = stacked.reshape(-1)
        ends = [0, cond_gain.size, cond_gain.size + cond_bias.size, cond_gain.size + cond_bias.size + query_bias.size]
        vectors = [small[a:b] for a, b in zip(ends[:-1], ends[1:])]
        vectors += [jnp.sum(pw * moments, axis=0), (moments * pair_gain).T]
    return (
        block_out[None],
        tokens_grad[None],
        cond_grad[None],
        pair_grad,
        vectors[0],
        cond_total,
        vectors[1],
        qkvg_total,
        vectors[2],
        out_total,
        vectors[3],
        vectors[4],
        up_total,
        down_total,
    )


def solution(mesh):
    dp, fsdp = mesh.shape["dp"], mesh.shape["fsdp"]
    lo = max(1, group_size // fsdp)
    fine = Mesh(mesh.devices.reshape(dp // lo, lo, fsdp), ("up", "lo", "fsdp"))
    every = ("up", "lo", "fsdp")
    in_specs = (
        P(every, None, None),
        P(every, None, None),
        P(None, every, None, None),
        P(),
        P(),
        P(every, None, None),
        P(),
        P("fsdp", None),
        P(),
        P("fsdp", None),
        P(),
        P("fsdp", None),
        P(),
        P(),
        P("fsdp", None),
        P("fsdp", None),
    )
    out_specs = (
        P(every, None, None),
        P(every, None, None),
        P(every, None, None),
        P(None, every, None, None),
        P(),
        P("fsdp", None),
        P(),
        P("fsdp", None),
        P(),
        P("fsdp", None),
        P(),
        P(),
        P("fsdp", None),
        P("fsdp", None),
    )
    return jax.shard_map(on_device, mesh=fine, in_specs=in_specs, out_specs=out_specs, check_vma=False)
```

```python
import functools

import jax
import jax.numpy as jnp
from jax import lax
from jax.experimental import pallas as pl
from jax.experimental.pallas import tpu as pltpu
from jax.sharding import Mesh, PartitionSpec as P

f32, bf16 = jnp.float32, jnp.bfloat16
norm_eps = 1e-05
mask_fill = -1000000000.0
log2e = 1.4426950408889634
ln2 = 0.6931471805599453
head_count = 16
group_size = 8
vmem_bytes = 58 << 20
nt_dims = (((1,), (1,)), ((), ()))


def dot(a, b):
    return jnp.dot(a, b, preferred_element_type=f32)


def dot_nt(a, b):
    return lax.dot_general(a, b, nt_dims, preferred_element_type=f32)


def dot_tn(a, b):
    return lax.dot_general(a, b, (((0,), (0,)), ((), ())), preferred_element_type=f32)


def norm_parts(values):
    centered = values - jnp.mean(values, axis=-1, keepdims=True)
    variance = jnp.mean(centered * centered, axis=-1, keepdims=True)
    scale = lax.rsqrt(variance + norm_eps)
    return centered * scale, scale


def norm_back(x, u, scale):
    mean_u = jnp.mean(u, axis=-1, keepdims=True)
    mean_ux = jnp.mean(u * x, axis=-1, keepdims=True)
    return (u - mean_u - x * mean_ux) * scale


def params(**kw):
    return pltpu.CompilerParams(vmem_limit_bytes=vmem_bytes, **kw)


def whole(a):
    zero = (0,) * a.ndim
    return pl.BlockSpec(a.shape, lambda *_: zero)


MESH = pl.DeviceIdType.MESH
BITS = {"c": ("lo", 1), "x": ("lo", 2), "y": ("fsdp", 1), "z0": ("up", 1), "z1": ("up", 2)}
PEERS = (("c",), ("x",), ("y",), ("c", "x"), ("c", "y"), ("x", "y"), ("c", "x", "y"))
SAMPLE_ORDER = (("x",), ("y",), ("x", "y"), ("c", "x"), ("c", "y"), ("c", "x", "y"), ("c",), ())
SUM_ORDERS = (
    ("c", "x", "y", "z0", "z1"),
    ("c", "x", "y", "z1", "z0"),
    ("c", "y", "x", "z0", "z1"),
    ("c", "z0", "x", "y", "z1"),
)
COPY_ORDERS = (
    ("z0", "x", "z1", "c"),
    ("z0", "z1", "x", "c"),
    ("z1", "x", "z0", "c"),
    ("z1", "z0", "x", "c"),
)


def coords():
    return {a: lax.axis_index(a) for a in ("up", "lo", "fsdp")}


def bit_of(where, name):
    axis, value = BITS[name]
    return lax.rem(where[axis] // value, 2)


def across(where, *names):
    other = dict(where)
    for name in names:
        axis, value = BITS[name]
        other[axis] = other[axis] + value * (1 - 2 * bit_of(where, name))
    return other


def device(where):
    return (where["up"], where["lo"], where["fsdp"])


def place(where):
    return where["lo"] * 2 + where["fsdp"]


def greet(devices):
    barrier = pltpu.get_barrier_semaphore()
    for other in devices:
        pl.semaphore_signal(barrier, inc=1, device_id=device(other), device_id_type=MESH)
    pl.semaphore_wait(barrier, len(devices))


def remote(src, dst, send_sem, recv_sem, other):
    copy = pltpu.make_async_remote_copy(
        src_ref=src, dst_ref=dst, send_sem=send_sem, recv_sem=recv_sem, device_id=device(other), device_id_type=MESH
    )
    copy.start()
    return copy


def lane_means(values):
    total = values.shape[-1]
    group = lax.broadcasted_iota(jnp.int32, (total, total), 0) // 128 == lax.broadcasted_iota(jnp.int32, (total, total), 1) // 128
    return dot(values, jnp.where(group, 1.0 / 128, 0.0).astype(bf16))


def pair_norm(*blocks):
    x = jnp.concatenate(blocks, axis=-1)
    centered = x.astype(f32) - lane_means(x)
    variance = lane_means((centered * centered).astype(bf16))
    scale = lax.rsqrt(variance + norm_eps)
    return centered * scale, scale


def pair_fwd_kernel(rows, counts_ref, x_ref, pw_ref, gain_ref, out_ref, scr_ref):
    step = pl.program_id(0)
    steps_each = pl.num_programs(0) // 2
    limit = counts_ref[step // steps_each]
    heads, length = scr_ref.shape[0], scr_ref.shape[2]
    valid = lax.broadcasted_iota(jnp.int32, (heads, length), 1) < limit
    pw = pw_ref[...]
    gain = gain_ref[...]
    for r in range(rows):
        low = (pair_norm(x_ref[0, r])[0] * gain).astype(bf16)
        bias = dot_nt(pw, low)
        scr_ref[:, r, :] = jnp.where(valid, bias * log2e, mask_fill)
    out_ref[:, 0] = scr_ref[...].astype(bf16)


def pair_fwd(counts, pair, pw_t, gain):
    _, total, length, width = pair.shape
    rows = 8 if total % 8 == 0 else total
    steps = total // rows
    heads = pw_t.shape[0]
    return pl.pallas_call(
        functools.partial(pair_fwd_kernel, rows),
        grid_spec=pltpu.PrefetchScalarGridSpec(
            num_scalar_prefetch=1,
            grid=(2 * steps,),
            in_specs=[
                pl.BlockSpec((1, rows, length, width), lambda i, _: (i // steps, i % steps, 0, 0)),
                whole(pw_t),
                whole(gain),
            ],
            out_specs=pl.BlockSpec((heads, 1, rows, length), lambda i, _: (0, i // steps, i % steps, 0)),
            scratch_shapes=[pltpu.VMEM((heads, rows, length), f32)],
        ),
        out_shape=jax.ShapeDtypeStruct((heads, 2, total, length), bf16),
        compiler_params=params(),
        cost_estimate=pl.CostEstimate(flops=2 * pair.size * 300, bytes_accessed=pair.size * 2, transcendentals=pair.size),
        name="pair_fwd",
    )(counts, pair, pw_t, gain)


def small_outputs(stacked, pw, gain, _, cond_gain_o, cond_bias_o, query_bias_o, pair_gain_o, pair_weight_o):
    row = 0
    for out in (cond_gain_o, cond_bias_o, query_bias_o):
        for k in range(out.shape[0] // 128):
            out[k * 128 : (k + 1) * 128] = stacked[row, :]
            row += 1
    moments = stacked[stacked.shape[0] - head_count :, :]
    pair_gain_o[...] = jnp.sum(pw[...] * moments, axis=0)
    pair_weight_o[...] = moments * gain[...]


def pair_bwd_kernel(rows, n_pieces, x_ref, bg_ref, a_ref, *refs):
    n_small = 4 if n_pieces else 0
    smalls, refs = refs[:n_small], refs[n_small:]
    pieces, (out_ref, *refs) = refs[:n_pieces], refs[n_pieces:]
    laid, sums = refs[:n_pieces], refs[n_pieces:]
    if n_pieces:
        vectors, sums = sums, ()

        @pl.when(pl.program_id(0) == 0)
        def _():
            small_outputs(*smalls, *vectors)

    if sums:
        q_ref, low_buf = sums

        @pl.when(pl.program_id(0) == 0)
        def _():
            q_ref[...] = jnp.zeros_like(q_ref)

    for piece, full in zip(pieces, laid):
        groups, cols = piece.shape[0] // full.shape[0], piece.shape[2]
        for g in range(groups):
            full[:, :, g * cols : (g + 1) * cols] = piece[g * full.shape[0] : (g + 1) * full.shape[0]].astype(f32)

    width = out_ref.shape[-1]
    heads, _, _, length = bg_ref.shape
    grads = bg_ref[:, 0].astype(f32).reshape(heads * rows, length)
    turned = grads.T.astype(bf16)
    u_all = dot(jnp.concatenate([turned, turned], axis=1), a_ref[...])
    step = 2 - rows % 2
    for r in range(0, rows, step):
        x_hat, scale = pair_norm(*(x_ref[0, r + t] for t in range(step)))
        if sums:
            low_buf[:, r * width : (r + step) * width] = x_hat.astype(bf16)
        u = u_all[:, r * width : (r + step) * width]
        grad = (u - x_hat * lane_means((u * x_hat).astype(bf16))) * scale
        for t in range(step):
            out_ref[0, r + t] = grad[:, t * width : (t + 1) * width]
    if sums:
        q_ref[...] += dot(grads.astype(bf16), low_buf[...])


def pair_bwd_weights(rows, pw, gain):
    rows = 8 if rows % 8 == 0 else rows
    heads, width = pw.shape
    scaled = pw * gain
    centered = scaled - jnp.mean(scaled, axis=-1, keepdims=True)
    high = centered.astype(bf16)
    low = (centered - high.astype(f32)).astype(bf16)
    eye = jnp.eye(rows, dtype=bf16)
    both = jnp.stack([high, low])
    weights = (both[:, :, None, None, :] * eye[None, None, :, :, None]).reshape(2 * heads * rows, rows * width)
    return weights


def pair_bwd(pair, bias_grad, weights, totals=(), heights=(), smalls=(), sizes=()):
    with_sums = not totals
    totals = [t.reshape(16, 48, t.shape[-1]) for t in totals]
    vectors = [jax.ShapeDtypeStruct(shape, f32) for shape in sizes]
    laid = [jax.ShapeDtypeStruct((h // 48, 48, 16 * 48 // h * t.shape[2]), f32) for t, h in zip(totals, heights)]

    _, total, length, width = pair.shape
    rows = 8 if total % 8 == 0 else total
    steps = total // rows
    heads = bias_grad.shape[0]
    grad, *moments = pl.pallas_call(
        functools.partial(pair_bwd_kernel, rows, len(totals)),
        grid=(2 * steps,),
        in_specs=[
            pl.BlockSpec((1, rows, length, width), lambda i: (i // steps, i % steps, 0, 0)),
            pl.BlockSpec((heads, 1, rows, length), lambda i: (0, i // steps, i % steps, 0)),
            whole(weights),
        ]
        + [whole(a) for a in smalls]
        + [pl.BlockSpec((16, 8, t.shape[2]), lambda i: (0, i, 0)) for t in totals],
        out_specs=[pl.BlockSpec((1, rows, length, width), lambda i: (i // steps, i % steps, 0, 0))]
        + [pl.BlockSpec((t.shape[0], 8, t.shape[2]), lambda i: (0, i, 0)) for t in laid]
        + [whole(a) for a in vectors]
        + [pl.BlockSpec((heads * rows, rows * width), lambda i: (0, 0))] * with_sums,
        out_shape=[jax.ShapeDtypeStruct(pair.shape, f32)]
        + laid
        + vectors
        + [jax.ShapeDtypeStruct((heads * rows, rows * width), f32)] * with_sums,
        scratch_shapes=[pltpu.VMEM((length, rows * width), bf16)][:with_sums],
        compiler_params=params(),
        cost_estimate=pl.CostEstimate(flops=2 * pair.size * 500, bytes_accessed=pair.size * 6, transcendentals=pair.size),
        name="pair_bwd",
    )(pair, bias_grad, weights, *smalls, *totals)
    if totals:
        return grad, [m.reshape(-1, m.shape[2]) for m in moments[: len(totals)]], moments[len(totals) :]
    moments = moments[0].reshape(heads, rows, rows, width)
    return grad, sum(moments[:, r, r] for r in range(rows))


class Mover:
    def __init__(self, where, order, own, full, stage, send, recv, keep):
        self.where, self.order, self.own, self.full, self.send, self.recv = where, order, own, full, send, recv
        self.half = own.shape[0]
        self.piece = self.half >> len(order)
        self.mine = sum(bit_of(where, name) << j for j, name in enumerate(order))
        self.copies = []
        self.kept = [
            pltpu.make_async_copy(own, stage, keep.at[0]),
            pltpu.make_async_copy(stage, full.at[pl.ds(where["fsdp"] * self.half, self.half)], keep.at[1]),
        ]

    def stage(self, k):
        if k:
            self.kept[k - 1].wait()
        if k < 2:
            self.kept[k].start()

    def advance(self, k):
        if k:
            self.copies[k - 1].wait_recv()
        if k == 0:
            name, src_at = "y", self.mine * self.piece
            at, size = self.where["fsdp"] * self.half + src_at, self.piece
            src = self.own.at[pl.ds(src_at, size)]
        elif k <= len(self.order):
            name, size = self.order[k - 1], self.piece << (k - 1)
            at = (1 - self.where["fsdp"]) * self.half + self.mine * self.piece // size * size
            src = self.full.at[pl.ds(at, size)]
        else:
            return
        dst = self.full.at[pl.ds(at, size)]
        self.copies.append(remote(src, dst, self.send.at[k], self.recv.at[k], across(self.where, name)))

    def finish(self):
        self.stage(2)
        for copy in self.copies:
            copy.wait_send()


MOVES = (("x", "c"), ("x", "z0", "c"), ("x", "z0", "c"), ("z0", "x", "c"), ("x", "z0", "c"))


def start_kernel(n_w, counts, pw, gain, pair, *refs):
    owns, others, spread = refs[:n_w], refs[n_w : 2 * n_w], refs[2 * n_w]
    *stages, x_buf, low_buf, bias_f, bias_v, x_sems, w_send, w_recv, w_keep, b_send, b_recv, b_sem = refs[2 * n_w + 1 :]
    where = coords()
    peers = [across(where, *names) for names in PEERS]
    total = pair.shape[1]
    length, width = pair.shape[2:]
    heads = bias_f.shape[0]
    groups = 2 * total // 8

    def fetch(g, slot):
        return pltpu.make_async_copy(
            pair.at[(g * 8) // total, pl.ds(lax.rem(g * 8, total), 8)], x_buf.at[slot], x_sems.at[slot]
        )

    fetch(0, 0).start()
    greet(peers + [across(where, "z0")])
    movers = [Mover(where, MOVES[i], owns[i], others[i], stages[i], w_send.at[i], w_recv.at[i], w_keep.at[i]) for i in range(n_w)]
    for m in movers:
        m.advance(0)
    for m in movers:
        m.stage(0)

    def group(g, _):
        slot = lax.rem(g, 2)

        @pl.when(g + 1 < groups)
        def _():
            fetch(g + 1, 1 - slot).start()

        fetch(g, slot).wait()
        for r in range(0, 8, 2):
            x_hat, _ = pair_norm(x_buf[slot, r], x_buf[slot, r + 1])
            low_buf[:, r * width : (r + 2) * width] = (x_hat * gain[...]).astype(bf16)
        bias = dot(low_buf[...], pw[...]).T
        limit = counts[(g * 8) // total]
        valid = lax.broadcasted_iota(jnp.int32, bias.shape, 1) < limit
        bias = jnp.where(valid, bias * log2e, mask_fill)
        bias_f[:, pl.ds(pl.multiple_of(g * 8, 8), 8), :] = bias.reshape(heads, 8, length)
        return 0

    third = groups // 3
    for k in range(3):
        lax.fori_loop(k * third, (k + 1) * third, group, 0)
        movers[k].advance(1)
    for m in movers:
        m.stage(1)
    bias_v[...] = bias_f[...].astype(bf16).reshape(bias_v.shape)

    keep = pltpu.make_async_copy(bias_v.at[place(where)], spread.at[place(where)], b_sem)
    keep.start()
    sent = []

    def send_bias():
        for k, peer in enumerate(peers):
            sent.append(remote(bias_v.at[place(peer)], spread.at[place(where)], b_send.at[k], b_recv.at[k], peer))

    for m in movers[3:]:
        m.advance(1)
    for k in range(2, 5):
        for m in movers:
            if k <= len(m.order) + 1:
                m.advance(k)
        if k == 2:
            send_bias()
    keep.wait()
    for copy in sent:
        copy.wait()
    for m in movers:
        m.finish()


def start(counts, pair, pw_big, gain, owns):
    heads, length, width = 16, pair.shape[2], pair.shape[3]
    rows = 2 * pair.shape[1]
    n = len(owns)
    any_spec = pl.BlockSpec(memory_space=pl.ANY)
    vm = pl.BlockSpec(memory_space=pltpu.VMEM)
    return pl.pallas_call(
        functools.partial(start_kernel, n),
        in_specs=[pl.BlockSpec(memory_space=pltpu.SMEM), vm, vm, any_spec] + [any_spec] * n,
        out_specs=[any_spec] * (n + 1),
        out_shape=[jax.ShapeDtypeStruct((2 * w.shape[0], w.shape[1]), bf16) for w in owns]
        + [jax.ShapeDtypeStruct((8, heads // 8, rows, length), bf16)],
        scratch_shapes=[pltpu.VMEM(w.shape, bf16) for w in owns]
        + [
            pltpu.VMEM((2, 8, length, width), bf16),
            pltpu.VMEM((length, 8 * width), bf16),
            pltpu.VMEM((heads, rows, length), f32),
            pltpu.VMEM((8, heads // 8, rows, length), bf16),
            pltpu.SemaphoreType.DMA((2,)),
            pltpu.SemaphoreType.DMA((n, 4)),
            pltpu.SemaphoreType.DMA((n, 4)),
            pltpu.SemaphoreType.DMA((n, 2)),
            pltpu.SemaphoreType.DMA((7,)),
            pltpu.SemaphoreType.DMA((7,)),
            pltpu.SemaphoreType.DMA,
        ],
        compiler_params=pltpu.CompilerParams(vmem_limit_bytes=vmem_bytes, collective_id=2, has_side_effects=True),
        name="start",
    )(counts, pw_big, gain, pair, *owns)


def big_weights(pw):
    width, heads = pw.shape
    eye = jnp.eye(8, dtype=pw.dtype)
    return (eye[:, None, None, :] * pw[None, :, :, None]).reshape(8 * width, heads * 8)


def attend(rb, c, x_ref, y_ref, bias_ref, add):
    length, hd = x_ref.shape[-1], x_ref.shape[-2]
    bz = bias_ref.shape[2]
    k_t, v_t = x_ref[1], x_ref[2]
    v_ext = jnp.concatenate([v_t, jnp.ones((16, length), bf16)], axis=0)
    dv = dk = 0.0
    for r in range(length // rb):
        sl = slice(r * rb, (r + 1) * rb)
        q_t = x_ref[0, :, sl]
        q = q_t.T
        dm = x_ref[3, :, sl].astype(f32).T
        z0 = r * rb // bz
        bias = jnp.concatenate([bias_ref[z0 + t, c].astype(f32) for t in range(rb // bz)], axis=0)
        s = dot(q, k_t) + bias
        e = jnp.exp2(s - jnp.max(s, axis=-1, keepdims=True))
        eb = e.astype(bf16)
        mx = dot_nt(eb, v_ext)
        inv = 1.0 / mx[:, hd : hd + 1]
        mixed = mx[:, :hd] * inv
        d = jnp.sum(mixed * dm, axis=-1, keepdims=True) * inv
        dms = (dm * inv).astype(bf16)
        ds = e * (dot(dms, v_t) - d)
        dsb = ds.astype(bf16)
        add(sl, ds)
        dq = dot_nt(dsb, k_t)
        dv = dv + dot(dms.T, eb)
        dk = dk + dot(q_t, dsb)
        y_ref[0, :, sl] = mixed.T.astype(bf16)
        y_ref[1, :, sl] = (dq * hd**-0.5).T.astype(bf16)
    y_ref[2] = (dk * ln2).astype(bf16)
    y_ref[3] = dv.astype(bf16)


def attn_kernel(rb, owner_ref, x_ref, bias_ref, y_ref, bg_ref, acc_ref):
    n = pl.program_id(0)
    c = owner_ref[n]
    up, bz = bias_ref.shape[0], bias_ref.shape[2]

    @pl.when(n == 0)
    def _():
        acc_ref[...] = jnp.zeros_like(acc_ref)

    def add(sl, ds):
        acc_ref[c, sl, :] += ds

    attend(rb, c, x_ref.at[0], y_ref.at[0], bias_ref, add)

    @pl.when(n == pl.num_programs(0) - 1)
    def _():
        for z in range(up):
            for cc in range(2):
                bg_ref[z, cc] = acc_ref[cc, z * bz : (z + 1) * bz, :].astype(bf16)


def sending_attn_kernel(
    rb, slot, owner_ref, x_ref, bias_ref, y_ref, bg_ref, both, second, x_buf, y_buf, x_sems, y_send, y_recv, y_keep
):
    step = pl.program_id(0)
    steps = pl.num_programs(0)
    where = coords()
    up, bz = bias_ref.shape[0], bias_ref.shape[2]

    def partner(k):
        other = dict(where)
        for name in ("c", "x", "y"):
            axis, value = BITS[name]
            flip = sum(jnp.where(k == i, 1, 0) for i, names in enumerate(SAMPLE_ORDER) if name in names)
            other[axis] = other[axis] + flip * value * (1 - 2 * bit_of(where, name))
        return other

    def fetch(k):
        return pltpu.make_async_copy(
            x_ref.at[place(partner(k)), pl.ds(slot * 4, 4)], x_buf.at[lax.rem(k, 2)], x_sems.at[lax.rem(k, 2)]
        )

    def sent(k, to):
        return pltpu.make_async_remote_copy(
            src_ref=y_buf.at[k],
            dst_ref=y_ref.at[place(to)],
            send_sem=y_send.at[k],
            recv_sem=y_recv.at[k],
            device_id=device(partner(k)),
            device_id_type=MESH,
        )

    keep = pltpu.make_async_copy(y_buf.at[len(PEERS)], y_ref.at[place(where)], y_keep)

    @pl.when(step == 0)
    def _():
        fetch(0).start()
        both[...] = jnp.zeros_like(both)
        second[...] = jnp.zeros_like(second)
        greet([across(where, *names) for names in PEERS])

    @pl.when(step + 1 < steps)
    def _():
        fetch(step + 1).start()

    fetch(step).wait()
    c = owner_ref[place(partner(step))]
    weight = c.astype(f32)

    def add(sl, ds):
        both[sl, :] += ds
        second[sl, :] += ds * weight

    attend(rb, c, x_buf.at[lax.rem(step, 2)], y_buf.at[step], bias_ref, add)

    @pl.when(step < steps - 1)
    def _():
        sent(step, where).start()

    @pl.when(step == steps - 1)
    def _():
        keep.start()
        for z in range(up):
            sl = slice(z * bz, (z + 1) * bz)
            bg_ref[z, 0] = (both[sl, :] - second[sl, :]).astype(bf16)
            bg_ref[z, 1] = second[sl, :].astype(bf16)
        keep.wait()
        for k in range(len(PEERS)):
            sent(k, partner(k)).wait_recv()
            sent(k, where).wait_send()


def sending_attention(owner, x, bias, slot):
    n, _, hd, length = x.shape
    any_spec = pl.BlockSpec(memory_space=pl.ANY)
    vm = pl.BlockSpec(memory_space=pltpu.VMEM)
    return pl.pallas_call(
        functools.partial(sending_attn_kernel, length // 2, slot),
        grid=(n,),
        in_specs=[pl.BlockSpec(memory_space=pltpu.SMEM), any_spec, vm],
        out_specs=[any_spec, vm],
        out_shape=[jax.ShapeDtypeStruct((n, 4, hd, length), bf16), jax.ShapeDtypeStruct(bias.shape, bf16)],
        scratch_shapes=[
            pltpu.VMEM((length, length), f32),
            pltpu.VMEM((length, length), f32),
            pltpu.VMEM((2, 4, hd, length), bf16),
            pltpu.VMEM((n, 4, hd, length), bf16),
            pltpu.SemaphoreType.DMA((2,)),
            pltpu.SemaphoreType.DMA((n,)),
            pltpu.SemaphoreType.DMA((n,)),
            pltpu.SemaphoreType.DMA,
        ],
        compiler_params=params(collective_id=3 + slot, has_side_effects=True),
        cost_estimate=pl.CostEstimate(
            flops=12 * n * length * length * 256, bytes_accessed=x.size * 2 + bias.size * 4, transcendentals=n * length * length
        ),
        name="attention_and_send",
    )(owner, x, bias)


def attention(owner, x, bias, slot):
    n, _, hd, length = x.shape
    four = 4
    return pl.pallas_call(
        functools.partial(attn_kernel, length // 2),
        grid_spec=pltpu.PrefetchScalarGridSpec(
            num_scalar_prefetch=1,
            grid=(n,),
            in_specs=[
                pl.BlockSpec((1, four, hd, length), lambda i, _: (i, slot, 0, 0)),
                pl.BlockSpec(bias.shape, lambda i, _: (0, 0, 0, 0)),
            ],
            out_specs=[
                pl.BlockSpec((1, four, hd, length), lambda i, _: (i, 0, 0, 0)),
                pl.BlockSpec(bias.shape, lambda i, _: (0, 0, 0, 0)),
            ],
            scratch_shapes=[pltpu.VMEM((2, length, length), f32)],
        ),
        out_shape=[jax.ShapeDtypeStruct((n, four, hd, length), bf16), jax.ShapeDtypeStruct(bias.shape, bf16)],
        compiler_params=params(),
        cost_estimate=pl.CostEstimate(
            flops=12 * n * length * length * 256, bytes_accessed=x.size * 2 + bias.size * 4, transcendentals=n * length * length
        ),
        name="attention",
    )(owner, x, bias)


def front_kernel(
    tok, cond, og, cgain, wc, cb, wq, qb, wo,
    *outs,
):
    x_o, sg_o, gg_o, s1_o, g1_o, first_o = outs
    width = tok.shape[-1]
    hd = width // head_count
    peers = x_o.shape[0]
    slots = head_count // peers
    cond_low = (norm_parts(cond[...].astype(f32))[0] * cgain[...]).astype(bf16)
    modul = dot(cond_low, wc[...]) + cb[...]
    s1 = jax.nn.sigmoid(modul[:, :width])
    g1 = jax.nn.sigmoid(modul[:, 2 * width :])
    tn, _ = norm_parts(tok[...].astype(f32))
    first = (s1 * tn + modul[:, width : 2 * width]).astype(bf16)
    proj = dot(first, wq[...])
    q = (proj[:, :width] + qb[...]) * (hd**-0.5 * log2e)
    sg = jax.nn.sigmoid(proj[:, 3 * width :])
    ga = (og[...].astype(f32) * g1).astype(bf16)
    gg = dot_nt(ga, wo[...])
    dm = sg * gg
    sg_o[...] = sg.astype(bf16)
    gg_o[...] = gg.astype(bf16)
    s1_o[...] = s1.astype(bf16)
    g1_o[...] = g1.astype(bf16)
    first_o[...] = first
    for i, part in enumerate((q, proj[:, width : 2 * width], proj[:, 2 * width : 3 * width], dm)):
        turned = part.T.astype(bf16).reshape(peers, slots, hd, part.shape[0])
        for t in range(slots):
            x_o[:, t * 4 + i] = turned[:, t]


def half_spec(a, h):
    return pl.BlockSpec((a.shape[0], a.shape[1] // 2), lambda *_: (0, h))


def row_spec(a, rb):
    return pl.BlockSpec((rb, a.shape[1]), lambda i, *_: (i, 0))


def front(tok, cond, og, cgain, wc, cb, wq, qb, wo, slots):
    length, width = tok.shape
    rb = 384
    peers, hd = head_count // slots, width // head_count
    small = jax.ShapeDtypeStruct((length, width), bf16)
    payload = jax.ShapeDtypeStruct((peers, 4 * slots, hd, length), bf16)
    return pl.pallas_call(
        front_kernel,
        grid_spec=pl.GridSpec(
            grid=(length // rb,),
            in_specs=[row_spec(tok, rb), row_spec(cond, rb), row_spec(og, rb)]
            + [whole(cgain)]
            + [half_spec(wc, 0)]
            + [whole(a) for a in (cb, wq, qb, wo)],
            out_specs=[pl.BlockSpec((peers, 4 * slots, hd, rb), lambda i: (0, 0, 0, i))] + [row_spec(tok, rb)] * 5,
        ),
        out_shape=[payload] + [small] * 5,
        compiler_params=params(),
        cost_estimate=pl.CostEstimate(flops=2 * length * width * width * 7, bytes_accessed=20 << 20, transcendentals=length * width * 4),
        name="front",
    )(tok, cond, og, cgain, wc, cb, wq, qb, wo)


def trans_kernel(
    tok, cond, og, cgain, wc, cb, wu, wd,
    part_o, u2_o, dcond_o, ml_o, cn_o, second_o, hid_o, act_o, gt_o, cbg_o,
):
    width = tok.shape[-1]
    cond_low = (norm_parts(cond[...].astype(f32))[0] * cgain[...]).astype(bf16)
    cn_o[...] = cond_low
    modul = dot(cond_low, wc[...]) + cb[...]
    s2 = jax.nn.sigmoid(modul[:, :width])
    g2 = jax.nn.sigmoid(modul[:, 2 * width :])
    tokens = tok[...].astype(f32)
    tn, _ = norm_parts(tokens)
    second = (s2 * tn + modul[:, width : 2 * width]).astype(bf16)
    second_o[...] = second
    hidden = dot(second, wu[...])
    ff = hidden.shape[1] // 2
    h_gate, h_up = hidden[:, :ff], hidden[:, ff:]
    sig = jax.nn.sigmoid(h_gate)
    silu = h_gate * sig
    act = (silu * h_up).astype(bf16)
    act_o[...] = act
    trans_out = dot(act, wd[...])
    part_o[...] = tokens + g2 * trans_out
    g = og[...].astype(f32)
    gt = (g * g2).astype(bf16)
    gt_o[...] = gt
    grad_act = dot_nt(gt, wd[...])
    hid = jnp.concatenate(
        [(grad_act * h_up * (sig * (1.0 + h_gate * (1.0 - sig)))).astype(bf16), (grad_act * silu).astype(bf16)], axis=-1
    )
    hid_o[...] = hid
    grad_second = dot_nt(hid, wu[...])
    u2_o[...] = (grad_second * s2).astype(bf16)
    grads = jnp.concatenate(
        [grad_second * tn * (s2 * (1.0 - s2)), grad_second, g * trans_out * (g2 * (1.0 - g2))], axis=-1
    )
    low = grads.astype(bf16)
    ml_o[...] = low

    @pl.when(pl.program_id(0) == 0)
    def _():
        cbg_o[...] = jnp.zeros_like(cbg_o)

    cbg_o[...] += jnp.sum(grads, axis=0, keepdims=True)
    dcond_o[...] = dot_nt(low, wc[...])


def transition(tok, cond, og, cgain, wc, cb, wu, wd):
    length, width = tok.shape
    rb = 384
    cs, mw = cond.shape[1], cb.shape[1]
    ff2 = wu.shape[1]

    def out(w, dtype):
        return jax.ShapeDtypeStruct((length, w), dtype)

    shapes = [
        out(width, f32), out(width, bf16), out(cs, f32), out(mw, bf16), out(cs, bf16), out(width, bf16),
        out(ff2, bf16), out(ff2 // 2, bf16), out(width, bf16),
    ]
    return pl.pallas_call(
        trans_kernel,
        grid_spec=pl.GridSpec(
            grid=(length // rb,),
            in_specs=[row_spec(tok, rb), row_spec(cond, rb), row_spec(og, rb)]
            + [whole(cgain)]
            + [half_spec(wc, 1)]
            + [whole(a) for a in (cb, wu, wd)],
            out_specs=[row_spec(s, rb) for s in shapes] + [pl.BlockSpec((1, mw), lambda i: (0, 0))],
        ),
        out_shape=shapes + [jax.ShapeDtypeStruct((1, mw), f32)],
        compiler_params=params(),
        cost_estimate=pl.CostEstimate(flops=2 * length * width * width * 15, bytes_accessed=40 << 20, transcendentals=length * width * 6),
        name="transition",
    )(tok, cond, og, cgain, wc, cb, wu, wd)


def back_kernel(slots, *refs):
    ys = refs[:slots]
    (
        sg, gg, s1, g1, part, u2, dcond2, tok, cond, og, cbg2, cgain, wc, wq, wo,
        out_o, tg_o, cg_o, gated_o, ga_o, gp_o, ml_o, small_o,
    ) = refs[slots:]
    rb, width = tok.shape
    hd = width // head_count
    peers = head_count // slots

    def heads(i):
        stacked = jnp.stack([y[:, i] for y in ys], axis=1)
        return stacked.reshape(width, rb).astype(f32).T

    mixed = heads(0)
    sgv = sg[...].astype(f32)
    g1v = g1[...].astype(f32)
    gated = (sgv * mixed).astype(bf16)
    gated_o[...] = gated
    attn_out = dot(gated, wo[...])
    out_o[...] = part[...] + g1v * attn_out
    g = og[...].astype(f32)
    ga_o[...] = (g * g1v).astype(bf16)
    dg = gg[...].astype(f32) * mixed * (sgv * (1.0 - sgv))
    dq = heads(1)
    grad_proj = jnp.concatenate([dq.astype(bf16), heads(2).astype(bf16), heads(3).astype(bf16), dg.astype(bf16)], axis=-1)
    gp_o[...] = grad_proj
    grad_first = dot_nt(grad_proj, wq[...])
    s1v = s1[...].astype(f32)
    tn, tscale = norm_parts(tok[...].astype(f32))
    grads = jnp.concatenate(
        [grad_first * tn * (s1v * (1.0 - s1v)), grad_first, g * attn_out * (g1v * (1.0 - g1v))], axis=-1
    )
    low = grads.astype(bf16)
    ml_o[...] = low
    tg_o[...] = g + norm_back(tn, grad_first * s1v + u2[...].astype(f32), tscale)
    dcond = dot_nt(low, wc[...]) + dcond2[...]
    cx, cscale = norm_parts(cond[...].astype(f32))
    cg_o[...] = norm_back(cx, dcond * cgain[...], cscale)

    step = pl.program_id(0)

    @pl.when(step == 0)
    def _():
        small_o[...] = jnp.zeros_like(small_o)

    row = 0
    last = jnp.where(step == pl.num_programs(0) - 1, 1.0, 0.0)
    for values in (
        jnp.sum(dcond * cx, axis=0, keepdims=True),
        jnp.sum(grads, axis=0, keepdims=True),
        cbg2[...] * last,
        jnp.sum(dq, axis=0, keepdims=True),
    ):
        for k in range(values.shape[1] // 128):
            small_o[row : row + 1, :] += values[:, k * 128 : (k + 1) * 128]
            row += 1


def back(ys, sg, gg, s1, g1, part, u2, dcond2, tok, cond, og, cbg2, cgain, wc, wq, wo):
    length, width = tok.shape
    rb = 384
    cs, mw = cond.shape[1], wc.shape[1] // 2
    rows = (sg, gg, s1, g1, part, u2, dcond2, tok, cond, og)
    consts = (wq, wo)

    def out(w, dtype):
        return jax.ShapeDtypeStruct((length, w), dtype)

    shapes = [
        out(width, f32), out(width, f32), out(cs, f32), out(width, bf16), out(width, bf16), out(wq.shape[1], bf16), out(mw, bf16),
    ]
    used = (width + 2 * mw + cs) // 128
    small = [jax.ShapeDtypeStruct((-(-used // 8) * 8 + head_count, 128), f32)]
    return pl.pallas_call(
        functools.partial(back_kernel, len(ys)),
        grid_spec=pl.GridSpec(
            grid=(length // rb,),
            in_specs=[pl.BlockSpec(y.shape[:3] + (rb,), lambda i: (0, 0, 0, i)) for y in ys]
            + [row_spec(a, rb) for a in rows]
            + [whole(cbg2), whole(cgain)]
            + [half_spec(wc, 0)]
            + [whole(a) for a in consts],
            out_specs=[row_spec(s, rb) for s in shapes] + [pl.BlockSpec(s.shape, lambda i: (0, 0)) for s in small],
        ),
        out_shape=shapes + small,
        compiler_params=params(),
        cost_estimate=pl.CostEstimate(flops=2 * length * width * width * 7, bytes_accessed=40 << 20, transcendentals=length * width),
        name="back",
    )(*ys, *rows, cbg2, cgain, wc, *consts)


def wgrad_kernel(steps, lhs, *refs):
    *rhs, out_ref, turned = refs
    step = pl.program_id(0)

    @pl.when(step == 0)
    def _():
        turned[...] = lhs[...].T

    for k, r in enumerate(rhs):

        @pl.when(step // steps == k)
        def _():
            out_ref[...] = dot(turned[...], r[...]).astype(bf16).reshape(out_ref.shape)


def wgrad(lhs, *rhs):
    length, k = lhs.shape
    n = sum(r.shape[1] for r in rhs)
    row_groups = k // 96
    col_groups = 16 // row_groups
    piece = n // col_groups
    cols = piece if piece <= 1536 else piece // 2
    steps = n // cols
    each = steps // len(rhs)
    per = piece // cols

    def rhs_spec(t):
        return pl.BlockSpec((length, cols), lambda i: (0, jnp.clip(i - t * each, 0, each - 1)))

    return pl.pallas_call(
        functools.partial(wgrad_kernel, each),
        grid=(steps,),
        in_specs=[whole(lhs)] + [rhs_spec(t) for t in range(len(rhs))],
        out_specs=pl.BlockSpec((2, row_groups, 48, cols), lambda i: (0, i // per, 0, i % per)),
        out_shape=jax.ShapeDtypeStruct((2, 16, 48, piece), bf16),
        scratch_shapes=[pltpu.VMEM((k, length), bf16)],
        compiler_params=params(),
        cost_estimate=pl.CostEstimate(flops=2 * length * k * n, bytes_accessed=2 * (length * (k + n) + k * n), transcendentals=0),
        name="wgrad",
    )(lhs, *rhs)


class Reducer:
    stages = 10

    def __init__(self, where, plan, ins, outs, xs, rs, load_sems, send_sems, recv_sems, keep_sems):
        self.where, self.plan, self.ins, self.outs, self.xs, self.rs = where, plan, ins, outs, xs, rs
        self.load_sems, self.send_sems, self.recv_sems, self.keep_sems = load_sems, send_sems, recv_sems, keep_sems
        n = len(plan)
        self.base, self.size, self.off, self.pending = [0] * n, [32] * n, [0] * n, [None] * n
        self.sends = []
        self.loads = [self.load(i) if ins else [] for i in range(n)]

    @staticmethod
    def scratch(plan):
        n = len(plan)
        return (
            [pltpu.VMEM((32, 48, w), bf16) for _, _, w, _, _ in plan]
            + [pltpu.VMEM((31, 48, w), bf16) for _, _, w, _, _ in plan]
            + [pltpu.SemaphoreType.DMA((n, 16))]
            + [pltpu.SemaphoreType.DMA((n, 9))] * 2
            + [pltpu.SemaphoreType.DMA((n,))]
        )

    def load(self, i):
        a, c0, w, order, _ = self.plan[i]
        at = SUM_ORDERS[order].index("y")
        run = 32 >> (at + 1)
        copies = []
        for b in range(1 << at):
            for f in range(2):
                copy = pltpu.make_async_copy(
                    self.ins[a].at[f, pl.ds(b * run, run), :, pl.ds(c0, w)],
                    self.xs[i].at[pl.ds((b * 2 + f) * run, run)],
                    self.load_sems.at[i, b * 2 + f],
                )
                copy.start()
                copies.append(copy)
        return copies

    def store(self, i, first_piece, rows):
        order = self.plan[i][3]
        low = 4 - SUM_ORDERS[order].index("y")
        row_groups = rows.shape[0] // 96
        for f in range(2):
            for g in range(row_groups):
                p = first_piece + g
                at = ((p >> low) * 2 + f) << low | p & ((1 << low) - 1)
                r0 = (f * row_groups + g) * 48
                self.xs[i][at] = rows[r0 : r0 + 48, :]

    def send(self, i, k, src, dst, name):
        copy = remote(src, dst, self.send_sems.at[i, k], self.recv_sems.at[i, k], across(self.where, name))
        self.sends.append(copy)
        self.pending[i] = copy

    def sum_start(self, i, k):
        name = SUM_ORDERS[self.plan[i][3]][k]
        half = self.size[i] // 2
        b = bit_of(self.where, name)
        src = self.xs[i].at[pl.ds(self.base[i] + (1 - b) * half, half)]
        self.send(i, k, src, self.rs[i].at[pl.ds(self.off[i], half)], name)
        self.base[i] = self.base[i] + b * half
        self.size[i] = half

    def sum_finish(self, i):
        self.pending[i].wait_recv()
        half, b0, r0 = self.size[i], self.base[i], self.off[i]
        x, r = self.xs[i], self.rs[i]

        def body(j, _):
            x[b0 + j] = (x[b0 + j].astype(f32) + r[r0 + j].astype(f32)).astype(bf16)
            return 0

        lax.fori_loop(0, half, body, 0)
        self.off[i] = r0 + half

    def block(self, i, done):
        a, c0, w, order, _ = self.plan[i]
        at = [
            slice(None) if name in done else bit_of(self.where, name) for name in SUM_ORDERS[order] if name != "y"
        ]
        return self.outs[a].at[(*at, slice(None), pl.ds(c0, w))]

    def copy_start(self, i, j):
        names = COPY_ORDERS[self.plan[i][4]]
        ref = self.block(i, names[:j])
        self.send(i, 5 + j, ref, ref, names[j])

    def advance(self, i, k):
        if k == 0:
            for copy in self.loads[i]:
                copy.wait()
            self.sum_start(i, 0)
        elif k < 5:
            self.sum_finish(i)
            self.sum_start(i, k)
        elif k == 5:
            self.sum_finish(i)
            keep = pltpu.make_async_copy(self.xs[i].at[self.base[i]], self.block(i, ()), self.keep_sems.at[i])
            keep.start()
            keep.wait()
            self.copy_start(i, 0)
        else:
            self.pending[i].wait_recv()
            if k < 9:
                self.copy_start(i, k - 5)

    def finish(self):
        for copy in self.sends:
            copy.wait_send()


class SmallSum:
    def __init__(self, where, buf, send_sems, recv_sems):
        self.where, self.buf, self.send_sems, self.recv_sems = where, buf, send_sems, recv_sems
        self.copies = []

    def advance(self, k):
        if k > 0:
            self.copies[k - 1].wait_recv()
            self.buf[2 * k] = self.buf[2 * k - 2] + self.buf[2 * k - 1]
        if k < 5:
            src, dst = self.buf.at[2 * k], self.buf.at[2 * k + 1]
            self.copies.append(
                remote(src, dst, self.send_sems.at[k], self.recv_sems.at[k], across(self.where, list(BITS)[k]))
            )


class BiasHome:
    def __init__(self, where, raw, done, home_out, home, kept, got, last, done_v, out, load_sems, send_sems, recv_sems):
        self.where, self.raw, self.home, self.kept, self.got, self.last = where, raw, home, kept, got, last
        self.done_v, self.out, self.send_sems, self.recv_sems = done_v, out, send_sems, recv_sems
        self.z0, self.z1 = bit_of(where, "z0"), bit_of(where, "z1")
        self.loads = [
            pltpu.make_async_copy(raw.at[:, self.z0], kept, load_sems.at[0]),
            pltpu.make_async_copy(done, done_v, load_sems.at[1]),
        ]
        self.keep = pltpu.make_async_copy(out.at[place(where)], home.at[place(where)], load_sems.at[2])
        self.written = pltpu.make_async_copy(home, home_out, load_sems.at[3])
        self.copies = []

    @staticmethod
    def scratch(block, members):
        plane, length = block[1], block[2]
        rows = pltpu.VMEM((members, 2, 2 * plane // members, length), bf16)
        return [
            rows,
            pltpu.VMEM((2,) + block, bf16),
            pltpu.VMEM((2,) + block, bf16),
            pltpu.VMEM(block, bf16),
            pltpu.VMEM(block, bf16),
            rows,
            pltpu.SemaphoreType.DMA((4,)),
            pltpu.SemaphoreType.DMA((2 + len(PEERS),)),
            pltpu.SemaphoreType.DMA((2 + len(PEERS),)),
        ]

    def send(self, k, src, dst, other):
        self.copies.append(remote(src, dst, self.send_sems.at[k], self.recv_sems.at[k], other))

    def lay(self, slot, value):
        members, _, rows, _ = self.out.shape
        each = rows // 2
        for m in range(members):
            part = [value[c, m * each : (m + 1) * each, :] for c in range(2)]
            self.out[m, slot] = jnp.concatenate(part, axis=0).astype(bf16)

    def advance(self, k):
        if k == 0:
            self.send(0, self.raw.at[:, 1 - self.z0], self.got, across(self.where, "z0"))
        elif k == 1:
            self.loads[0].wait()
            self.copies[0].wait_recv()
            self.kept[...] = (self.kept[...].astype(f32) + self.got[...].astype(f32)).astype(bf16)
            self.send(1, self.kept.at[1 - self.z1], self.last, across(self.where, "z1"))
            self.loads[1].wait()
            self.lay(0, self.done_v[...].astype(f32))
        elif k == 2:
            self.copies[1].wait_recv()
            self.lay(1, self.kept[self.z1].astype(f32) + self.last[...].astype(f32))
            for j, names in enumerate(PEERS):
                peer = across(self.where, *names)
                self.send(2 + j, self.out.at[place(peer)], self.home.at[place(self.where)], peer)
            self.keep.start()
        elif k == 3:
            self.keep.wait()
            for copy in self.copies[2:]:
                copy.wait_recv()
            self.written.start()


def reduce_kernel(n_left, *refs):
    refs = list(refs)

    def take(n):
        out, refs[:] = refs[:n], refs[n:]
        return out

    early_in, acts, (raw, done, pair), (small, small_o) = take(2), take(7), take(3), take(2)
    late_out, early_out, (home,) = take(3), take(2), take(1)
    n_late, n_early = len(late_plan), len(early_plan)
    late_scratch, early_scratch = take(2 * n_late + 4), take(2 * n_early + 4)
    bufs, (sbuf, s_send, s_recv, a_sems) = take(7), take(4)
    where = coords()
    bias = BiasHome(where, raw, done, home, *take(9))
    (moment_buf, p_sems) = take(2)
    loads = [pltpu.make_async_copy(src, dst, a_sems.at[i]) for i, (src, dst) in enumerate(zip(acts, bufs))]

    def reducer(plan, ins, outs, scratch):
        n = len(plan)
        return Reducer(where, plan, ins, outs, scratch[:n], scratch[n : 2 * n], *scratch[2 * n :])

    early = reducer(early_plan, early_in, early_out, early_scratch)
    for copy in loads:
        copy.start()
    late = reducer(late_plan, None, late_out, late_scratch)
    for copy in bias.loads:
        copy.start()
    sbuf[0] = small[...]
    greet([across(where, *names) for names in PEERS + (("z0",), ("z1",))])
    small_sum = SmallSum(where, sbuf, s_send, s_recv)
    bias.advance(0)

    first, gp, cn, ml1, ml2, gated, ga = bufs
    sides = ((first, (gp,)), (cn, (ml1, ml2)), (gated, (ga,)))
    turned = {}
    waited = set()

    def ready(k):
        if k not in waited:
            loads[k].wait()
            waited.add(k)

    def multiply(i):
        a, c0, w, _, _ = late_plan[i]
        lhs, rhs = sides[a]
        k0 = (0, 2, 5)[a]
        for k in range(k0, k0 + 1 + len(rhs)):
            ready(k)
        if a not in turned:
            turned[a] = lhs[...].T
        row_groups = turned[a].shape[0] // 96
        total = sum(r.shape[1] for r in rhs)
        piece = total * row_groups // 16
        for g in range(16 // row_groups):
            c = g * piece
            r = rhs[c // rhs[0].shape[1]]
            c = c % rhs[0].shape[1] + c0
            late.store(i, g * row_groups, dot(turned[a], r[:, c : c + w]).astype(bf16))

    pair_rows, length, width = pair.shape[1:]
    heads = bias.home.shape[0] * bias.home.shape[1]

    def pair_copy(c, r):
        return pltpu.make_async_copy(pair.at[c, r], gp.at[:, pl.ds(r * width, width)], p_sems.at[r])

    def moments(c):
        for r in range(pair_rows):
            pair_copy(c, r).wait()
        for r in range(0, pair_rows, 2):
            cols = slice(r * width, (r + 2) * width)
            gp[:, cols] = pair_norm(gp[:, cols])[0].astype(bf16)
        total = 0.0
        for g in range(0, pair_rows, 8):
            grads = bias.home[...].astype(f32)[:, :, c * pair_rows + g : c * pair_rows + g + 8, :]
            total += dot(grads.reshape(heads * 8, length).astype(bf16), gp[:, g * width : (g + 8) * width])
        if c == 0:
            for r in range(pair_rows):
                pair_copy(1, r).start()
            moment_buf[...] = total
        else:
            total = total + moment_buf[...]
            row = lax.rem(lax.broadcasted_iota(jnp.int32, (heads * 8, width), 0), 8)
            own = sum(jnp.where(row == r, total[:, r * width : (r + 1) * width], 0.0) for r in range(8))
            sbuf[0, small.shape[0] - heads :, :] = jnp.sum(own.reshape(heads, 8, width), axis=1)

    stage = {}
    multiplied = 0
    for at, s in enumerate(schedule):
        k = stage.get(s, 0)
        stage[s] = k + 1
        if s == -2:
            small_sum.advance(k)
        elif s == -1:
            bias.advance(k + 1)
            if k > 1:
                moments(k - 2)
        elif s < n_late:
            if k == 0:
                multiply(s)
                multiplied += late_plan[s][0] == 0
                if late_plan[s][0] == 0 and multiplied == sum(p[0] == 0 for p in late_plan):
                    for r in range(pair_rows):
                        pair_copy(0, r).start()
            late.advance(s, k)
        else:
            early.advance(s - n_late, k)
    bias.written.wait()
    small_o[...] = sbuf[10]
    for copy in late.sends + early.sends + small_sum.copies + bias.copies:
        copy.wait_send()


def reduce_all(early, acts, raw, done, pair, small):
    raw = raw.reshape((2, 2) + raw.shape[1:])
    block = done.shape
    members = group_size
    widths = (1536, 1152, 384, 1536, 768)
    shapes = [jax.ShapeDtypeStruct((2, 2, 2, 2, 48, w), bf16) for w in widths]
    any_spec = pl.BlockSpec(memory_space=pl.ANY)
    vm = pl.BlockSpec(memory_space=pltpu.VMEM)
    return pl.pallas_call(
        functools.partial(reduce_kernel, None),
        out_shape=[jax.ShapeDtypeStruct(small.shape, f32)]
        + shapes
        + [jax.ShapeDtypeStruct((members, 2, 2 * block[1] // members, block[2]), bf16)],
        in_specs=[any_spec] * (len(early) + len(acts) + 3) + [vm],
        out_specs=[vm] + [any_spec] * (len(shapes) + 1),
        scratch_shapes=Reducer.scratch(late_plan)
        + Reducer.scratch(early_plan)
        + [pltpu.VMEM(a.shape, bf16) for a in acts]
        + [
            pltpu.VMEM((11,) + small.shape, f32),
            pltpu.SemaphoreType.DMA((5,)),
            pltpu.SemaphoreType.DMA((5,)),
            pltpu.SemaphoreType.DMA((len(acts),)),
        ]
        + BiasHome.scratch(block, members)
        + [pltpu.VMEM((2 * members * 8, 8 * pair.shape[3]), f32), pltpu.SemaphoreType.DMA((pair.shape[1],))],
        compiler_params=params(collective_id=1, has_side_effects=True),
        name="reduce_grads",
    )(*early, *acts, raw, done, pair, small)


late_plan = (
    (0, 0, 1024, 3, 1),
    (0, 1024, 512, 0, 3),
    (1, 0, 640, 0, 0),
    (1, 640, 512, 2, 1),
    (2, 0, 384, 2, 2),
)
early_plan = (
    (0, 0, 768, 1, 3),
    (0, 768, 768, 0, 2),
    (1, 0, 768, 2, 2),
)
schedule = (
    5, 2, 7, 5, 0, 2, 6, 7, 4, 1, 4, 0, 5, -1, 6, 3, 2, 3, 1, 2, 6, 7, 4, 5,
    3, 4, 0, 2, 6, 5, 1, 4, 1, -1, 5, 6, 7, 3, 6, 1, 5, 7, 3, 2, 0, 6, 1, 3,
    7, 1, 0, 5, 6, -1, 4, 0, 5, 3, 7, 2, -1, 4, -2, 0, 7, 3, -2, 1, 3, 0, -2, 2,
    5, 6, 1, 4, 7, 6, 4, -2, 3, 0, -2, 2, -2, 2, 0, 4, 1, 7,
)


def on_device(
    tokens, cond, pair, counts, owner, out_grad, cond_gain, cond_weight, cond_bias, qkvg_weight, query_bias,
    out_weight, pair_gain, pair_weight, up_weight, down_weight,
):
    ups, los, ffs = lax.axis_size("up"), lax.axis_size("lo"), lax.axis_size("fsdp")
    plane = ("lo", "fsdp")
    members = los * ffs
    slots = head_count // members
    length, width = tokens.shape[1:]
    rows = pair.shape[1]
    direct = ffs == 2 and los == 4 and ups == 4

    wide = 3 * width

    def spread(got):
        mine = got.reshape(members, 2, rows, length).transpose(1, 0, 2, 3).reshape(2, members * rows, length)
        return lax.all_gather(mine, "up", axis=0, tiled=False)

    matrices = (cond_weight, qkvg_weight, out_weight, up_weight, down_weight)
    if direct:
        wc, wq, wo, wu, wd, spreads = start(
            counts, pair, big_weights(pair_weight), jnp.tile(pair_gain, 2)[None], matrices
        )
    else:
        bias = pair_fwd(counts, pair, pair_weight.T, pair_gain[None])
        bias = bias.reshape(members, slots, 2 * rows, length)
        spreads = lax.all_to_all(bias, plane, 0, 0, tiled=True)
        wc, wq, wo, wu, wd = [lax.all_gather(w, "fsdp", axis=0, tiled=True) for w in matrices]
    biases = [spread(spreads[:, t]) for t in range(slots)]

    pw = pair_weight.astype(f32).T
    bwd_weights = pair_bwd_weights(rows, pw, pair_gain)
    tok, cnd, og = tokens[0], cond[0], out_grad[0]
    cgain = cond_gain[None]
    x, sg, gg, s1, g1, first = front(
        tok, cnd, og, cgain, wc, cond_bias[None, :wide], wq, query_bias[None], wo, slots
    )
    x = lax.all_to_all(x, plane, 0, 0, tiled=True)
    part, u2, dcond2, ml2, cn, second, hid, act, gt, cbg2 = transition(
        tok, cnd, og, cgain, wc, cond_bias[None, wide:], wu, wd
    )
    def fold(g):
        k, n = g.shape
        if k == width:
            return g
        if k > width:
            times = k // width
            parts = g.reshape(ffs, times, width // ffs, n)
            return jnp.concatenate([parts[:, t] for t in range(times)], axis=-1).reshape(width, n * times)
        times = width // k
        parts = g.reshape(ffs, k // ffs, times, n // times)
        return jnp.concatenate([parts[:, :, t] for t in range(times)], axis=1).reshape(width, n // times)

    def unfold(h, k, n):
        rows_each = width // ffs
        if k == width:
            return h
        if k > width:
            times = k // width
            return jnp.concatenate([h[:, t * n : (t + 1) * n] for t in range(times)], axis=0)
        times = width // k
        step = rows_each // times
        return jnp.concatenate([h[t * step : (t + 1) * step] for t in range(times)], axis=1)

    def reduced(grads):
        folded = [fold(g) for g in grads]
        mine = lax.psum_scatter(
            jnp.concatenate(folded, axis=1), ("fsdp", "up", "lo"), scatter_dimension=0, tiled=True
        )
        full = lax.all_gather(mine, ("up", "lo"), axis=0, tiled=True)
        outs, at = [], 0
        for g, h in zip(grads, folded):
            outs.append(unfold(full[:, at : at + h.shape[1]], *g.shape).astype(f32))
            at += h.shape[1]
        return outs

    if direct:
        early = [wgrad(second, hid), wgrad(act, gt)]
        x, bwd_weights, *early = lax.optimization_barrier((x, bwd_weights, *early))
    else:
        up_total, down_total = reduced([dot_tn(second, hid).astype(bf16), dot_tn(act, gt).astype(bf16)])

    owners = lax.dynamic_slice_in_dim(owner, lax.axis_index("up") * members, members)
    ys, bias_grads = [], []
    for t in range(slots):
        if direct:
            y, bg = sending_attention(owners, x, biases[t], t)
        else:
            y, bg = attention(owners, x, biases[t], t)
            y = lax.all_to_all(y, plane, 0, 0, tiled=True)
        ys.append(y)
        if direct and t == slots - 1:
            bias_grads.append(bg)
            continue
        mine = lax.psum_scatter(bg, "up", scatter_dimension=0, tiled=True)
        bias_grads.append(mine.reshape(2, members * rows, length))

    block_out, tokens_grad, cond_grad, gated, ga, gp, ml1, stacked = back(
        ys, sg, gg, s1, g1, part, u2, dcond2, tok, cnd, og, cbg2, cgain, wc, wq, wo
    )
    if not direct:
        ml = jnp.concatenate([ml1, ml2], axis=1)
        qkvg_total, out_total, cond_total = reduced(
            [dot_tn(first, gp).astype(bf16), dot_tn(gated, ga).astype(bf16), dot_tn(cn, ml).astype(bf16)]
        )

    if direct:
        stacked, *totals, bias_grad = reduce_all(
            early, (first, gp, cn, ml1, ml2, gated, ga), bias_grads[1], bias_grads[0], pair, stacked
        )
    else:
        stacked = lax.psum(stacked, ("up", "lo", "fsdp"))
        split = [b.reshape(2, members, rows, length).transpose(1, 0, 2, 3) for b in bias_grads]
        bias_grad = lax.all_to_all(jnp.stack(split, axis=1), plane, 0, 0, tiled=True)
    bias_grad = bias_grad.reshape(head_count, 2, rows, length)
    if direct:
        heights = [w.shape[0] for w in (qkvg_weight, cond_weight, out_weight, up_weight, down_weight)]
        smalls = (stacked, pw, pair_gain[None], pair_gain[None])
        sizes = (cond_gain.shape, cond_bias.shape, query_bias.shape, pair_gain.shape, pw.shape)
        pair_grad, laid, vectors = pair_bwd(pair, bias_grad, bwd_weights, totals, heights, smalls, sizes)
        vectors[4] = vectors[4].T
        qkvg_total, cond_total, out_total, up_total, down_total = laid
    else:
        pair_grad, moments = pair_bwd(pair, bias_grad, bwd_weights)
    moments = stacked[-head_count:] if direct else lax.psum(moments, ("up", "lo", "fsdp"))
    if not direct:
        small = stacked.reshape(-1)
        ends = [0, cond_gain.size, cond_gain.size + cond_bias.size, cond_gain.size + cond_bias.size + query_bias.size]
        vectors = [small[a:b] for a, b in zip(ends[:-1], ends[1:])]
        vectors += [jnp.sum(pw * moments, axis=0), (moments * pair_gain).T]
    return (
        block_out[None],
        tokens_grad[None],
        cond_grad[None],
        pair_grad,
        vectors[0],
        cond_total,
        vectors[1],
        qkvg_total,
        vectors[2],
        out_total,
        vectors[3],
        vectors[4],
        up_total,
        down_total,
    )


def solution(mesh):
    dp, fsdp = mesh.shape["dp"], mesh.shape["fsdp"]
    lo = max(1, group_size // fsdp)
    fine = Mesh(mesh.devices.reshape(dp // lo, lo, fsdp), ("up", "lo", "fsdp"))
    every = ("up", "lo", "fsdp")
    in_specs = (
        P(every, None, None),
        P(every, None, None),
        P(None, every, None, None),
        P(),
        P(),
        P(every, None, None),
        P(),
        P("fsdp", None),
        P(),
        P("fsdp", None),
        P(),
        P("fsdp", None),
        P(),
        P(),
        P("fsdp", None),
        P("fsdp", None),
    )
    out_specs = (
        P(every, None, None),
        P(every, None, None),
        P(every, None, None),
        P(None, every, None, None),
        P(),
        P("fsdp", None),
        P(),
        P("fsdp", None),
        P(),
        P("fsdp", None),
        P(),
        P(),
        P("fsdp", None),
        P("fsdp", None),
    )
    return jax.shard_map(on_device, mesh=fine, in_specs=in_specs, out_specs=out_specs, check_vma=False)
```
